32 devices in a mesh: dp: 8 (over y, x, core), mp: 4 (over z).
Axes of the slice: x: 2, y: 2, z: 4, core: 2. Of those that a mesh axis runs over, the one named last changes fastest.
Arguments:
- residual_input: bfloat16 [16, 1024, 768], P('dp'), may hold values from -6 to 6
- article_numbers: int32 [16, 1024], P('dp'), may hold values from 0 to 3, never falling along the last dimension, each value on 1 to 512 neighbouring positions
- upstream_gradient: bfloat16 [16, 1024, 768], P('dp'), may hold values from -6 to 6
- prenorm_scaling: bfloat16 [768], P(('dp', 'mp')), may hold values from 0.099609375 to 1.8984375
- prenorm_offset: bfloat16 [768], P(('dp', 'mp')), may hold values from -0.8984375 to 0.8984375
- postnorm_scaling: bfloat16 [768], P(('dp', 'mp')), may hold values from 0.099609375 to 1.8984375
- postnorm_offset: bfloat16 [768], P(('dp', 'mp')), may hold values from -0.8984375 to 0.8984375
- attention_blend: bfloat16 [3, 768], P(None, ('dp', 'mp')), may hold values from 0.049804688 to 0.94921875
- feedforward_blend: bfloat16 [2, 768], P(None, ('dp', 'mp')), may hold values from 0.049804688 to 0.94921875
- forgetting_logrates: bfloat16 [768], P(('dp', 'mp')), may hold values from -7.59375 to -3
- present_reward: bfloat16 [768], P(('dp', 'mp')), may hold values from -1 to 1
- projection_matrices: bfloat16 [4, 768, 768], P(None, ('dp', 'mp')), may hold values from -0.21875 to 0.21875
- final_matrix: bfloat16 [768, 768], P(('dp', 'mp')), may hold values from -0.875 to 0.875
- address_matrix: bfloat16 [768, 3072], P('dp', 'mp'), may hold values from -0.21875 to 0.21875
- content_matrix: bfloat16 [3072, 768], P('mp', 'dp'), may hold values from -0.109375 to 0.109375
Outputs:
- output: bfloat16 [16, 1024, 768], P('dp')
- input_grad: float32 [16, 1024, 768], P('dp')
- grad_ln1_gain: float32 [768], P(('dp', 'mp'))
- grad_ln1_bias: float32 [768], P(('dp', 'mp'))
- grad_ln2_gain: float32 [768], P(('dp', 'mp'))
- grad_ln2_bias: float32 [768], P(('dp', 'mp'))
- grad_time_mix: float32 [3, 768], P(None, ('dp', 'mp'))
- grad_channel_mix: float32 [2, 768], P(None, ('dp', 'mp'))
- grad_time_decay: float32 [768], P(('dp', 'mp'))
- grad_time_first: float32 [768], P(('dp', 'mp'))
- grad_mix_weights: float32 [4, 768, 768], P(None, ('dp', 'mp'))
- grad_out_weight: float32 [768, 768], P(('dp', 'mp'))
- grad_key_weight: float32 [768, 3072], P('dp', 'mp')
- grad_value_weight: float32 [3072, 768], P('mp', 'dp')
The draws below stay inside these ranges and needn't reach their ends.
Inputs may be any that keep to these rules, and one draw needn't show every extreme that they name: `article_numbers`: along a row the document numbers never fall.
All inputs are finite; a program needn't handle non-finite values.
Results may differ from the reference program's by a relative error of at most 0.015.
Values may be sent and summed in bfloat16 or wider, within the bound.
A program may use at most 256 MiB of HBM per device.

```python
import math
import jax
import jax.numpy as jnp
import numpy as np
from jax import lax

MODEL_SIZE = 768
FF = 3072
L = 1024
ROWS = 16


def level_of(key, shape, split, smallest, high):
    loudness, own = 1.0, jax.random.fold_in(key, 6)
    for dim, blocks in split:
        heights = jnp.exp(jax.random.uniform(jax.random.fold_in(own, dim), (blocks,), jnp.float32, smallest / len(split), high / len(split)))
        loudness = loudness * jnp.repeat(heights, shape[dim] // blocks).reshape([-1 if axis == dim else 1 for axis in range(len(shape))])
    return loudness


def split_up(count, total, reach, slope):
    loads = [(1 << 20) // math.isqrt(rank ** slope) + 1 for rank in range(2, count + 1)]
    rest, counts = total - reach - (count - 1), [1] * (count - 1)
    while rest > 0:
        movable = [i for i in range(count - 1) if counts[i] < reach]
        whole, remaining = sum([loads[i] for i in movable]), rest
        for i in movable:
            addition = min(reach - counts[i], max(1, remaining * loads[i] // whole), rest)
            counts[i] = counts[i] + addition
            rest = rest - addition
    return np.array([reach] + counts)


def ragged_sizes(key, count, total, reach, lean):
    if count == 2:
        one = jax.random.randint(key, (), max(1, total - reach), min(reach, total - 1) + 1)
        return jnp.stack([one, total - one])
    lengths = jnp.asarray(split_up(count, total, reach, lean), jnp.int32)
    couples = (count - 1) // 2
    source_of, receiver = lengths[1:1 + 2 * couples:2], lengths[2:2 + 2 * couples:2]
    room = jnp.minimum(source_of - 1, reach - receiver)
    moved = jax.random.randint(jax.random.fold_in(key, 1), (couples,), 0, 1 << 20) % (room + 1)
    lengths = lengths.at[1:1 + 2 * couples:2].set(source_of - moved).at[2:2 + 2 * couples:2].set(receiver + moved)
    return lengths[jax.random.permutation(jax.random.fold_in(key, 2), count)]


def noise(stream_key, shape, deviation, reach, shards=(), dtype=jnp.bfloat16):
    gain = level_of(stream_key, shape, shards, -0.22, 0.18) if shards else 1.0
    array = jax.random.normal(stream_key, shape, jnp.float32) * deviation * gain
    return jnp.minimum(jnp.maximum(array, -reach), reach).astype(dtype)


def setup_inputs(seed: int = 0) -> dict:
    seeds = jax.random.split(jax.random.key(seed), 16)
    residual_input = noise(seeds[0], (ROWS, L, MODEL_SIZE), 1.0, 6.0, ((0, 8),))
    article_numbers = jax.vmap(lambda own: jnp.searchsorted(jnp.cumsum(ragged_sizes(own, 4, L, L // 2, 2)), jnp.arange(L), side="right"))(jax.random.split(seeds[1], ROWS)).reshape((ROWS, L)).astype(jnp.int32)
    upstream_gradient = noise(seeds[2], (ROWS, L, MODEL_SIZE), 1.0, 6.0, ((0, 8),))
    prenorm_scaling = jnp.clip(1.0 + 0.18 * jax.random.normal(seeds[3], (MODEL_SIZE,), jnp.float32), 0.099609375, 1.8984375).astype(jnp.bfloat16)
    prenorm_offset = noise(seeds[4], (MODEL_SIZE,), 0.3, 0.8984375, ((0, 32),))
    postnorm_scaling = jnp.clip(1.0 + 0.18 * jax.random.normal(seeds[5], (MODEL_SIZE,), jnp.float32), 0.099609375, 1.8984375).astype(jnp.bfloat16)
    postnorm_offset = noise(seeds[6], (MODEL_SIZE,), 0.3, 0.8984375, ((0, 32),))
    attention_blend = jnp.clip(0.049804688 + 0.89941406 * jax.random.uniform(seeds[7], (3, MODEL_SIZE), jnp.float32) ** level_of(seeds[7], (3, MODEL_SIZE), ((1, 32),), -0.2, 0.2), 0.049804688, 0.94921875).astype(jnp.bfloat16)
    feedforward_blend = jnp.clip(0.049804688 + 0.89941406 * jax.random.uniform(seeds[8], (2, MODEL_SIZE), jnp.float32) ** level_of(seeds[8], (2, MODEL_SIZE), ((1, 32),), -0.2, 0.2), 0.049804688, 0.94921875).astype(jnp.bfloat16)
    forgetting_logrates = jnp.clip(-7.59375 + 4.59375 * jax.random.uniform(seeds[9], (MODEL_SIZE,), jnp.float32) ** level_of(seeds[9], (MODEL_SIZE,), ((0, 32),), -0.2, 0.2), -7.59375, -3.0).astype(jnp.bfloat16)
    present_reward = jnp.clip(jax.random.uniform(seeds[10], (MODEL_SIZE,), jnp.float32, -1.0, 1.0) * level_of(seeds[10], (MODEL_SIZE,), ((0, 32),), -0.4, 0.0), -1.0, 1.0).astype(jnp.bfloat16)
    projection_matrices = noise(seeds[11], (4, MODEL_SIZE, MODEL_SIZE), MODEL_SIZE ** -0.5, 0.21875, ((1, 32),))
    final_matrix = noise(seeds[12], (MODEL_SIZE, MODEL_SIZE), (MODEL_SIZE // 16) ** -0.5, 0.875, ((0, 32),))
    address_matrix = noise(seeds[13], (MODEL_SIZE, FF), MODEL_SIZE ** -0.5, 0.21875, ((0, 8), (1, 4)))
    content_matrix = noise(seeds[14], (FF, MODEL_SIZE), FF ** -0.5, 0.109375, ((0, 4), (1, 8)))
    return {"residual_input": residual_input, "article_numbers": article_numbers, "upstream_gradient": upstream_gradient, "prenorm_scaling": prenorm_scaling, "prenorm_offset": prenorm_offset, "postnorm_scaling": postnorm_scaling, "postnorm_offset": postnorm_offset, "attention_blend": attention_blend, "feedforward_blend": feedforward_blend, "forgetting_logrates": forgetting_logrates, "present_reward": present_reward, "projection_matrices": projection_matrices, "final_matrix": final_matrix, "address_matrix": address_matrix, "content_matrix": content_matrix}


@jax.custom_vjp
def low(v):
    return lax.optimization_barrier(v.astype(jnp.bfloat16)).astype(jnp.float32)

@jax.custom_vjp
def low_back(v):
    return v

def low_keep(v):
    return (low(v), None)

def low_pass(kept, grad):
    return (grad,)

def back_keep(v):
    return (v, None)

def back_low(kept, grad):
    return (low(grad),)
low.defvjp(low_keep, low_pass)
low_back.defvjp(back_keep, back_low)
epsilon = 1e-05

def layer_norm(values_in, gain_vec, bias_vec):
    average = lax.optimization_barrier(jnp.mean(values_in, axis=-1, keepdims=True))
    centered = values_in - average
    variance = lax.optimization_barrier(jnp.mean(centered * centered, axis=-1, keepdims=True))
    return centered * lax.rsqrt(variance + epsilon) * gain_vec + bias_vec

def shifted(values_in, retain_marker):
    earlier = jnp.concatenate([jnp.zeros_like(values_in[:, :1]), values_in[:, :-1]], axis=1)
    return earlier * retain_marker[:, :, None]

def blend(normed, earlier, factor):
    return normed * factor + earlier * (1.0 - factor)

def product(operand, weights):
    return jnp.einsum('rtk,kf->rtf', operand, weights, precision=lax.Precision.HIGHEST)

def weighted_recurrence(address_series, content_series, retain_marker, forgetting_logrates, present_reward):
    fading = jnp.exp(-jnp.exp(forgetting_logrates))

    @jax.checkpoint
    def advance(carry, pieces):
        accumulated_dividend, accumulated_divisor = carry
        present_address, present_content, keep_now = pieces
        saved_dividend = accumulated_dividend * keep_now[:, None]
        saved_divisor = accumulated_divisor * keep_now[:, None]
        reward_power = jnp.exp(present_reward + present_address)
        recurrence_result = (saved_dividend + reward_power * present_content) / (saved_divisor + reward_power)
        key_exp = jnp.exp(present_address)
        return ((saved_dividend * fading + key_exp * present_content, saved_divisor * fading + key_exp), recurrence_result)
    zero_state = jnp.zeros(address_series[:, 0].shape, jnp.float32)
    pieces = (jnp.swapaxes(address_series, 0, 1), jnp.swapaxes(content_series, 0, 1), jnp.swapaxes(retain_marker, 0, 1))
    _, blended_input = lax.scan(advance, (zero_state, zero_state), pieces)
    return jnp.swapaxes(blended_input, 0, 1)

def forward(stream_f, retain_marker, learned_tensors):
    prenorm_scaling, prenorm_offset, postnorm_scaling, postnorm_offset, attention_blend, feedforward_blend, forgetting_logrates, present_reward, projection_matrices, final_matrix, address_matrix, content_matrix = learned_tensors
    normed = layer_norm(stream_f, prenorm_scaling, prenorm_offset)
    earlier = shifted(normed, retain_marker)
    key_in = low(blend(normed, earlier, attention_blend[0]))
    value_in = low(blend(normed, earlier, attention_blend[1]))
    rec_in = low(blend(normed, earlier, attention_blend[2]))
    address_series = low_back(product(key_in, projection_matrices[0]))
    content_series = low_back(product(value_in, projection_matrices[1]))
    acceptance_gate = low_back(product(rec_in, projection_matrices[2]))
    blended_input = weighted_recurrence(address_series, content_series, retain_marker, forgetting_logrates, present_reward)
    gated = low(jax.nn.sigmoid(acceptance_gate) * blended_input)
    branch = low_back(product(gated, final_matrix))
    middle = stream_f + branch
    normed2 = layer_norm(middle, postnorm_scaling, postnorm_offset)
    earlier2 = shifted(normed2, retain_marker)
    ckey_in = low(blend(normed2, earlier2, feedforward_blend[0]))
    crec_in = low(blend(normed2, earlier2, feedforward_blend[1]))
    hidden = low_back(product(ckey_in, address_matrix))
    active = jax.nn.relu(hidden)
    squared = low(active * active)
    carried = low_back(product(squared, content_matrix))
    gate_pre = low_back(product(crec_in, projection_matrices[3]))
    return middle + jax.nn.sigmoid(gate_pre) * carried

def reference(residual_input, article_numbers, upstream_gradient, prenorm_scaling, prenorm_offset, postnorm_scaling, postnorm_offset, attention_blend, feedforward_blend, forgetting_logrates, present_reward, projection_matrices, final_matrix, address_matrix, content_matrix):
    learned_tensors = (prenorm_scaling.astype(jnp.float32), prenorm_offset.astype(jnp.float32), postnorm_scaling.astype(jnp.float32), postnorm_offset.astype(jnp.float32), attention_blend.astype(jnp.float32), feedforward_blend.astype(jnp.float32), forgetting_logrates.astype(jnp.float32), present_reward.astype(jnp.float32), projection_matrices.astype(jnp.float32), final_matrix.astype(jnp.float32), address_matrix.astype(jnp.float32), content_matrix.astype(jnp.float32))
    same_doc = article_numbers[:, 1:] == article_numbers[:, :-1]
    retain_marker = jnp.concatenate([jnp.zeros((ROWS, 1), jnp.bool_), same_doc], axis=1).astype(jnp.float32)
    group_rows = math.gcd(ROWS, max(1, 4096 // L))
    group_count = ROWS // group_rows
    stream_g = residual_input.astype(jnp.float32).reshape(group_count, group_rows, L, MODEL_SIZE)
    cot_g = upstream_gradient.astype(jnp.float32).reshape(group_count, group_rows, L, MODEL_SIZE)
    keep_g = retain_marker.reshape(group_count, group_rows, L)

    def one_group(totals, pieces):
        rows_in, keep_in, cot_in = pieces
        recurrence_result, pull = jax.vjp(lambda values_in, weights: forward(values_in, keep_in, weights), rows_in, learned_tensors)
        grad_rows, grad_params = pull(cot_in)
        return (jax.tree.map(jnp.add, totals, grad_params), (recurrence_result, grad_rows))
    zero_grads = jax.tree.map(jnp.zeros_like, learned_tensors)
    totals, (results, grad_rows) = lax.scan(one_group, zero_grads, (stream_g, keep_g, cot_g))
    output = results.reshape(ROWS, L, MODEL_SIZE).astype(jnp.bfloat16)
    input_grad = grad_rows.reshape(ROWS, L, MODEL_SIZE)
    return (output, input_grad, totals[0], totals[1], totals[2], totals[3], totals[4], totals[5], totals[6], totals[7], totals[8], totals[9], totals[10], totals[11])
```

```python
import functools

import jax
import jax.numpy as jnp
from jax import lax
from jax.experimental import pallas as pl
from jax.experimental.pallas import tpu as pltpu
from jax.sharding import PartitionSpec as P

BLOCK = 64
MICRO = 2


epsilon = 1e-05


def layer_norm(values_in, gain_vec, bias_vec):
    average = jnp.mean(values_in, axis=-1, keepdims=True)
    centered = values_in - average
    variance = jnp.mean(centered * centered, axis=-1, keepdims=True)
    return centered * lax.rsqrt(variance + epsilon) * gain_vec + bias_vec


def shifted(values_in, retain_marker):
    earlier = jnp.concatenate([jnp.zeros_like(values_in[:, :1]), values_in[:, :-1]], axis=1)
    return earlier * retain_marker[:, :, None]


def blend(normed, earlier, factor):
    return normed * factor + earlier * (1.0 - factor)


def project(operand, weights):
    return lax.dot_general(
        operand, weights, (((2,), (0,)), ((), ())), preferred_element_type=jnp.float32
    )


def back_project(gradient, weights):
    return lax.dot_general(
        gradient, weights, (((2,), (1,)), ((), ())), preferred_element_type=jnp.float32
    )


def weight_grad(operand, gradient):
    return lax.dot_general(
        operand, gradient, (((0, 1), (0, 1)), ((), ())), preferred_element_type=jnp.float32
    )


def take_share(array, axis_at, groups, shares, place):
    shape = array.shape
    piece_len = shape[axis_at] // (groups * shares)
    split_shape = shape[:axis_at] + (groups, shares, piece_len) + shape[axis_at + 1 :]
    chosen = lax.dynamic_index_in_dim(
        array.reshape(split_shape), place, axis_at + 1, keepdims=False
    )
    return chosen.reshape(shape[:axis_at] + (groups * piece_len,) + shape[axis_at + 1 :])


def first_piece(stream_f, gain_vec, bias_vec, factors, retain_marker):
    normed = layer_norm(stream_f, gain_vec, bias_vec)
    earlier = shifted(normed, retain_marker)
    return (
        blend(normed, earlier, factors[0]),
        blend(normed, earlier, factors[1]),
        blend(normed, earlier, factors[2]),
    )


def channel_piece(middle, gain_vec, bias_vec, factors, retain_marker):
    normed = layer_norm(middle, gain_vec, bias_vec)
    earlier = shifted(normed, retain_marker)
    return (blend(normed, earlier, factors[0]), blend(normed, earlier, factors[1]))


def time_piece(
    address_series,
    content_series,
    acceptance_gate,
    forgetting_logrates,
    present_reward,
    retain_marker,
    article_labels,
    span_length,
):
    batch_rows, length, feature_count = address_series.shape
    block_count = length // span_length
    decay_rate = jnp.exp(forgetting_logrates)
    position = jnp.arange(span_length, dtype=jnp.float32)[:, None]
    rising = jnp.exp(position * decay_rate)
    sinking = jnp.exp(-position * decay_rate)
    falling = jnp.exp(-(position + 1.0) * decay_rate)
    rising = jnp.concatenate([rising, rising], axis=-1)
    sinking = jnp.concatenate([sinking, sinking], axis=-1)
    falling = jnp.concatenate([falling, falling], axis=-1)
    whole_fade = jnp.exp(-span_length * decay_rate)
    whole_fade = jnp.concatenate([whole_fade, whole_fade], axis=-1)
    key_exp = jnp.exp(address_series)
    weighted = jnp.concatenate([key_exp * content_series, key_exp], axis=-1)
    weighted = weighted.reshape(batch_rows, block_count, span_length, 2 * feature_count)
    block_docs = article_labels.reshape(batch_rows, block_count, span_length)
    causal = jnp.arange(span_length)[:, None] >= jnp.arange(span_length)[None, :]
    same_doc = block_docs[:, :, :, None] == block_docs[:, :, None, :]
    doc_mask = (causal[None, None] & same_doc).astype(jnp.float32)
    partial_value = (
        jnp.einsum("rnji,rnid->rnjd", doc_mask, weighted * rising, precision=lax.Precision.HIGHEST)
        * sinking
    )
    last_docs = block_docs[:, :, -1]
    prior_docs = jnp.concatenate(
        [jnp.full((batch_rows, 1), -1, jnp.int32), last_docs[:, :-1]], axis=1
    )
    linked = (block_docs == prior_docs[:, :, None]).astype(jnp.float32)
    chained = linked[:, :, -1]

    def carry_step(state, pieces):
        tail_state, joined = pieces
        return (tail_state + whole_fade * joined[:, None] * state, state)

    zero_state = jnp.zeros((batch_rows, 2 * feature_count), jnp.float32)
    _, starts = lax.scan(
        carry_step,
        zero_state,
        (jnp.swapaxes(partial_value[:, :, -1], 0, 1), jnp.swapaxes(chained, 0, 1)),
    )
    starts = jnp.swapaxes(starts, 0, 1)
    states = partial_value + falling * linked[..., None] * starts[:, :, None, :]
    states = states.reshape(batch_rows, length, 2 * feature_count)
    entering_memory = shifted(states, retain_marker)
    reward_power = jnp.exp(present_reward + address_series)
    accumulated_dividend = entering_memory[..., :feature_count] + reward_power * content_series
    accumulated_divisor = entering_memory[..., feature_count:] + reward_power
    return jax.nn.sigmoid(acceptance_gate) * (accumulated_dividend / accumulated_divisor)


def general_device(
    residual_input,
    article_numbers,
    upstream_gradient,
    prenorm_scaling,
    prenorm_offset,
    postnorm_scaling,
    postnorm_offset,
    attention_blend,
    feedforward_blend,
    forgetting_logrates,
    present_reward,
    projection_matrices,
    final_matrix,
    address_matrix,
    content_matrix,
):
    batch_rows = residual_input.shape[0] // MICRO
    same_doc = article_numbers[:, 1:] == article_numbers[:, :-1]
    keep_all = jnp.concatenate([jnp.zeros_like(same_doc[:, :1]), same_doc], axis=1).astype(
        jnp.float32
    )
    groups = lax.axis_size("dp")
    shares = lax.axis_size("mp")
    mp_place = lax.axis_index("mp")
    totals = None
    outputs = []
    input_grads = []
    for micro_index in range(MICRO):
        shared = (
            lax.all_gather(prenorm_scaling, ("dp", "mp"), axis=0, tiled=True),
            lax.all_gather(prenorm_offset, ("dp", "mp"), axis=0, tiled=True),
            lax.all_gather(postnorm_scaling, ("dp", "mp"), axis=0, tiled=True),
            lax.all_gather(postnorm_offset, ("dp", "mp"), axis=0, tiled=True),
            lax.all_gather(attention_blend, ("dp", "mp"), axis=1, tiled=True),
            lax.all_gather(feedforward_blend, ("dp", "mp"), axis=1, tiled=True),
            lax.all_gather(forgetting_logrates, ("dp", "mp"), axis=0, tiled=True),
            lax.all_gather(present_reward, ("dp", "mp"), axis=0, tiled=True),
            lax.all_gather(projection_matrices, ("dp", "mp"), axis=1, tiled=True),
            lax.all_gather(final_matrix, ("dp", "mp"), axis=0, tiled=True),
        )
        local = (
            lax.all_gather(address_matrix, "dp", axis=0, tiled=True),
            lax.all_gather(content_matrix, "dp", axis=1, tiled=True),
        )
        fetched = (shared, local)
        shared, local = fetched
        gain_one, bias_one, gain_two, bias_two, tmix_w, cmix_w, decay_w, first_w, mix_w, out_w = (
            shared
        )
        key_w, value_w = local
        mix_part = take_share(mix_w[0:3], 2, groups, shares, mp_place)
        out_part = take_share(out_w, 0, groups, shares, mp_place)
        decay_part = take_share(decay_w, 0, groups, shares, mp_place)
        first_part = take_share(first_w, 0, groups, shares, mp_place)
        lower_row = micro_index * batch_rows
        upper_row = lower_row + batch_rows
        stream_f = residual_input[lower_row:upper_row].astype(jnp.float32)
        retain_marker = keep_all[lower_row:upper_row]
        article_labels = article_numbers[lower_row:upper_row]
        grad_out = upstream_gradient[lower_row:upper_row].astype(jnp.float32)

        def first_local(values_in, gain_vec, bias_vec, factors):
            return first_piece(values_in, gain_vec, bias_vec, factors, retain_marker)

        def time_local(address_series, content_series, acceptance_gate, decay_vec, first_vec):
            return time_piece(
                address_series,
                content_series,
                acceptance_gate,
                decay_vec,
                first_vec,
                retain_marker,
                article_labels,
                BLOCK,
            )

        def channel_local(values_in, gain_vec, bias_vec, factors):
            return channel_piece(values_in, gain_vec, bias_vec, factors, retain_marker)

        mixes, pull_first = jax.vjp(
            first_local,
            stream_f,
            gain_one.astype(jnp.float32),
            bias_one.astype(jnp.float32),
            tmix_w.astype(jnp.float32),
        )
        key_in = mixes[0].astype(jnp.bfloat16)
        value_in = mixes[1].astype(jnp.bfloat16)
        rec_in = mixes[2].astype(jnp.bfloat16)
        address_series = project(key_in, mix_part[0])
        content_series = project(value_in, mix_part[1])
        acceptance_gate = project(rec_in, mix_part[2])
        gated, pull_time = jax.vjp(
            time_local,
            address_series,
            content_series,
            acceptance_gate,
            decay_part.astype(jnp.float32),
            first_part.astype(jnp.float32),
        )
        gated_low = gated.astype(jnp.bfloat16)
        branch = project(gated_low, out_part)
        branch = lax.psum(branch, "mp")
        middle = stream_f + branch
        channel_ins, pull_channel = jax.vjp(
            channel_local,
            middle,
            gain_two.astype(jnp.float32),
            bias_two.astype(jnp.float32),
            cmix_w.astype(jnp.float32),
        )
        ckey_in = channel_ins[0].astype(jnp.bfloat16)
        crec_in = channel_ins[1].astype(jnp.bfloat16)
        hidden = project(ckey_in, key_w)
        active = jax.nn.relu(hidden)
        squared = (active * active).astype(jnp.bfloat16)
        carried = lax.psum(project(squared, value_w).astype(jnp.bfloat16), "mp").astype(jnp.float32)
        gate_sig = jax.nn.sigmoid(project(crec_in, mix_w[3]))
        outputs.append((middle + gate_sig * carried).astype(jnp.bfloat16))
        grad_carried = (grad_out * gate_sig).astype(jnp.bfloat16)
        grad_gate = (grad_out * carried * gate_sig * (1.0 - gate_sig)).astype(jnp.bfloat16)
        grad_value_w = weight_grad(squared, grad_carried)
        grad_hidden = (back_project(grad_carried, value_w) * 2.0 * active).astype(jnp.bfloat16)
        grad_key_w = weight_grad(ckey_in, grad_hidden)
        grad_crec_w = weight_grad(crec_in, grad_gate)
        grad_ckey = lax.psum(back_project(grad_hidden, key_w).astype(jnp.bfloat16), "mp").astype(
            jnp.float32
        )
        grad_crec = back_project(grad_gate, mix_w[3])
        grad_middle, grad_gain_two, grad_bias_two, grad_cmix = pull_channel((grad_ckey, grad_crec))
        grad_middle = grad_middle + grad_out
        grad_branch = grad_middle.astype(jnp.bfloat16)
        grad_out_w = weight_grad(gated_low, grad_branch)
        grad_gated = back_project(grad_branch, out_part)
        grad_keys, grad_values, grad_recept, grad_decay, grad_first = pull_time(grad_gated)
        grad_keys = grad_keys.astype(jnp.bfloat16)
        grad_values = grad_values.astype(jnp.bfloat16)
        grad_recept = grad_recept.astype(jnp.bfloat16)
        grad_mix_three = jnp.stack(
            [
                weight_grad(key_in, grad_keys),
                weight_grad(value_in, grad_values),
                weight_grad(rec_in, grad_recept),
            ]
        )
        grad_ins = (
            back_project(grad_keys, mix_part[0]),
            back_project(grad_values, mix_part[1]),
            back_project(grad_recept, mix_part[2]),
        )
        pulled = pull_first(grad_ins)
        pulled = (
            lax.psum(pulled[0].astype(jnp.bfloat16), "mp").astype(jnp.float32),
            lax.psum(pulled[1].astype(jnp.bfloat16), "mp").astype(jnp.float32),
            lax.psum(pulled[2].astype(jnp.bfloat16), "mp").astype(jnp.float32),
            lax.psum(pulled[3].astype(jnp.bfloat16), "mp").astype(jnp.float32),
        )
        grad_stream, grad_gain_one, grad_bias_one, grad_tmix = pulled
        input_grads.append(grad_stream + grad_middle)
        current = [
            grad_gain_one,
            grad_bias_one,
            grad_gain_two,
            grad_bias_two,
            grad_tmix,
            grad_cmix,
            grad_decay,
            grad_first,
            grad_mix_three,
            grad_crec_w,
            grad_out_w,
            grad_key_w,
            grad_value_w,
        ]
        totals = (
            current
            if totals is None
            else [earlier + latest for earlier, latest in zip(totals, current)]
        )

    def pick(gradient, axis_at):
        return take_share(gradient, axis_at, groups, shares, mp_place)

    split_grads = (
        lax.psum_scatter(pick(totals[0], 0), "dp", scatter_dimension=0, tiled=True),
        lax.psum_scatter(pick(totals[1], 0), "dp", scatter_dimension=0, tiled=True),
        lax.psum_scatter(pick(totals[2], 0), "dp", scatter_dimension=0, tiled=True),
        lax.psum_scatter(pick(totals[3], 0), "dp", scatter_dimension=0, tiled=True),
        lax.psum_scatter(pick(totals[4], 1), "dp", scatter_dimension=1, tiled=True),
        lax.psum_scatter(pick(totals[5], 1), "dp", scatter_dimension=1, tiled=True),
        lax.psum_scatter(totals[6], "dp", scatter_dimension=0, tiled=True),
        lax.psum_scatter(totals[7], "dp", scatter_dimension=0, tiled=True),
        lax.psum_scatter(totals[10], "dp", scatter_dimension=0, tiled=True),
    )
    feature_count = totals[9].shape[0]
    share_mask = jax.nn.one_hot(mp_place, shares, dtype=jnp.float32)
    three_full = (
        totals[8].reshape(3, feature_count, groups, 1, feature_count // (groups * shares))
        * share_mask[None, None, None, :, None]
    )
    three_full = three_full.reshape(3, feature_count, feature_count)
    crec_grad = totals[9] * (mp_place == 0).astype(jnp.float32)
    mix_grad = lax.psum_scatter(
        jnp.concatenate([three_full, crec_grad[None]], axis=0),
        ("dp", "mp"),
        scatter_dimension=1,
        tiled=True,
    )
    shared_grads = (
        split_grads[0],
        split_grads[1],
        split_grads[2],
        split_grads[3],
        split_grads[4],
        split_grads[5],
        split_grads[6],
        split_grads[7],
        mix_grad,
        split_grads[8],
    )
    channel_grads = (
        lax.psum_scatter(totals[11], "dp", scatter_dimension=0, tiled=True),
        lax.psum_scatter(totals[12], "dp", scatter_dimension=1, tiled=True),
    )
    output = jnp.concatenate(outputs, axis=0)
    input_grad = jnp.concatenate(input_grads, axis=0)
    return (
        output,
        input_grad,
        shared_grads[0],
        shared_grads[1],
        shared_grads[2],
        shared_grads[3],
        shared_grads[4],
        shared_grads[5],
        shared_grads[6],
        shared_grads[7],
        shared_grads[8],
        shared_grads[9],
        channel_grads[0],
        channel_grads[1],
    )


MESH = pl.DeviceIdType.MESH
MIB = 2**20

class Place:
    def __init__(self):
        self.dp = lax.axis_index("dp")
        self.mp = lax.axis_index("mp")
        self.core = self.dp % 2
        self.x = (self.dp // 2) % 2
        self.y = self.dp // 4
        self.sib = (self.dp + 1 - 2 * self.core, self.mp)
        self.xn = (self.dp + 2 - 4 * self.x, self.mp)
        self.yn = (self.dp + 4 - 8 * self.y, self.mp)
        self.up_z = (self.mp + 1) % 4
        self.down_z = (self.mp + 3) % 4
        self.far_z = (self.mp + 2) % 4
        self.up = (self.dp, self.up_z)
        self.down = (self.dp, self.down_z)
        self.pair = (self.dp, self.mp + 1 - 2 * (self.mp % 2))


def greet(devices):
    barrier = pltpu.get_barrier_semaphore()
    for device in devices:
        pl.semaphore_signal(barrier, inc=1, device_id=device, device_id_type=MESH)
    pl.semaphore_wait(barrier, len(devices))


class Messages:
    def __init__(self, send_sem, recv_sems):
        self.send_sem, self.recv_sems, self.count, self.sent = send_sem, recv_sems, 0, []

    def send(self, source, target, arrival, device, when=None):
        index = self.count
        self.count += 1
        copy = pltpu.make_async_remote_copy(source, target, self.send_sem, self.recv_sems.at[index], device_id=device, device_id_type=MESH)
        only(when, copy.start)
        self.sent.append((when, copy))
        return pltpu.make_async_remote_copy(arrival, arrival, self.send_sem, self.recv_sems.at[index], device_id=device, device_id_type=MESH)

    def finish(self):
        for when, copy in self.sent:
            only(when, copy.wait_send)
        self.sent = []


def only(when, action):
    if when is None:
        action()
    else:
        pl.when(when)(action)


ALL = slice(None)


class Stream:
    def __init__(self, place, messages, order, piece, own, twin_sem):
        self.p, self.msg, self.order, self.piece, self.own, self.twin_sem = place, messages, order, piece, own, twin_sem
        p = place
        self.first = order.replace("z", "")[0]
        self.z_leads = order[0] == "z"
        self.a, self.b = (p.x, p.y) if self.first == "x" else (p.y, p.x)
        self.na, self.nb = (p.xn, p.yn) if self.first == "x" else (p.yn, p.xn)
        self.base = messages.count
        messages.count += 15

    def at(self, col, other, slab, core=None):
        a = self.a if col == 0 else 1 - self.a
        b = 1 - self.b if other else self.b
        y, x = (b, a) if self.first == "x" else (a, b)
        return self.piece(y, x, self.p.core if core is None else core, slab)

    def slab(self, j):
        m = self.p.mp
        if j == 0:
            return m
        flip = (m >= 2).astype(jnp.int32)
        near = m + flip * (3 - 2 * m)
        picked = j - (j <= near).astype(jnp.int32)
        return picked + flip * (3 - 2 * picked)

    def rank(self, m, slab):
        flip = (m >= 2).astype(jnp.int32)
        near = m + flip * (3 - 2 * m)
        picked = slab + flip * (3 - 2 * slab)
        return picked - (picked > near).astype(jnp.int32) + 1

    def index(self, kind, col, j):
        if self.z_leads:
            return self.base + {"z": j - 1, "a": 3 + j, "b": 7 + 4 * col + j}[kind]
        return self.base + {"z": 3 * col + j - 1, "a": 6, "b": 7 + 4 * col + j}[kind]

    def copy(self, piece, index, device, when=None, source=None):
        copy = pltpu.make_async_remote_copy(
            piece if source is None else source, piece, self.msg.send_sem, self.msg.recv_sems.at[index],
            device_id=device, device_id_type=MESH,
        )
        only(when, copy.start)
        self.msg.sent.append((when, copy))

    def twin(self, col, other, slab, source=None):
        piece = self.at(col, other, slab)
        copy = pltpu.make_async_remote_copy(
            piece if source is None else source, piece, self.msg.send_sem, self.twin_sem,
            device_id=self.p.sib, device_id_type=MESH,
        )
        copy.start()
        self.msg.sent.append((None, copy))

    def send_z(self, col, j, source=None):
        m = self.p.mp
        slab = self.slab(j)
        piece = self.at(col, 0, slab)
        if j == 0:
            self.copy(piece, self.index("z", col, 1) + self.rank(m + 1, slab) - 1, self.p.up, m < 3, source)
            self.copy(piece, self.index("z", col, 1) + self.rank(m - 1, slab) - 1, self.p.down, m > 0, source)
            return
        target = m - 1 + 2 * (slab < m).astype(jnp.int32)
        safe = (target + 4) % 4
        self.copy(piece, self.index("z", col, 1) + self.rank(target, slab) - 1, (self.p.dp, safe), (target >= 0) & (target <= 3))

    def send_a(self, j, source=None):
        self.copy(self.at(0, 0, self.slab(j)), self.index("a", 0, j), self.na, source=source)

    def send_b(self, col, j, source=None):
        self.copy(self.at(col, 0, self.slab(j)), self.index("b", col, j), self.nb, source=source)

    def event(self, kind, col, j):
        if kind == "o":
            self.send_z(0, 0, self.own)
            self.send_a(0, self.own)
            self.send_b(0, 0, self.own)
            self.twin(0, 0, self.p.mp, self.own)
            return
        slab = self.slab(j)
        piece = self.at(1 if kind == "a" else col, kind == "b", slab)
        sem = self.msg.recv_sems.at[self.index(kind, col, j)]
        pltpu.make_async_remote_copy(piece, piece, self.msg.send_sem, sem, device_id=self.na, device_id_type=MESH).wait_recv()
        if kind == "z":
            self.send_z(col, j)
            if self.z_leads:
                self.send_a(j)
            self.send_b(col, j)
            self.twin(col, 0, slab)
        elif kind == "a":
            if not self.z_leads:
                self.send_z(1, 0)
            self.send_b(1, j)
            self.twin(1, 0, slab)
        else:
            self.twin(col, 1, slab)


def streams(place, messages, twin_sems, pk, kw, vt, tw, kg, vg):
    def time_piece(part):
        return lambda y, x, c, m: tw.at[y, x, c, m, pl.ds(64 * part, 64)]

    def channel_piece(array, part):
        return lambda y, x, c, m: array.at[m, y, x, c, pl.ds(48 * part, 48)]

    made = [Stream(place, messages, ("zxy", "zyx")[i], time_piece(i), pk.at[pl.ds(64 * i, 64)], twin_sems.at[0]) for i in range(2)]
    for n, (source, array) in enumerate(((kw, kg), (vt, vg))):
        made += [
            Stream(place, messages, ("xzy", "yzx")[i], channel_piece(array, i), source.at[pl.ds(48 * i, 48)], twin_sems.at[1 + n])
            for i in range(2)
        ]
    return made


def play(made, events):
    for event in events:
        made[int(event[0])].event(event[1], int(event[2]), int(event[3]))


EVENTS = (
    ("0o00", "1o00", "0a00", "0b00", "0z01", "1a00", "1b00", "1z01", "0z02", "1z02", "0a01", "0b01", "0b10", "0z03", "0a02", "1z03", "0b02", "1b01", "1b10", "1a01", "1b02", "2o00", "3o00", "1a02", "0b11", "2z01", "0a03", "0b03", "3z01", "2z02", "1b03", "0b12", "1b11", "3z02", "2a00", "2z03", "1a03", "3b00", "3z03", "2b00", "1b12", "3a00", "2z11", "4o00", "5o00", "2z12", "3b01", "3b02", "0b13", "2b01", "1b13", ),
    ("3z11", "2b02", "3b03", "4z01", ),
    ("5z01", "2b03", "2b10", "3b10", ),
    ("2z13", "4a00", ),
    ("3z12", "2b11", "5b00", ),
    ("4z02", "4b00", "3b11", ),
    ("5z02", "2b12", "5a00", ),
    ("3z13", "5b01", "3b12", ),
    ("4z03", "4z11", "2b13", "4b01", ),
    ("5z03", "5b02", ),
    ("4z12", "3b13", "4b02", "4b10", "5b10", ),
    ("5z11", "5b03", "4b03", "4b11", ),
    ("4z13", "4b12", ),
    ("5z12", "5b11", ),
    ("5z13", "4b13", ),
    ("5b12", ),
    ("5b13", ),
    (),
)


def greet_all(p):
    barrier = pltpu.get_barrier_semaphore()
    for device in (p.sib, p.xn, p.yn):
        pl.semaphore_signal(barrier, inc=1, device_id=device, device_id_type=MESH)
    only(p.mp < 3, lambda: pl.semaphore_signal(barrier, inc=1, device_id=p.up, device_id_type=MESH))
    only(p.mp > 0, lambda: pl.semaphore_signal(barrier, inc=1, device_id=p.down, device_id_type=MESH))
    pl.semaphore_wait(barrier, 3 + (p.mp < 3).astype(jnp.int32) + (p.mp > 0).astype(jnp.int32))


TILE = 256
SPAN = 128
WIDE = 512


def dot(a, b):
    return jnp.dot(a, b, preferred_element_type=jnp.float32)


def dot_nt(a, b):
    return lax.dot_general(a, b, (((1,), (1,)), ((), ())), preferred_element_type=jnp.float32)


def dot_tn(a, b):
    return lax.dot_general(a, b, (((0,), (0,)), ((), ())), preferred_element_type=jnp.float32)


def low(values):
    return values.astype(jnp.bfloat16)


def wide(values):
    return values.astype(jnp.float32)


def row_sums(values):
    rows, width = values.shape
    return jnp.sum(values.reshape(rows // 8, 8, width), axis=0)


def standardise(values):
    centered = values - jnp.mean(values, axis=-1, keepdims=True)
    variance = jnp.mean(centered * centered, axis=-1, keepdims=True)
    scale = lax.rsqrt(variance + epsilon)
    return centered * scale, scale


def norm_back(grad, normal, scale):
    mean_grad = jnp.mean(grad, axis=-1, keepdims=True)
    mean_both = jnp.mean(grad * normal, axis=-1, keepdims=True)
    return scale * (grad - mean_grad - normal * mean_both)


def later(values, first_row):
    row = lax.broadcasted_iota(jnp.int32, values.shape, 0)
    return jnp.where(row == 0, first_row, pltpu.roll(values, 1, 0))


def sooner(values, last_row):
    rows = values.shape[0]
    row = lax.broadcasted_iota(jnp.int32, values.shape, 0)
    return jnp.where(row == rows - 1, last_row, pltpu.roll(values, rows - 1, 0))


def masked_sum(mask, values):
    high = low(values)
    rest = low(values - wide(high))
    return dot(mask, high) + dot(mask, rest)


GAIN1, BIAS1, GAIN2, BIAS2, MIX, DECAY, FIRST, BLEND = 0, 1, 2, 3, 4, 7, 8, 9


def vec(ref, index):
    return ref[index : index + 1, :]


def rows_at(start, count):
    return pl.ds(pl.multiple_of(start, 128), count)


def forward_kernel(
    pk, kw, vt, x_any, gy_any, cols, doc_row,
    kg, vg, acts, kvs, middle_o, sq_o, act_o, grads_o, out_o, wts_o, vecs_o,
    w5, kv, sa, acs, xb, st, f5, mid, sig, tables, vecs, prev, sems, twin_sems, send_sem, recv_sems,
):
    place_of = Place()
    p = place_of
    row = p.mp % 2
    load_x = pltpu.make_async_copy(x_any.at[row], xb, sems.at[0])
    load_x.start()
    keep = [
        pltpu.make_async_copy(pk, sa.at[p.y, p.x, p.core, p.mp], sems.at[26]),
        pltpu.make_async_copy(kw, kg.at[p.mp, p.y, p.x, p.core], sems.at[27]),
        pltpu.make_async_copy(vt, vg.at[p.mp, p.y, p.x, p.core], sems.at[28]),
    ]
    for copy in keep:
        copy.start()
    greet_all(place_of)
    messages = Messages(send_sem, recv_sems)
    made = streams(place_of, messages, twin_sems, pk, kw, vt, sa, kg, vg)

    def twins(i, half):
        pltpu.make_async_copy(half, half, twin_sems.at[i]).wait()

    prev[...] = jnp.zeros_like(prev)
    play(made, EVENTS[0])
    for copy in keep:
        copy.wait()
    twins(0, sa.at[:, :, 1 - p.core])

    def relay(half):
        def body(i, total):
            core, m = i // 2, 2 * (i % 2)
            pair = 8 * half + i
            spot = half, i // 4, core % 2
            first, second = wide(sa[spot + (m,)]), wide(sa[spot + (m + 1,)])
            for j in range(5):
                piece = jnp.concatenate([first[24 * j : 24 * j + 24], second[24 * j : 24 * j + 24]], axis=0)
                w5[j, pl.ds(pl.multiple_of(48 * pair, 16), 48), :] = low(piece)
            return total + first[120:128] + second[120:128]

        return lax.fori_loop(0, 8, body, jnp.zeros((8, 768), jnp.float32))

    left, right = relay(0), relay(1)
    vecs[0:8, :] = jnp.concatenate([left[:, :384], right[:, :384]], axis=1)
    vecs[8:16, :] = jnp.concatenate([left[:, 384:], right[:, 384:]], axis=1)
    save_w = pltpu.make_async_copy(w5, wts_o, sems.at[10])
    save_v = pltpu.make_async_copy(vecs, vecs_o, sems.at[11])
    save_w.start()
    save_v.start()

    rate = jnp.exp(vec(vecs, DECAY))
    fade = jnp.exp(-rate)
    place = wide(lax.broadcasted_iota(jnp.int32, (SPAN, 1), 0))
    tables[0] = jnp.exp((place - 64.0) * rate)
    tables[1] = jnp.exp((65.0 - place) * rate)
    tables[2] = jnp.exp(-place * rate)
    load_x.wait()
    saves = []
    phase = 1
    for t in range(1024 // TILE):
        r = pl.ds(t * TILE, TILE)
        play(made, EVENTS[phase])
        x = wide(xb[r, :])
        keep_col = cols[r, 1:2]
        normal, _ = standardise(x)
        normed = normal * vec(vecs, GAIN1) + vec(vecs, BIAS1)
        earlier = later(normed, prev[0:1, :]) * keep_col
        prev[0:1, :] = normed[TILE - 1 :, :]
        delta = normed - earlier
        ins = [low(earlier + delta * vec(vecs, MIX + j)) for j in range(3)]
        for j in range(3):
            st[j, r, :] = ins[j]
        f5[0, r, :] = dot(ins[0], w5[0])
        f5[1, r, :] = dot(ins[1], w5[1])
        f5[2, r, :] = jax.nn.sigmoid(dot(ins[2], w5[2]))
        play(made, EVENTS[phase + 1])
        keys, values, gate = f5[0, r, :], f5[1, r, :], f5[2, r, :]
        key_exp = jnp.exp(keys)
        bonus = jnp.exp(keys + vec(vecs, FIRST))
        weighted = key_exp * values
        time = lax.broadcasted_iota(jnp.int32, (SPAN, SPAN), 0)
        source = lax.broadcasted_iota(jnp.int32, (SPAN, SPAN), 1)
        tops, bottoms = [], []
        for i in range(TILE // SPAN):
            q = pl.ds(t * TILE + i * SPAN, SPAN)
            block = t * (TILE // SPAN) + i
            part = slice(i * SPAN, (i + 1) * SPAN)
            same = cols[q, 0:1] == doc_row[block : block + 1, :]
            mask = jnp.where(same & (source < time), 1.0, 0.0).astype(jnp.bfloat16)
            link = cols[q, 2:3] * tables[2]
            top = masked_sum(mask, weighted[part] * tables[0]) * tables[1] + link * prev[2:3, :]
            bottom = masked_sum(mask, key_exp[part] * tables[0]) * tables[1] + link * prev[3:4, :]
            prev[2:3, :] = fade * top[SPAN - 1 :] + weighted[part][SPAN - 1 :]
            prev[3:4, :] = fade * bottom[SPAN - 1 :] + key_exp[part][SPAN - 1 :]
            f5[3, q, :] = top
            f5[4, q, :] = bottom
            tops.append(top)
            bottoms.append(bottom)
        top, bottom = jnp.concatenate(tops, axis=0), jnp.concatenate(bottoms, axis=0)
        gated = low(gate * ((top + bonus * values) / (bottom + bonus)))
        st[3, r, :] = gated
        mid[r, :] = x + dot(gated, w5[4])
        play(made, EVENTS[phase + 2])
        normal, _ = standardise(mid[r, :])
        normed = normal * vec(vecs, GAIN2) + vec(vecs, BIAS2)
        earlier = later(normed, prev[1:2, :]) * keep_col
        prev[1:2, :] = normed[TILE - 1 :, :]
        delta = normed - earlier
        st[4, r, :] = low(earlier + delta * vec(vecs, BLEND))
        receive = low(earlier + delta * vec(vecs, BLEND + 1))
        st[5, r, :] = receive
        sig[r, :] = jax.nn.sigmoid(dot(receive, w5[3]))
        phase += 3
        saves += [
            pltpu.make_async_copy(st.at[:, r], acts.at[:, r], sems.at[12 + t]),
            pltpu.make_async_copy(f5.at[:, r], kvs.at[:, r], sems.at[16 + t]),
            pltpu.make_async_copy(mid.at[r], middle_o.at[r], sems.at[20 + t]),
        ]
        for copy in saves[-3:]:
            copy.start()
    load_gy = pltpu.make_async_copy(gy_any.at[row], xb, sems.at[24])
    load_gy.start()
    messages.finish()

    def load_kv(m, which, array):
        target = kv.at[m]
        return pltpu.make_async_copy(array.at[m], target, sems.at[4 * which + 1 + m])

    pending = {}
    for m in range(4):
        play(made, EVENTS[phase + m])
        if m == 0:
            twins(1, kg.at[:, :, :, 1 - p.core])
            for i in range(4):
                load_kv(i, 0, kg).start()
        load_kv(m, 0, kg).wait()
        slot = m % 2
        if m >= 2:
            pending.pop(m - 2).wait()

        def hidden(t, carry):
            r = rows_at(t * WIDE, WIDE)
            active = jnp.maximum(dot(st[4, r, :], kv[m].reshape(768, 768)), 0.0)
            squared = low(active * active)
            spot = m // 2, m % 2, t
            sa[spot] = squared.reshape(4, 128, 768)
            acs[slot, pl.ds(t * 4, 4)] = low(active).reshape(4, 128, 768)
            return carry

        lax.fori_loop(0, 1024 // WIDE, hidden, 0)
        pending[m] = pltpu.make_async_copy(acs.at[slot], act_o.at[m], sems.at[29 + m])
        pending[m].start()
    play(made, EVENTS[phase + 4])
    twins(2, vg.at[:, :, :, 1 - p.core])
    for i in range(4):
        load_kv(i, 1, vg).start()
    save_sq = pltpu.make_async_copy(sa, sq_o, sems.at[33])
    save_sq.start()
    for copy in saves:
        copy.wait()
    for m in range(4):
        load_kv(m, 1, vg).wait()

        def content(t, carry):
            r = rows_at(t * WIDE, WIDE)
            squared = sa[m // 2, m % 2, t].reshape(WIDE, 768)
            part = dot_nt(squared, kv[m].reshape(768, 768))
            f5[0, r, :] = part if m == 0 else f5[0, r, :] + part
            return carry

        lax.fori_loop(0, 1024 // WIDE, content, 0)

    load_gy.wait()

    def finish(t, carry):
        r = rows_at(t * TILE, TILE)
        upstream, gate, carried = wide(xb[r, :]), sig[r, :], f5[0, r, :]
        st[0, r, :] = low(mid[r, :] + gate * carried)
        passed = upstream * gate
        st[1, r, :] = low(passed)
        st[2, r, :] = low(passed * carried * (1.0 - gate))
        return carry

    lax.fori_loop(0, 1024 // TILE, finish, 0)
    last = [
        pltpu.make_async_copy(st.at[0], out_o, sems.at[34]),
        pltpu.make_async_copy(st.at[pl.ds(1, 2)], grads_o, sems.at[35]),
    ]
    for copy in last:
        copy.start()
    save_w.wait()
    save_v.wait()
    save_sq.wait()
    for m in (2, 3):
        pending.pop(m).wait()
    messages.finish()
    for copy in last:
        copy.wait()


ANY = pl.BlockSpec(memory_space=pl.ANY)
ON_CORE = pl.BlockSpec(memory_space=pltpu.VMEM)
LIMIT = 63 * MIB


def forward(pk, kw, vt, x, gy, cols, doc_row):
    bf, f32 = jnp.bfloat16, jnp.float32
    shape = jax.ShapeDtypeStruct
    return pl.pallas_call(
        forward_kernel,
        out_shape=(
            shape((4, 2, 2, 2, 96, 768), bf), shape((4, 2, 2, 2, 96, 768), bf),
            shape((6, 1024, 768), bf), shape((5, 1024, 768), f32), shape((1024, 768), f32),
            shape((2, 2, 2, 4, 128, 768), bf), shape((4, 8, 128, 768), bf), shape((2, 1024, 768), bf),
            shape((1024, 768), bf), shape((5, 768, 768), bf), shape((16, 768), f32),
        ),
        in_specs=[ON_CORE] * 3 + [ANY] * 2 + [ON_CORE] * 2,
        out_specs=[ANY] * 11,
        scratch_shapes=[
            pltpu.VMEM((5, 768, 768), bf), pltpu.VMEM((4, 2, 2, 2, 96, 768), bf), pltpu.VMEM((2, 2, 2, 4, 128, 768), bf),
            pltpu.VMEM((2, 8, 128, 768), bf),
            pltpu.VMEM((1024, 768), bf), pltpu.VMEM((6, 1024, 768), bf), pltpu.VMEM((5, 1024, 768), f32),
            pltpu.VMEM((1024, 768), f32), pltpu.VMEM((1024, 768), f32),
            pltpu.VMEM((3, SPAN, 768), f32), pltpu.VMEM((16, 768), f32), pltpu.VMEM((8, 768), f32),
            pltpu.SemaphoreType.DMA((36,)), pltpu.SemaphoreType.DMA((3,)), pltpu.SemaphoreType.DMA,
            pltpu.SemaphoreType.DMA((90,)),
        ],
        compiler_params=pltpu.CompilerParams(vmem_limit_bytes=LIMIT, collective_id=0, has_side_effects=True),
        name="forward",
    )(pk, kw, vt, x, gy, cols, doc_row)


def channel_back_kernel(
    kg, vg, wts, acts, sq, act, grads, middle, gy_any, out_row, cols, vecs,
    gm_o, gkv_o, out_o, sums_o,
    kv, sqs, acs, gcg, cc, dh, acc, wg, midp, gy, gm, stage, gate_w, sums, nxt, result, sems, send_sem, recv_sems,
):
    place = Place()
    mp = place.mp
    row, pair = mp % 2, mp // 2
    load_row = pltpu.make_async_copy(out_row, result, sems.at[22])
    load_row.start()
    greet([place.pair])
    messages = Messages(send_sem, recv_sems)
    load_row.wait()
    arrival = messages.send(result, out_o.at[row], out_o.at[1 - row], place.pair)
    keep_row = pltpu.make_async_copy(result, out_o.at[row], sems.at[21])
    keep_row.start()
    order = [2 * pair, 2 * pair + 1, 2 - 2 * pair, 3 - 2 * pair]

    def loads(j):
        m, slot = order[j], j % 2
        copies = [
            pltpu.make_async_copy(kg.at[m], kv.at[0, slot], sems.at[3 * j]),
            pltpu.make_async_copy(vg.at[m], kv.at[1, slot], sems.at[3 * j + 1]),
            pltpu.make_async_copy(act.at[m], acs.at[slot], sems.at[3 * j + 2]),
        ]
        return copies

    load_g = pltpu.make_async_copy(grads, gcg, sems.at[12])
    load_g.start()
    for j in range(2):
        for copy in loads(j):
            copy.start()
    others = [
        pltpu.make_async_copy(sq.at[pl.ds(2 * pair, 2)], sqs, sems.at[13]),
        pltpu.make_async_copy(acts.at[pl.ds(4, 2)], cc, sems.at[14]),
        pltpu.make_async_copy(wts.at[3], wg, sems.at[15]),
        pltpu.make_async_copy(middle, midp.at[pl.ds(8, 1024)], sems.at[16]),
        pltpu.make_async_copy(gy_any.at[row], gy, sems.at[17]),
    ]
    for copy in others:
        copy.start()
    midp[0:8, :] = jnp.zeros((8, 768), jnp.float32)
    load_g.wait()
    waited = False
    stores = []
    for j in range(4):
        slot = j % 2
        for copy in loads(j):
            copy.wait()

        def hidden_back(t, carry):
            r = rows_at(t * WIDE, WIDE)
            spot = pl.ds(t * (WIDE // 128), WIDE // 128)
            active = wide(acs[slot, spot].reshape(WIDE, 768))
            grad = low(dot(gcg[0, r, :], kv[1, slot]) * (2.0 * active))
            if j < 2:
                dh[j, r, :] = grad
            part = dot_nt(grad, kv[0, slot])
            acc[j // 2, r, :] = part if j % 2 == 0 else acc[j // 2, r, :] + part
            return carry

        lax.fori_loop(0, 1024 // WIDE, hidden_back, 0)
        if j < 2:
            for copy in loads(j + 2):
                copy.start()
            if not waited:
                waited = True
                for copy in others:
                    copy.wait()

            def weights(t, carry):
                c = pl.ds(pl.multiple_of(t * 384, 128), 384)
                spot = pl.ds(t * 4, 4)
                key = low(dot_tn(cc[0, :, c], dh[j]))
                stage[j, spot, 0:96, :] = key.reshape(4, 96, 768)
                value = low(dot_tn(gcg[0, :, c], sqs[j].reshape(1024, 768)))
                stage[j, spot, 96:192, :] = value.reshape(4, 96, 768)
                return carry

            lax.fori_loop(0, 2, weights, 0)

    def gate_weights(t, carry):
        c = pl.ds(pl.multiple_of(t * 384, 128), 384)
        gate_w[c, :] = dot_tn(cc[1, :, c], gcg[1])
        return carry

    lax.fori_loop(0, 2, gate_weights, 0)

    def gate_pack(dp, carry):
        for j in range(2):
            start = pl.multiple_of(96 * dp + 48 * pair + 24 * j, 8)
            piece = jnp.concatenate([gate_w[pl.ds(start, 24), :], jnp.zeros((8, 768), jnp.float32)], axis=0)
            stage[j, dp, 192:224, :] = low(piece)
        return carry

    lax.fori_loop(0, 8, gate_pack, 0)
    store = pltpu.make_async_copy(stage, gkv_o, sems.at[18])
    store.start()
    sums[...] = jnp.zeros_like(sums)
    nxt[...] = jnp.zeros_like(nxt)

    def tile(i, carry):
        t = 1024 // TILE - 1 - i
        r = rows_at(t * TILE, TILE)
        keep = cols[r, 1:2]
        grad_key = acc[0, r, :] + acc[1, r, :]
        grad_rec = dot_nt(gcg[1, r, :], wg[...])
        gain = vec(vecs, GAIN2)
        key_mix, rec_mix = vec(vecs, BLEND), vec(vecs, BLEND + 1)
        normal, scale = standardise(midp[pl.ds(pl.multiple_of(t * TILE, 128), TILE + 8), :])
        normed = normal * gain + vec(vecs, BIAS2)
        earlier = pltpu.roll(normed, 1, 0)[8:] * keep
        delta = normed[8:] - earlier
        normal, scale = normal[8:], scale[8:]
        sums[2] += row_sums(grad_key * delta)
        sums[3] += row_sums(grad_rec * delta)
        back = (grad_key * (1.0 - key_mix) + grad_rec * (1.0 - rec_mix)) * keep
        grad = grad_key * key_mix + grad_rec * rec_mix + sooner(back, nxt[0:1, :])
        nxt[0:1, :] = back[0:1]
        sums[0] += row_sums(grad * normal)
        sums[1] += row_sums(grad)
        gm[r, :] = wide(gy[r, :]) + norm_back(grad * gain, normal, scale)
        return carry

    lax.fori_loop(0, 1024 // TILE, tile, 0)
    store_gm = pltpu.make_async_copy(gm, gm_o, sems.at[20])
    store_gm.start()
    for i in range(4):
        sums_o[i : i + 1, :] = jnp.sum(sums[i], axis=0, keepdims=True)
    sums_o[4:8, :] = jnp.zeros((4, 768), jnp.float32)
    store.wait()
    store_gm.wait()
    keep_row.wait()
    arrival.wait_recv()
    messages.finish()


def channel_back(kg, vg, wts, acts, sq, act, grads, middle, gy, out_row, cols, vecs):
    bf, f32 = jnp.bfloat16, jnp.float32
    shape = jax.ShapeDtypeStruct
    return pl.pallas_call(
        channel_back_kernel,
        out_shape=(
            shape((1024, 768), f32), shape((2, 8, 224, 768), bf),
            shape((2, 1024, 768), bf), shape((8, 768), f32),
        ),
        in_specs=[ANY] * 10 + [ON_CORE] * 2,
        out_specs=[ANY] * 3 + [ON_CORE],
        scratch_shapes=[
            pltpu.VMEM((2, 2, 768, 768), bf), pltpu.VMEM((2, 8, 128, 768), bf), pltpu.VMEM((2, 8, 128, 768), bf),
            pltpu.VMEM((2, 1024, 768), bf), pltpu.VMEM((2, 1024, 768), bf), pltpu.VMEM((2, 1024, 768), bf),
            pltpu.VMEM((2, 1024, 768), f32), pltpu.VMEM((768, 768), bf), pltpu.VMEM((1032, 768), f32),
            pltpu.VMEM((1024, 768), bf), pltpu.VMEM((1024, 768), f32), pltpu.VMEM((2, 8, 224, 768), bf),
            pltpu.VMEM((768, 768), f32), pltpu.VMEM((4, 8, 768), f32), pltpu.VMEM((8, 768), f32),
            pltpu.VMEM((1024, 768), bf),
            pltpu.SemaphoreType.DMA((23,)), pltpu.SemaphoreType.DMA, pltpu.SemaphoreType.DMA((1,)),
        ],
        compiler_params=pltpu.CompilerParams(vmem_limit_bytes=LIMIT, collective_id=1, has_side_effects=True),
        name="channel_back",
    )(kg, vg, wts, acts, sq, act, grads, middle, gy, out_row, cols, vecs)


class Scatter:
    def __init__(self, place, messages, source, load_sem, received, kept, steps, final, orders):
        self.p, self.msg, self.load_sem = place, messages, load_sem
        self.source, self.received, self.kept, self.steps, self.final = source, received, kept, steps, final
        self.orders = orders
        self.parts = len(orders)
        self.waits = []

    def cols(self, part):
        width = self.kept.shape[-1] // self.parts
        return pl.ds(part * width, width)

    def start(self):
        p = self.p
        self.core_wait = self.msg.send(self.source.at[:, :, :, :, 1 - p.core], self.received, self.received, p.sib)
        self.load = pltpu.make_async_copy(self.source.at[:, :, :, :, p.core], self.kept, self.load_sem)
        self.load.start()

    def core(self):
        p = self.p
        self.load.wait()
        self.core_wait.wait_recv()
        n = self.kept.shape[0]
        for i in range(n):
            for j in range(2):
                for y in range(2):
                    for x in range(2):
                        total = wide(self.kept[i, j, y, x]) + wide(self.received[i, j, y, x])
                        self.kept[i, j, y, x] = total.astype(self.kept.dtype)
        self.send(0)

    def index(self, order, step, flip):
        p = self.p
        mine = {"x": p.x, "y": p.y, "j": p.mp % 2}
        picked = {}
        for at, axis in enumerate(order):
            if at < step:
                picked[axis] = mine[axis]
            elif at == step:
                picked[axis] = 1 - mine[axis] if flip else mine[axis]
            else:
                picked[axis] = None
        return picked

    def send(self, step):
        p = self.p
        device = {"x": p.xn, "y": p.yn, "j": p.pair}
        self.waits = []
        for part in range(self.parts):
            order = self.orders[part]
            picked = self.index(order, step, True)
            select = tuple(ALL if picked[a] is None else picked[a] for a in "jyx")
            piece = self.kept.at[(ALL,) + select + (ALL, self.cols(part))]
            target = self.steps[step].at[part]
            self.waits.append(self.msg.send(piece, target, target, device[order[step]]))

    def add(self, step):
        for part in range(self.parts):
            order = self.orders[part]
            self.waits[part].wait_recv()
            picked = self.index(order, step, False)
            free = [a for a in "jyx" if picked[a] is None]
            n = self.kept.shape[0]
            for i in range(n):
                for number in range(2 ** len(free)):
                    bits = {a: (number >> (len(free) - 1 - k)) & 1 for k, a in enumerate(free)}
                    select = tuple(bits[a] if picked[a] is None else picked[a] for a in "jyx")
                    spot = (i,) + select + (ALL, self.cols(part))
                    arrived = self.steps[step][(part, i) + tuple(bits[a] for a in free)]
                    total = wide(self.kept[spot]) + wide(arrived)
                    if step == 2:
                        self.final[i, :, self.cols(part)] = total
                    else:
                        self.kept[spot] = total.astype(self.kept.dtype)
        if step < 2:
            self.send(step + 1)


def scatter_scratch(n, rows, cols, parts, dtype):
    width = cols // parts
    return [
        pltpu.VMEM((n, 2, 2, 2, rows, cols), dtype), pltpu.VMEM((n, 2, 2, 2, rows, cols), dtype),
        pltpu.VMEM((parts, n, 2, 2, rows, width), dtype), pltpu.VMEM((parts, n, 2, rows, width), dtype),
        pltpu.VMEM((parts, n, rows, width), dtype),
    ]


def time_back_kernel(
    wts, acts, kvs, gm_any, x_any, gkv_any, cols, doc_row, vecs, sums_c,
    ig_o, gkv_o, gt_o, small_o,
    w4, ins, f5, gm, xp, gb, gkvr, pack, tables, sums, nxt, small_cut, *scratch,
):
    kv_scratch, s_scratch = scratch[:5], scratch[5:10]
    t_scratch = [scratch[10 + 5 * i : 15 + 5 * i] for i in range(4)]
    sems, send_sem, recv_sems = scratch[30:]
    place_of = Place()
    mp = place_of.mp
    row, pair = mp % 2, mp // 2
    loads = [
        pltpu.make_async_copy(gm_any, gm, sems.at[0]),
        pltpu.make_async_copy(wts.at[pl.ds(0, 3)], w4.at[pl.ds(0, 3)], sems.at[1]),
        pltpu.make_async_copy(wts.at[4], w4.at[3], sems.at[5]),
        pltpu.make_async_copy(kvs, f5, sems.at[2]),
        pltpu.make_async_copy(x_any.at[row], xp.at[pl.ds(16, 1024)], sems.at[3]),
        pltpu.make_async_copy(acts.at[pl.ds(0, 4)], ins, sems.at[4]),
    ]
    for copy in loads:
        copy.start()
    greet([place_of.sib, place_of.xn, place_of.yn, place_of.pair])
    messages = Messages(send_sem, recv_sems)
    channel = Scatter(place_of, messages, gkv_any, sems.at[8], kv_scratch[0], kv_scratch[1], kv_scratch[2:], gkv_o, ("xyj", "yxj"))
    vectors = Scatter(place_of, messages, small_cut, sems.at[9], s_scratch[0], s_scratch[1], s_scratch[2:], small_o, ("xyj",))
    mixing = []
    for i in range(4):
        buffers = t_scratch[i]
        final = gt_o.at[pl.ds(i, 1)]
        order = ("xyj", "yxj")[i % 2]
        mixing.append(Scatter(place_of, messages, pack.at[pl.ds(i, 1)], sems.at[10 + i], buffers[0], buffers[1], buffers[2:], final, (order,)))
    channel.start()
    xp[0:16, :] = jnp.zeros((16, 768), jnp.bfloat16)
    rate = jnp.exp(vec(vecs, DECAY))
    fade = jnp.exp(-rate)
    place = wide(lax.broadcasted_iota(jnp.int32, (SPAN, 1), 0))
    tables[0] = jnp.exp((64.0 - place) * rate)
    tables[1] = jnp.exp((place - 63.0) * rate)
    tables[2] = jnp.exp((place - 127.0) * rate)
    sums[...] = jnp.zeros_like(sums)
    nxt[...] = jnp.zeros_like(nxt)
    for copy in loads:
        copy.wait()

    def tile(t):
        r = pl.ds(t * TILE, TILE)
        keep = cols[r, 1:2]
        grad_middle = gm[r, :]
        branch = low(grad_middle)
        gb[r, :] = branch
        grad_gated = dot_nt(branch, w4[3])
        keys, values, gate, top, bottom = (f5[i, r, :] for i in range(5))
        key_exp = jnp.exp(keys)
        bonus = jnp.exp(keys + vec(vecs, FIRST))
        inverse = 1.0 / (bottom + bonus)
        mixed = (top + bonus * values) * inverse
        grad_mixed = grad_gated * gate
        gkvr[2, r, :] = low(grad_mixed * mixed * (1.0 - gate))
        grad_top = grad_mixed * inverse
        grad_bottom = -grad_top * mixed
        time = lax.broadcasted_iota(jnp.int32, (SPAN, SPAN), 0)
        source = lax.broadcasted_iota(jnp.int32, (SPAN, SPAN), 1)
        tops, bottoms = [], []
        for i in reversed(range(TILE // SPAN)):
            q = pl.ds(t * TILE + i * SPAN, SPAN)
            block = t * (TILE // SPAN) + i
            part = slice(i * SPAN, (i + 1) * SPAN)
            same = cols[q, 0:1] == doc_row[block : block + 1, :]
            mask = jnp.where(same & (source > time), 1.0, 0.0).astype(jnp.bfloat16)
            link = cols[q, 3:4] * tables[2]
            state_top = masked_sum(mask, grad_top[part] * tables[0]) * tables[1] + link * nxt[1:2, :]
            state_bottom = masked_sum(mask, grad_bottom[part] * tables[0]) * tables[1] + link * nxt[2:3, :]
            nxt[1:2, :] = fade * state_top[:1] + grad_top[part][:1]
            nxt[2:3, :] = fade * state_bottom[:1] + grad_bottom[part][:1]
            tops.insert(0, state_top)
            bottoms.insert(0, state_bottom)
        state_top, state_bottom = jnp.concatenate(tops, axis=0), jnp.concatenate(bottoms, axis=0)
        own = bonus * (grad_top * (values - mixed))
        sums[0] += row_sums(own)
        sums[1] += row_sums(state_top * top + state_bottom * bottom)
        grads = (
            low(own + key_exp * (state_top * values + state_bottom)),
            low(bonus * grad_top + key_exp * state_top),
            gkvr[2, r, :],
        )
        gkvr[0, r, :] = grads[0]
        gkvr[1, r, :] = grads[1]
        gain = vec(vecs, GAIN1)
        window = wide(xp[pl.ds(t * TILE, TILE + 16), :])
        normal, scale = standardise(window)
        normed = normal * gain + vec(vecs, BIAS1)
        earlier = pltpu.roll(normed, 1, 0)[16:] * keep
        delta = normed[16:] - earlier
        normal, scale = normal[16:], scale[16:]
        back = jnp.zeros((TILE, 768), jnp.float32)
        grad = jnp.zeros((TILE, 768), jnp.float32)
        for j in range(3):
            mix = vec(vecs, MIX + j)
            into = dot_nt(grads[j], w4[j])
            sums[4 + j] += row_sums(into * delta)
            grad += into * mix
            back += into * (1.0 - mix)
        back = back * keep
        grad = grad + sooner(back, nxt[0:1, :])
        nxt[0:1, :] = back[0:1]
        sums[2] += row_sums(grad * normal)
        sums[3] += row_sums(grad)
        xp[pl.ds(t * TILE + 16, TILE), :] = low(grad_middle + norm_back(grad * gain, normal, scale))

    arrivals = []
    keeps = []
    for t in reversed(range(1024 // TILE)):
        tile(t)
        r = pl.ds(t * TILE, TILE)
        done = xp.at[pl.ds(t * TILE + 16, TILE)]
        arrivals.append(messages.send(done, ig_o.at[row, r], ig_o.at[1 - row, r], place_of.pair))
        keeps.append(pltpu.make_async_copy(done, ig_o.at[row, r], sems.at[14 + t]))
        keeps[-1].start()
        if t == 3:
            channel.core()
        elif t == 1:
            channel.add(0)
        elif t == 0:
            channel.add(1)

    def product(slot, left, right):
        def body(t, carry):
            c = pl.ds(pl.multiple_of(t * 384, 128), 384)
            f5[0, c, :] = dot_tn(left[:, c], right[...])
            return carry

        lax.fori_loop(0, 2, body, 0)

        def packed(dp, carry):
            for j in range(2):
                start = pl.multiple_of(96 * dp + 48 * pair + 24 * j, 8)
                piece = jnp.concatenate([f5[0, pl.ds(start, 24), :], jnp.zeros((8, 768), jnp.float32)], axis=0)
                pack[slot, j, dp // 4, (dp // 2) % 2, dp % 2] = low(piece)
            return carry

        lax.fori_loop(0, 8, packed, 0)
        mixing[slot].start()

    totals = [jnp.sum(sums[i], axis=0, keepdims=True) for i in range(7)]
    totals[1] = totals[1] * (-rate * fade)
    small = jnp.concatenate([sums_c[0:4, :]] + totals + [jnp.zeros((5, 768), jnp.float32)], axis=0)
    turned = pltpu.roll(small, (768 - 48 * pair) % 768, 1)
    for dp in range(8):
        for j in range(2):
            start = 96 * dp + 24 * j
            piece = turned if start == 0 else pltpu.roll(turned, 768 - start, 1)
            small_cut[0, j, dp // 4, (dp // 2) % 2, dp % 2] = piece[:, :128]
    vectors.start()
    product(0, ins.at[0], gkvr.at[0])
    vectors.core()
    product(1, ins.at[1], gkvr.at[1])
    mixing[0].core()
    product(2, ins.at[2], gkvr.at[2])
    mixing[1].core()
    mixing[0].add(0)
    vectors.add(0)
    product(3, ins.at[3], gb)
    mixing[2].core()
    mixing[1].add(0)
    mixing[0].add(1)
    mixing[3].core()
    mixing[2].add(0)
    mixing[1].add(1)
    vectors.add(1)
    mixing[3].add(0)
    mixing[2].add(1)
    mixing[3].add(1)
    channel.add(2)
    vectors.add(2)
    for group in mixing:
        group.add(2)
    for copy in keeps:
        copy.wait()
    for wait in arrivals:
        wait.wait_recv()
    messages.finish()


def time_back(wts, acts, kvs, gm, x, gkv, cols, doc_row, vecs, sums_c):
    bf, f32 = jnp.bfloat16, jnp.float32
    shape = jax.ShapeDtypeStruct
    return pl.pallas_call(
        time_back_kernel,
        out_shape=(
            shape((2, 1024, 768), bf), shape((1, 224, 768), f32), shape((4, 32, 768), f32), shape((1, 16, 128), f32),
        ),
        in_specs=[ANY] * 6 + [ON_CORE] * 4,
        out_specs=[ANY] + [ON_CORE] * 3,
        scratch_shapes=[
            pltpu.VMEM((4, 768, 768), bf), pltpu.VMEM((4, 1024, 768), bf), pltpu.VMEM((5, 1024, 768), f32),
            pltpu.VMEM((1024, 768), f32), pltpu.VMEM((1040, 768), bf), pltpu.VMEM((1024, 768), bf),
            pltpu.VMEM((3, 1024, 768), bf),
            pltpu.VMEM((4, 2, 2, 2, 2, 32, 768), bf), pltpu.VMEM((3, SPAN, 768), f32), pltpu.VMEM((7, 8, 768), f32),
            pltpu.VMEM((8, 768), f32), pltpu.VMEM((1, 2, 2, 2, 2, 16, 128), f32),
        ]
        + scatter_scratch(1, 224, 768, 2, bf)
        + scatter_scratch(1, 16, 128, 1, f32)
        + scatter_scratch(1, 32, 768, 1, bf) * 4
        + [pltpu.SemaphoreType.DMA((18,)), pltpu.SemaphoreType.DMA, pltpu.SemaphoreType.DMA((32,))],
        compiler_params=pltpu.CompilerParams(vmem_limit_bytes=LIMIT, collective_id=2, has_side_effects=True),
        name="time_back",
    )(wts, acts, kvs, gm, x, gkv, cols, doc_row, vecs, sums_c)


def on_device(
    residual_input, article_numbers, upstream_gradient,
    prenorm_scaling, prenorm_offset, postnorm_scaling, postnorm_offset,
    attention_blend, feedforward_blend, forgetting_logrates, present_reward,
    projection_matrices, final_matrix, address_matrix, content_matrix,
):
    dp, mp = lax.axis_index("dp"), lax.axis_index("mp")
    place = dp * 4 + mp
    vectors = jnp.concatenate(
        [
            prenorm_scaling[None], prenorm_offset[None], postnorm_scaling[None], postnorm_offset[None],
            attention_blend, forgetting_logrates[None], present_reward[None], feedforward_blend,
            jnp.zeros((5, 24), jnp.bfloat16),
        ],
        axis=0,
    )
    spread = lax.dynamic_update_slice(jnp.zeros((16, 384), jnp.bfloat16), vectors, (0, 24 * (place % 16)))
    spread = jnp.concatenate([spread[:8], spread[8:]], axis=1)
    packed = jnp.concatenate([projection_matrices.reshape(96, 768), final_matrix, spread], axis=0)
    docs = lax.dynamic_index_in_dim(article_numbers, mp % 2, 0, keepdims=False)
    doc_row = docs.reshape(8, 128)
    blocks = doc_row.astype(jnp.float32)
    keep = jnp.concatenate([jnp.zeros((1,), jnp.bool_), docs[1:] == docs[:-1]]).astype(jnp.float32)
    before = jnp.concatenate([jnp.full((1,), -1.0, jnp.float32), blocks[:-1, 127]])
    after = jnp.concatenate([blocks[1:, 0], jnp.full((1,), -1.0, jnp.float32)])
    cols = jnp.stack(
        [
            docs.astype(jnp.float32), keep,
            (blocks == before[:, None]).astype(jnp.float32).reshape(1024),
            (blocks == after[:, None]).astype(jnp.float32).reshape(1024),
        ],
        axis=1,
    )
    kg, vg, acts, kvs, middle, sq, act, grads, out_row, wts, vecs = forward(
        packed, address_matrix, content_matrix.T, residual_input, upstream_gradient, cols, blocks
    )
    kg, vg, sq = kg.reshape(4, 768, 768), vg.reshape(4, 768, 768), sq.reshape(4, 8, 128, 768)
    gm, gkv, output, sums_c = channel_back(
        kg, vg, wts, acts, sq, act, grads, middle, upstream_gradient, out_row, cols, vecs
    )
    input_grad, gkv, gt, small = time_back(
        wts, acts, kvs, gm, residual_input, gkv.reshape(1, 2, 2, 2, 2, 224, 768), cols, blocks, vecs, sums_c
    )
    small = small[0, :, :24]
    gkv = gkv[0]
    grad_mix = jnp.stack([gt[0, :24], gt[1, :24], gt[2, :24], gkv[192:216]], axis=0)
    return (
        output, input_grad.astype(jnp.float32),
        small[6], small[7], small[0], small[1],
        small[8:11], small[2:4], small[5], small[4],
        grad_mix, gt[3, :24], gkv[:96], gkv[96:192].T,
    )


def fits(mesh):
    return dict(mesh.shape) == {"dp": 8, "mp": 4}


def solution(mesh):
    return jax.shard_map(
        on_device if fits(mesh) else general_device,
        mesh=mesh,
        in_specs=(
            P("dp", None, None),
            P("dp", None),
            P("dp", None, None),
            P(("dp", "mp")),
            P(("dp", "mp")),
            P(("dp", "mp")),
            P(("dp", "mp")),
            P(None, ("dp", "mp")),
            P(None, ("dp", "mp")),
            P(("dp", "mp")),
            P(("dp", "mp")),
            P(None, ("dp", "mp"), None),
            P(("dp", "mp"), None),
            P("dp", "mp"),
            P("mp", "dp"),
        ),
        out_specs=(
            P("dp", None, None),
            P("dp", None, None),
            P(("dp", "mp")),
            P(("dp", "mp")),
            P(("dp", "mp")),
            P(("dp", "mp")),
            P(None, ("dp", "mp")),
            P(None, ("dp", "mp")),
            P(("dp", "mp")),
            P(("dp", "mp")),
            P(None, ("dp", "mp"), None),
            P(("dp", "mp"), None),
            P("dp", "mp"),
            P("mp", "dp"),
        ),
        check_vma=False,
    )
```

```python
import functools

import jax
import jax.numpy as jnp
from jax import lax
from jax.experimental import pallas as pl
from jax.experimental.pallas import tpu as pltpu
from jax.sharding import PartitionSpec as P

BLOCK = 64
MICRO = 2


epsilon = 1e-05


def layer_norm(values_in, gain_vec, bias_vec):
    average = jnp.mean(values_in, axis=-1, keepdims=True)
    centered = values_in - average
    variance = jnp.mean(centered * centered, axis=-1, keepdims=True)
    return centered * lax.rsqrt(variance + epsilon) * gain_vec + bias_vec


def shifted(values_in, retain_marker):
    earlier = jnp.concatenate([jnp.zeros_like(values_in[:, :1]), values_in[:, :-1]], axis=1)
    return earlier * retain_marker[:, :, None]


def blend(normed, earlier, factor):
    return normed * factor + earlier * (1.0 - factor)


def project(operand, weights):
    return lax.dot_general(
        operand, weights, (((2,), (0,)), ((), ())), preferred_element_type=jnp.float32
    )


def back_project(gradient, weights):
    return lax.dot_general(
        gradient, weights, (((2,), (1,)), ((), ())), preferred_element_type=jnp.float32
    )


def weight_grad(operand, gradient):
    return lax.dot_general(
        operand, gradient, (((0, 1), (0, 1)), ((), ())), preferred_element_type=jnp.float32
    )


def take_share(array, axis_at, groups, shares, place):
    shape = array.shape
    piece_len = shape[axis_at] // (groups * shares)
    split_shape = shape[:axis_at] + (groups, shares, piece_len) + shape[axis_at + 1 :]
    chosen = lax.dynamic_index_in_dim(
        array.reshape(split_shape), place, axis_at + 1, keepdims=False
    )
    return chosen.reshape(shape[:axis_at] + (groups * piece_len,) + shape[axis_at + 1 :])


def first_piece(stream_f, gain_vec, bias_vec, factors, retain_marker):
    normed = layer_norm(stream_f, gain_vec, bias_vec)
    earlier = shifted(normed, retain_marker)
    return (
        blend(normed, earlier, factors[0]),
        blend(normed, earlier, factors[1]),
        blend(normed, earlier, factors[2]),
    )


def channel_piece(middle, gain_vec, bias_vec, factors, retain_marker):
    normed = layer_norm(middle, gain_vec, bias_vec)
    earlier = shifted(normed, retain_marker)
    return (blend(normed, earlier, factors[0]), blend(normed, earlier, factors[1]))


def time_piece(
    address_series,
    content_series,
    acceptance_gate,
    forgetting_logrates,
    present_reward,
    retain_marker,
    article_labels,
    span_length,
):
    batch_rows, length, feature_count = address_series.shape
    block_count = length // span_length
    decay_rate = jnp.exp(forgetting_logrates)
    position = jnp.arange(span_length, dtype=jnp.float32)[:, None]
    rising = jnp.exp(position * decay_rate)
    sinking = jnp.exp(-position * decay_rate)
    falling = jnp.exp(-(position + 1.0) * decay_rate)
    rising = jnp.concatenate([rising, rising], axis=-1)
    sinking = jnp.concatenate([sinking, sinking], axis=-1)
    falling = jnp.concatenate([falling, falling], axis=-1)
    whole_fade = jnp.exp(-span_length * decay_rate)
    whole_fade = jnp.concatenate([whole_fade, whole_fade], axis=-1)
    key_exp = jnp.exp(address_series)
    weighted = jnp.concatenate([key_exp * content_series, key_exp], axis=-1)
    weighted = weighted.reshape(batch_rows, block_count, span_length, 2 * feature_count)
    block_docs = article_labels.reshape(batch_rows, block_count, span_length)
    causal = jnp.arange(span_length)[:, None] >= jnp.arange(span_length)[None, :]
    same_doc = block_docs[:, :, :, None] == block_docs[:, :, None, :]
    doc_mask = (causal[None, None] & same_doc).astype(jnp.float32)
    partial_value = (
        jnp.einsum("rnji,rnid->rnjd", doc_mask, weighted * rising, precision=lax.Precision.HIGHEST)
        * sinking
    )
    last_docs = block_docs[:, :, -1]
    prior_docs = jnp.concatenate(
        [jnp.full((batch_rows, 1), -1, jnp.int32), last_docs[:, :-1]], axis=1
    )
    linked = (block_docs == prior_docs[:, :, None]).astype(jnp.float32)
    chained = linked[:, :, -1]

    def carry_step(state, pieces):
        tail_state, joined = pieces
        return (tail_state + whole_fade * joined[:, None] * state, state)

    zero_state = jnp.zeros((batch_rows, 2 * feature_count), jnp.float32)
    _, starts = lax.scan(
        carry_step,
        zero_state,
        (jnp.swapaxes(partial_value[:, :, -1], 0, 1), jnp.swapaxes(chained, 0, 1)),
    )
    starts = jnp.swapaxes(starts, 0, 1)
    states = partial_value + falling * linked[..., None] * starts[:, :, None, :]
    states = states.reshape(batch_rows, length, 2 * feature_count)
    entering_memory = shifted(states, retain_marker)
    reward_power = jnp.exp(present_reward + address_series)
    accumulated_dividend = entering_memory[..., :feature_count] + reward_power * content_series
    accumulated_divisor = entering_memory[..., feature_count:] + reward_power
    return jax.nn.sigmoid(acceptance_gate) * (accumulated_dividend / accumulated_divisor)


def general_device(
    residual_input,
    article_numbers,
    upstream_gradient,
    prenorm_scaling,
    prenorm_offset,
    postnorm_scaling,
    postnorm_offset,
    attention_blend,
    feedforward_blend,
    forgetting_logrates,
    present_reward,
    projection_matrices,
    final_matrix,
    address_matrix,
    content_matrix,
):
    batch_rows = residual_input.shape[0] // MICRO
    same_doc = article_numbers[:, 1:] == article_numbers[:, :-1]
    keep_all = jnp.concatenate([jnp.zeros_like(same_doc[:, :1]), same_doc], axis=1).astype(
        jnp.float32
    )
    groups = lax.axis_size("dp")
    shares = lax.axis_size("mp")
    mp_place = lax.axis_index("mp")
    totals = None
    outputs = []
    input_grads = []
    for micro_index in range(MICRO):
        shared = (
            lax.all_gather(prenorm_scaling, ("dp", "mp"), axis=0, tiled=True),
            lax.all_gather(prenorm_offset, ("dp", "mp"), axis=0, tiled=True),
            lax.all_gather(postnorm_scaling, ("dp", "mp"), axis=0, tiled=True),
            lax.all_gather(postnorm_offset, ("dp", "mp"), axis=0, tiled=True),
            lax.all_gather(attention_blend, ("dp", "mp"), axis=1, tiled=True),
            lax.all_gather(feedforward_blend, ("dp", "mp"), axis=1, tiled=True),
            lax.all_gather(forgetting_logrates, ("dp", "mp"), axis=0, tiled=True),
            lax.all_gather(present_reward, ("dp", "mp"), axis=0, tiled=True),
            lax.all_gather(projection_matrices, ("dp", "mp"), axis=1, tiled=True),
            lax.all_gather(final_matrix, ("dp", "mp"), axis=0, tiled=True),
        )
        local = (
            lax.all_gather(address_matrix, "dp", axis=0, tiled=True),
            lax.all_gather(content_matrix, "dp", axis=1, tiled=True),
        )
        fetched = (shared, local)
        shared, local = fetched
        gain_one, bias_one, gain_two, bias_two, tmix_w, cmix_w, decay_w, first_w, mix_w, out_w = (
            shared
        )
        key_w, value_w = local
        mix_part = take_share(mix_w[0:3], 2, groups, shares, mp_place)
        out_part = take_share(out_w, 0, groups, shares, mp_place)
        decay_part = take_share(decay_w, 0, groups, shares, mp_place)
        first_part = take_share(first_w, 0, groups, shares, mp_place)
        lower_row = micro_index * batch_rows
        upper_row = lower_row + batch_rows
        stream_f = residual_input[lower_row:upper_row].astype(jnp.float32)
        retain_marker = keep_all[lower_row:upper_row]
        article_labels = article_numbers[lower_row:upper_row]
        grad_out = upstream_gradient[lower_row:upper_row].astype(jnp.float32)

        def first_local(values_in, gain_vec, bias_vec, factors):
            return first_piece(values_in, gain_vec, bias_vec, factors, retain_marker)

        def time_local(address_series, content_series, acceptance_gate, decay_vec, first_vec):
            return time_piece(
                address_series,
                content_series,
                acceptance_gate,
                decay_vec,
                first_vec,
                retain_marker,
                article_labels,
                BLOCK,
            )

        def channel_local(values_in, gain_vec, bias_vec, factors):
            return channel_piece(values_in, gain_vec, bias_vec, factors, retain_marker)

        mixes, pull_first = jax.vjp(
            first_local,
            stream_f,
            gain_one.astype(jnp.float32),
            bias_one.astype(jnp.float32),
            tmix_w.astype(jnp.float32),
        )
        key_in = mixes[0].astype(jnp.bfloat16)
        value_in = mixes[1].astype(jnp.bfloat16)
        rec_in = mixes[2].astype(jnp.bfloat16)
        address_series = project(key_in, mix_part[0])
        content_series = project(value_in, mix_part[1])
        acceptance_gate = project(rec_in, mix_part[2])
        gated, pull_time = jax.vjp(
            time_local,
            address_series,
            content_series,
            acceptance_gate,
            decay_part.astype(jnp.float32),
            first_part.astype(jnp.float32),
        )
        gated_low = gated.astype(jnp.bfloat16)
        branch = project(gated_low, out_part)
        branch = lax.psum(branch, "mp")
        middle = stream_f + branch
        channel_ins, pull_channel = jax.vjp(
            channel_local,
            middle,
            gain_two.astype(jnp.float32),
            bias_two.astype(jnp.float32),
            cmix_w.astype(jnp.float32),
        )
        ckey_in = channel_ins[0].astype(jnp.bfloat16)
        crec_in = channel_ins[1].astype(jnp.bfloat16)
        hidden = project(ckey_in, key_w)
        active = jax.nn.relu(hidden)
        squared = (active * active).astype(jnp.bfloat16)
        carried = lax.psum(project(squared, value_w).astype(jnp.bfloat16), "mp").astype(jnp.float32)
        gate_sig = jax.nn.sigmoid(project(crec_in, mix_w[3]))
        outputs.append((middle + gate_sig * carried).astype(jnp.bfloat16))
        grad_carried = (grad_out * gate_sig).astype(jnp.bfloat16)
        grad_gate = (grad_out * carried * gate_sig * (1.0 - gate_sig)).astype(jnp.bfloat16)
        grad_value_w = weight_grad(squared, grad_carried)
        grad_hidden = (back_project(grad_carried, value_w) * 2.0 * active).astype(jnp.bfloat16)
        grad_key_w = weight_grad(ckey_in, grad_hidden)
        grad_crec_w = weight_grad(crec_in, grad_gate)
        grad_ckey = lax.psum(back_project(grad_hidden, key_w).astype(jnp.bfloat16), "mp").astype(
            jnp.float32
        )
        grad_crec = back_project(grad_gate, mix_w[3])
        grad_middle, grad_gain_two, grad_bias_two, grad_cmix = pull_channel((grad_ckey, grad_crec))
        grad_middle = grad_middle + grad_out
        grad_branch = grad_middle.astype(jnp.bfloat16)
        grad_out_w = weight_grad(gated_low, grad_branch)
        grad_gated = back_project(grad_branch, out_part)
        grad_keys, grad_values, grad_recept, grad_decay, grad_first = pull_time(grad_gated)
        grad_keys = grad_keys.astype(jnp.bfloat16)
        grad_values = grad_values.astype(jnp.bfloat16)
        grad_recept = grad_recept.astype(jnp.bfloat16)
        grad_mix_three = jnp.stack(
            [
                weight_grad(key_in, grad_keys),
                weight_grad(value_in, grad_values),
                weight_grad(rec_in, grad_recept),
            ]
        )
        grad_ins = (
            back_project(grad_keys, mix_part[0]),
            back_project(grad_values, mix_part[1]),
            back_project(grad_recept, mix_part[2]),
        )
        pulled = pull_first(grad_ins)
        pulled = (
            lax.psum(pulled[0].astype(jnp.bfloat16), "mp").astype(jnp.float32),
            lax.psum(pulled[1].astype(jnp.bfloat16), "mp").astype(jnp.float32),
            lax.psum(pulled[2].astype(jnp.bfloat16), "mp").astype(jnp.float32),
            lax.psum(pulled[3].astype(jnp.bfloat16), "mp").astype(jnp.float32),
        )
        grad_stream, grad_gain_one, grad_bias_one, grad_tmix = pulled
        input_grads.append(grad_stream + grad_middle)
        current = [
            grad_gain_one,
            grad_bias_one,
            grad_gain_two,
            grad_bias_two,
            grad_tmix,
            grad_cmix,
            grad_decay,
            grad_first,
            grad_mix_three,
            grad_crec_w,
            grad_out_w,
            grad_key_w,
            grad_value_w,
        ]
        totals = (
            current
            if totals is None
            else [earlier + latest for earlier, latest in zip(totals, current)]
        )

    def pick(gradient, axis_at):
        return take_share(gradient, axis_at, groups, shares, mp_place)

    split_grads = (
        lax.psum_scatter(pick(totals[0], 0), "dp", scatter_dimension=0, tiled=True),
        lax.psum_scatter(pick(totals[1], 0), "dp", scatter_dimension=0, tiled=True),
        lax.psum_scatter(pick(totals[2], 0), "dp", scatter_dimension=0, tiled=True),
        lax.psum_scatter(pick(totals[3], 0), "dp", scatter_dimension=0, tiled=True),
        lax.psum_scatter(pick(totals[4], 1), "dp", scatter_dimension=1, tiled=True),
        lax.psum_scatter(pick(totals[5], 1), "dp", scatter_dimension=1, tiled=True),
        lax.psum_scatter(totals[6], "dp", scatter_dimension=0, tiled=True),
        lax.psum_scatter(totals[7], "dp", scatter_dimension=0, tiled=True),
        lax.psum_scatter(totals[10], "dp", scatter_dimension=0, tiled=True),
    )
    feature_count = totals[9].shape[0]
    share_mask = jax.nn.one_hot(mp_place, shares, dtype=jnp.float32)
    three_full = (
        totals[8].reshape(3, feature_count, groups, 1, feature_count // (groups * shares))
        * share_mask[None, None, None, :, None]
    )
    three_full = three_full.reshape(3, feature_count, feature_count)
    crec_grad = totals[9] * (mp_place == 0).astype(jnp.float32)
    mix_grad = lax.psum_scatter(
        jnp.concatenate([three_full, crec_grad[None]], axis=0),
        ("dp", "mp"),
        scatter_dimension=1,
        tiled=True,
    )
    shared_grads = (
        split_grads[0],
        split_grads[1],
        split_grads[2],
        split_grads[3],
        split_grads[4],
        split_grads[5],
        split_grads[6],
        split_grads[7],
        mix_grad,
        split_grads[8],
    )
    channel_grads = (
        lax.psum_scatter(totals[11], "dp", scatter_dimension=0, tiled=True),
        lax.psum_scatter(totals[12], "dp", scatter_dimension=1, tiled=True),
    )
    output = jnp.concatenate(outputs, axis=0)
    input_grad = jnp.concatenate(input_grads, axis=0)
    return (
        output,
        input_grad,
        shared_grads[0],
        shared_grads[1],
        shared_grads[2],
        shared_grads[3],
        shared_grads[4],
        shared_grads[5],
        shared_grads[6],
        shared_grads[7],
        shared_grads[8],
        shared_grads[9],
        channel_grads[0],
        channel_grads[1],
    )


MESH = pl.DeviceIdType.MESH
MIB = 2**20

class Place:
    def __init__(self):
        self.dp = lax.axis_index("dp")
        self.mp = lax.axis_index("mp")
        self.core = self.dp % 2
        self.x = (self.dp // 2) % 2
        self.y = self.dp // 4
        self.sib = (self.dp + 1 - 2 * self.core, self.mp)
        self.xn = (self.dp + 2 - 4 * self.x, self.mp)
        self.yn = (self.dp + 4 - 8 * self.y, self.mp)
        self.up_z = (self.mp + 1) % 4
        self.down_z = (self.mp + 3) % 4
        self.far_z = (self.mp + 2) % 4
        self.up = (self.dp, self.up_z)
        self.down = (self.dp, self.down_z)
        self.pair = (self.dp, self.mp + 1 - 2 * (self.mp % 2))


def greet(devices):
    barrier = pltpu.get_barrier_semaphore()
    for device in devices:
        pl.semaphore_signal(barrier, inc=1, device_id=device, device_id_type=MESH)
    pl.semaphore_wait(barrier, len(devices))


class Messages:
    def __init__(self, send_sem, recv_sems):
        self.send_sem, self.recv_sems, self.count, self.sent = send_sem, recv_sems, 0, []

    def send(self, source, target, arrival, device, when=None):
        index = self.count
        self.count += 1
        copy = pltpu.make_async_remote_copy(source, target, self.send_sem, self.recv_sems.at[index], device_id=device, device_id_type=MESH)
        only(when, copy.start)
        self.sent.append((when, copy))
        return pltpu.make_async_remote_copy(arrival, arrival, self.send_sem, self.recv_sems.at[index], device_id=device, device_id_type=MESH)

    def finish(self):
        for when, copy in self.sent:
            only(when, copy.wait_send)
        self.sent = []


def only(when, action):
    if when is None:
        action()
    else:
        pl.when(when)(action)


ALL = slice(None)


class Stream:
    def __init__(self, place, messages, order, piece, own, twin_sem):
        self.p, self.msg, self.order, self.piece, self.own, self.twin_sem = place, messages, order, piece, own, twin_sem
        p = place
        self.first = order.replace("z", "")[0]
        self.z_leads = order[0] == "z"
        self.a, self.b = (p.x, p.y) if self.first == "x" else (p.y, p.x)
        self.na, self.nb = (p.xn, p.yn) if self.first == "x" else (p.yn, p.xn)
        self.base = messages.count
        messages.count += 15

    def at(self, col, other, slab, core=None):
        a = self.a if col == 0 else 1 - self.a
        b = 1 - self.b if other else self.b
        y, x = (b, a) if self.first == "x" else (a, b)
        return self.piece(y, x, self.p.core if core is None else core, slab)

    def slab(self, j):
        m = self.p.mp
        if j == 0:
            return m
        flip = (m >= 2).astype(jnp.int32)
        near = m + flip * (3 - 2 * m)
        picked = j - (j <= near).astype(jnp.int32)
        return picked + flip * (3 - 2 * picked)

    def rank(self, m, slab):
        flip = (m >= 2).astype(jnp.int32)
        near = m + flip * (3 - 2 * m)
        picked = slab + flip * (3 - 2 * slab)
        return picked - (picked > near).astype(jnp.int32) + 1

    def index(self, kind, col, j):
        if self.z_leads:
            return self.base + {"z": j - 1, "a": 3 + j, "b": 7 + 4 * col + j}[kind]
        return self.base + {"z": 3 * col + j - 1, "a": 6, "b": 7 + 4 * col + j}[kind]

    def copy(self, piece, index, device, when=None, source=None):
        copy = pltpu.make_async_remote_copy(
            piece if source is None else source, piece, self.msg.send_sem, self.msg.recv_sems.at[index],
            device_id=device, device_id_type=MESH,
        )
        only(when, copy.start)
        self.msg.sent.append((when, copy))

    def twin(self, col, other, slab, source=None):
        piece = self.at(col, other, slab)
        sem = self.twin_sem(slab)
        copy = pltpu.make_async_remote_copy(
            piece if source is None else source, piece, self.msg.send_sem, sem,
            device_id=self.p.sib, device_id_type=MESH,
        )
        copy.start()
        self.msg.sent.append((None, copy))

    def send_z(self, col, j, source=None):
        m = self.p.mp
        slab = self.slab(j)
        piece = self.at(col, 0, slab)
        if j == 0:
            self.copy(piece, self.index("z", col, 1) + self.rank(m + 1, slab) - 1, self.p.up, m < 3, source)
            self.copy(piece, self.index("z", col, 1) + self.rank(m - 1, slab) - 1, self.p.down, m > 0, source)
            return
        target = m - 1 + 2 * (slab < m).astype(jnp.int32)
        safe = (target + 4) % 4
        self.copy(piece, self.index("z", col, 1) + self.rank(target, slab) - 1, (self.p.dp, safe), (target >= 0) & (target <= 3))

    def send_a(self, j, source=None):
        self.copy(self.at(0, 0, self.slab(j)), self.index("a", 0, j), self.na, source=source)

    def send_b(self, col, j, source=None):
        self.copy(self.at(col, 0, self.slab(j)), self.index("b", col, j), self.nb, source=source)

    def event(self, kind, col, j):
        if kind == "o":
            self.send_z(0, 0, self.own)
            self.send_a(0, self.own)
            self.send_b(0, 0, self.own)
            self.twin(0, 0, self.p.mp, self.own)
            return
        slab = self.slab(j)
        piece = self.at(1 if kind == "a" else col, kind == "b", slab)
        sem = self.msg.recv_sems.at[self.index(kind, col, j)]
        pltpu.make_async_remote_copy(piece, piece, self.msg.send_sem, sem, device_id=self.na, device_id_type=MESH).wait_recv()
        if kind == "z":
            self.send_z(col, j)
            if self.z_leads:
                self.send_a(j)
            self.send_b(col, j)
            self.twin(col, 0, slab)
        elif kind == "a":
            if not self.z_leads:
                self.send_z(1, 0)
            self.send_b(1, j)
            self.twin(1, 0, slab)
        else:
            self.twin(col, 1, slab)


PARTS = (
    ("t", 0, 48, "zxy"),
    ("t", 48, 32, "zyx"),
    ("t", 80, 48, "zyx"),
    ("k", 0, 96, "xzy"),
    ("v", 0, 96, "yzx"),
)
EVENTS = {
    "relayA": ("0o00", "1o00", "2o00", "0z02", "0z01", "1z01", "0a00", "2z02", "1z02", "0z03", "1a00", "1z03", "0b01", "3o00", "1b00", "2z01", "1a02", "0a01", "0a02", "0a03", "2z03", "1a01", "1a03", "0b10", "0b03", "4o00", "3a00", "1b02", "2a02", "2a01", "1b12", "0b11", "2a00", "0b02", "3z01", "3z02", "0b00", "4z01", "1b01", "0b13", "2b01", "1b13", "1b11", "4z02", "0b12", "1b03", "2b00", "1b10", ),
    "a0.0": ("3z03", "3b00", ),
    "a0.1": ("2b02", "2a03", "4a00", ),
    "a0.2": ("2b12", ),
    "a1.0": ("3b10", ),
    "a1.1": (),
    "a1.2": ("2b10", "4b00", "3z12", "2b11", ),
    "a2.0": ("3b01", "3z11", ),
    "a2.1": (),
    "a2.2": (),
    "a3.0": ("4b02", "2b03", "4z03", ),
    "a3.1": (),
    "a3.2": ("2b13", ),
    "relayB": (),
    "b0.0": ("4b01", ),
    "b0.1": ("4z11", "3b12", "3b02", ),
    "b1.0": ("3z13", ),
    "b1.1": (),
    "b2.0": (),
    "b2.1": (),
    "b3.0": ("3b11", "3b03", ),
    "b3.1": ("4b11", ),
    "h0": ("4b10", "3b13", ),
    "h1": ("4b03", "4z13", ),
    "h2": (),
    "h3": ("4z12", ),
    "c0": (),
    "c1": (),
    "c2": ("4b12", "4b13", ),
    "c3": (),
    "fin": (),
    "end": (),
}


def streams(place, messages, twin_sems, pk, kw, vt, tw, kg, vg):
    def piece_of(name, start, rows):
        if name == "t":
            return lambda y, x, c, m: tw.at[y, x, c, m, pl.ds(start, rows)]
        array = kg if name == "k" else vg
        return lambda y, x, c, m: array.at[m, y, x, c, pl.ds(start, rows)]

    made = []
    for name, start, rows, order in PARTS:
        own = {"t": pk, "k": kw, "v": vt}[name].at[pl.ds(start, rows)]
        if name == "t":
            twin = lambda slab, i=start // 80: twin_sems.at[i]
        else:
            twin = lambda slab, i=2 if name == "k" else 6: twin_sems.at[i + slab]
        made.append(Stream(place, messages, order, piece_of(name, start, rows), own, twin))
    return made


def play(made, marker):
    for event in EVENTS[marker]:
        made[int(event[0])].event(event[1], int(event[2]), int(event[3]))


def greet_all(p):
    barrier = pltpu.get_barrier_semaphore()
    for device in (p.sib, p.xn, p.yn):
        pl.semaphore_signal(barrier, inc=1, device_id=device, device_id_type=MESH)
    only(p.mp < 3, lambda: pl.semaphore_signal(barrier, inc=1, device_id=p.up, device_id_type=MESH))
    only(p.mp > 0, lambda: pl.semaphore_signal(barrier, inc=1, device_id=p.down, device_id_type=MESH))
    pl.semaphore_wait(barrier, 3 + (p.mp < 3).astype(jnp.int32) + (p.mp > 0).astype(jnp.int32))


TILE = 256
SPAN = 128
WIDE = 512


def dot(a, b):
    return jnp.dot(a, b, preferred_element_type=jnp.float32)


def dot_nt(a, b):
    return lax.dot_general(a, b, (((1,), (1,)), ((), ())), preferred_element_type=jnp.float32)


def dot_tn(a, b):
    return lax.dot_general(a, b, (((0,), (0,)), ((), ())), preferred_element_type=jnp.float32)


def low(values):
    return values.astype(jnp.bfloat16)


def wide(values):
    return values.astype(jnp.float32)


def row_sums(values):
    rows, width = values.shape
    return jnp.sum(values.reshape(rows // 8, 8, width), axis=0)


def standardise(values):
    centered = values - jnp.mean(values, axis=-1, keepdims=True)
    variance = jnp.mean(centered * centered, axis=-1, keepdims=True)
    scale = lax.rsqrt(variance + epsilon)
    return centered * scale, scale


def norm_back(grad, normal, scale):
    mean_grad = jnp.mean(grad, axis=-1, keepdims=True)
    mean_both = jnp.mean(grad * normal, axis=-1, keepdims=True)
    return scale * (grad - mean_grad - normal * mean_both)


def later(values, first_row):
    row = lax.broadcasted_iota(jnp.int32, values.shape, 0)
    return jnp.where(row == 0, first_row, pltpu.roll(values, 1, 0))


def sooner(values, last_row):
    rows = values.shape[0]
    row = lax.broadcasted_iota(jnp.int32, values.shape, 0)
    return jnp.where(row == rows - 1, last_row, pltpu.roll(values, rows - 1, 0))


def halves(target, values):
    for span in range(values.shape[0] // SPAN):
        part = values[span * SPAN : (span + 1) * SPAN]
        high = low(part)
        target[span, 0:SPAN, :] = high
        target[span, SPAN : 2 * SPAN, :] = low(part - wide(high))


GAIN1, BIAS1, GAIN2, BIAS2, MIX, DECAY, FIRST, BLEND = 0, 1, 2, 3, 4, 7, 8, 9


def vec(ref, index):
    return ref[index : index + 1, :]


def rows_at(start, count):
    return pl.ds(pl.multiple_of(start, 128), count)


def pack_block(p, proj, final, vectors, pk):
    spread = jnp.concatenate([wide(vectors[...]), jnp.zeros((16, 256), jnp.float32)], axis=1)
    spread = pltpu.roll(spread, 24 * ((4 * p.dp + p.mp) % 16), 1)
    spread = jnp.concatenate([spread[:8], spread[8:]], axis=1)
    rows = [wide(proj[0]), wide(proj[1]), wide(proj[2]), spread, wide(proj[3]), wide(final[...])]
    pk[...] = low(jnp.concatenate(rows, axis=0))


def row_of(docs, row):
    return wide(jnp.where(row == 0, docs[0:1, :], docs[1:2, :]))


def describe(docs, row, cols):
    own = row_of(docs, row)
    lane = lax.broadcasted_iota(jnp.int32, own.shape, 1)
    keep = jnp.where((lane > 0) & (own == pltpu.roll(own, 1, 1)), 1.0, 0.0)
    spans = own.shape[1] // SPAN
    none = jnp.zeros((1, SPAN), jnp.float32)
    for i in range(spans):
        part = own[:, i * SPAN : (i + 1) * SPAN]
        before = after = none
        if i > 0:
            before = jnp.where(part == own[:, i * SPAN - 1 : i * SPAN], 1.0, 0.0)
        if i < spans - 1:
            after = jnp.where(part == own[:, (i + 1) * SPAN : (i + 1) * SPAN + 1], 1.0, 0.0)
        rows = [part, keep[:, i * SPAN : (i + 1) * SPAN], before, after, jnp.zeros((SPAN - 4, SPAN), jnp.float32)]
        cols[i * SPAN : (i + 1) * SPAN, :] = jnp.concatenate(rows, axis=0).T


def forward_kernel(
    proj, final, vectors, kw, vt, docs, x_any, gy_any,
    kg, vg, acts, kvs, middle_o, sq_o, act_o, grads_o, out_o, wts_o, vecs_o, cols_o,
    w5, kv, sa, xb, st, f5, mid, sig, tables, vecs, prev, cols, split, pk, sems, twin_sems, send_sem, recv_sems,
):
    place_of = Place()
    p = place_of
    row = p.mp % 2
    load_x = pltpu.make_async_copy(x_any.at[row], xb, sems.at[0])
    load_x.start()
    pack_block(p, proj, final, vectors, pk)
    keep = [
        pltpu.make_async_copy(pk, sa.at[p.y, p.x, p.core, p.mp], sems.at[26]),
        pltpu.make_async_copy(kw, kg.at[p.mp, p.y, p.x, p.core], sems.at[27]),
        pltpu.make_async_copy(vt, vg.at[p.mp, p.y, p.x, p.core], sems.at[28]),
    ]
    for copy in keep:
        copy.start()
    greet_all(place_of)
    messages = Messages(send_sem, recv_sems)
    made = streams(place_of, messages, twin_sems, pk, kw, vt, sa, kg, vg)

    def twins(i, half):
        pltpu.make_async_copy(half, half, twin_sems.at[i]).wait()

    def time_twins(i):
        twins(i, sa.at[:, :, 1 - p.core, :, (pl.ds(0, 80), pl.ds(80, 48))[i]])

    prev[...] = jnp.zeros_like(prev)
    describe(docs, row, cols)
    own_docs = row_of(docs, row)
    play(made, "relayA")
    for copy in keep:
        copy.wait()
    time_twins(0)

    def relay(half, first_row, count, slots):
        def body(i, total):
            core, m = i // 2, 2 * (i % 2)
            pair = 8 * half + i
            spot = half, i // 4, core % 2
            rows = pl.ds(first_row, count)
            one, two = wide(sa[spot + (m, rows)]), wide(sa[spot + (m + 1, rows)])
            for n, j in enumerate(slots):
                piece = jnp.concatenate([one[24 * n : 24 * n + 24], two[24 * n : 24 * n + 24]], axis=0)
                w5[j, pl.ds(pl.multiple_of(48 * pair, 16), 48), :] = low(piece)
            return total + one[count - 8 :] + two[count - 8 :]

        return lax.fori_loop(0, 8, body, jnp.zeros((8, 768), jnp.float32))

    left, right = relay(0, 0, 80, (0, 1, 2)), relay(1, 0, 80, (0, 1, 2))
    vecs[0:8, :] = jnp.concatenate([left[:, :384], right[:, :384]], axis=1)
    vecs[8:16, :] = jnp.concatenate([left[:, 384:], right[:, 384:]], axis=1)
    save_v = pltpu.make_async_copy(vecs, vecs_o, sems.at[11])
    save_v.start()

    rate = jnp.exp(vec(vecs, DECAY))
    fade = jnp.exp(-rate)
    place = wide(lax.broadcasted_iota(jnp.int32, (TILE, 1), 0) % SPAN)
    tables[0] = jnp.exp((place - 64.0) * rate)
    tables[1] = jnp.exp((65.0 - place) * rate)
    tables[2] = jnp.exp(-place * rate)
    load_x.wait()
    tiles = [(t, t * TILE, pl.ds(t * TILE, TILE)) for t in range(1024 // TILE)]
    for t, base, r in tiles:
        play(made, f"a{t}.0")

        def first(q, last):
            x = wide(xb[q, :])
            mean = jnp.mean(x, axis=-1, keepdims=True)
            centered = x - mean
            scale = lax.rsqrt(jnp.mean(centered * centered, axis=-1, keepdims=True) + epsilon)
            cols[q, 4:5] = mean
            cols[q, 5:6] = scale
            normed = centered * scale * vec(vecs, GAIN1) + vec(vecs, BIAS1)
            earlier = later(normed, last) * cols[q, 1:2]
            delta = normed - earlier
            for j in range(3):
                st[j, q, :] = low(earlier + delta * vec(vecs, MIX + j))
            st[6, q, :] = low(delta)
            return normed[TILE - 1 :]

        prev[0:1, :] = first(r, prev[0:1, :])
        for j in range(3):
            f5[j, r, :] = dot(st[j, r, :], w5[j])
        play(made, f"a{t}.1")

        key_exp = jnp.exp(f5[0, r, :])
        f5[2, r, :] = jax.nn.sigmoid(f5[2, r, :])
        grown = key_exp * tables[0]
        halves(split.at[0], grown * f5[1, r, :])
        halves(split.at[1], grown)
        time = lax.broadcasted_iota(jnp.int32, (SPAN, SPAN), 0)
        source = lax.broadcasted_iota(jnp.int32, (SPAN, SPAN), 1)
        for i in range(TILE // SPAN):
            block = t * (TILE // SPAN) + i
            same = cols[pl.ds(block * SPAN, SPAN), 0:1] == own_docs[:, block * SPAN : (block + 1) * SPAN]
            mask = jnp.where(same & (source < time), 1.0, 0.0).astype(jnp.bfloat16)
            mask = jnp.concatenate([mask, mask], axis=1)
            for k in range(2):
                f5[3 + k, pl.ds(block * SPAN, SPAN), :] = dot(mask, split[k, i])
        play(made, f"a{t}.2")
        for i in range(TILE // SPAN):
            begin = base + i * SPAN
            top_in, bottom_in = prev[2:3, :], prev[3:4, :]

            q = pl.ds(begin, SPAN)
            values = f5[1, q, :]
            link = cols[q, 2:3] * tables[2, 0:SPAN, :]
            top = f5[3, q, :] * tables[1, 0:SPAN, :] + link * top_in
            bottom = f5[4, q, :] * tables[1, 0:SPAN, :] + link * bottom_in
            f5[3, q, :] = top
            f5[4, q, :] = bottom
            bonus = jnp.exp(f5[0, q, :] + vec(vecs, FIRST))
            st[3, q, :] = low(f5[2, q, :] * ((top + bonus * values) / (bottom + bonus)))
            end = begin + SPAN - 1
            key_exp = jnp.exp(f5[0, end : end + 1, :])
            prev[2:3, :] = fade * f5[3, end : end + 1, :] + key_exp * f5[1, end : end + 1, :]
            prev[3:4, :] = fade * f5[4, end : end + 1, :] + key_exp
    saves = [pltpu.make_async_copy(f5, kvs, sems.at[16])]
    saves[0].start()
    play(made, "relayB")
    time_twins(1)
    relay(0, 80, 48, (3, 4))
    relay(1, 80, 48, (3, 4))
    save_w = pltpu.make_async_copy(w5, wts_o, sems.at[10])
    save_w.start()
    for t, base, r in tiles:
        play(made, f"b{t}.0")
        mid[r, :] = dot(st[3, r, :], w5[4])

        def fourth(q, last):
            middle = wide(xb[q, :]) + mid[q, :]
            mid[q, :] = middle
            mean = jnp.mean(middle, axis=-1, keepdims=True)
            centered = middle - mean
            scale = lax.rsqrt(jnp.mean(centered * centered, axis=-1, keepdims=True) + epsilon)
            cols[q, 6:7] = mean
            cols[q, 7:8] = scale
            normed = centered * scale * vec(vecs, GAIN2) + vec(vecs, BIAS2)
            earlier = later(normed, last) * cols[q, 1:2]
            delta = normed - earlier
            for j in range(2):
                st[4 + j, q, :] = low(earlier + delta * vec(vecs, BLEND + j))
            st[7, q, :] = low(delta)
            return normed[TILE - 1 :]

        prev[1:2, :] = fourth(r, prev[1:2, :])
        play(made, f"b{t}.1")
        sig[r, :] = dot(st[5, r, :], w5[3])
        saves += [
            pltpu.make_async_copy(st.at[:, r], acts.at[:, r], sems.at[12 + t]),
            pltpu.make_async_copy(mid.at[r], middle_o.at[r], sems.at[20 + t]),
        ]
        for copy in saves[-2:]:
            copy.start()
    saves.append(pltpu.make_async_copy(cols, cols_o, sems.at[36]))
    saves[-1].start()
    load_gy = pltpu.make_async_copy(gy_any.at[row], xb, sems.at[24])
    load_gy.start()
    messages.finish()

    def load_kv(m, which, array):
        target = kv.at[m]
        return pltpu.make_async_copy(array.at[m], target, sems.at[4 * which + 1 + m])

    pending = {}
    for m in range(4):
        play(made, f"h{m}")
        if m == 0:
            for slab in range(4):
                twins(2 + slab, kg.at[slab, :, :, 1 - p.core])
            for i in range(4):
                load_kv(i, 0, kg).start()
        load_kv(m, 0, kg).wait()
        if m == 0:
            for copy in saves:
                copy.wait()

        def hidden(t, carry):
            r = rows_at(t * WIDE, WIDE)
            active = jnp.maximum(dot(st[4, r, :], kv[m].reshape(768, 768)), 0.0)
            squared = low(active * active)
            spot = m // 2, m % 2, t
            sa[spot] = squared.reshape(4, 128, 768)
            st[m, r, :] = low(active)
            return carry

        lax.fori_loop(0, 1024 // WIDE, hidden, 0)
        pending[m] = pltpu.make_async_copy(st.at[m], act_o.at[m], sems.at[29 + m])
        pending[m].start()
    save_sq = pltpu.make_async_copy(sa, sq_o, sems.at[33])
    save_sq.start()
    pair = p.mp // 2
    for turn in range(2):
        play(made, f"c{2 * turn}")
        at = pair if turn == 0 else 1 - pair
        loads = []
        for i in range(2):
            slab = 2 * at + i
            twins(6 + slab, vg.at[slab, :, :, 1 - p.core])
            loads.append(pltpu.make_async_copy(vg.at[slab], kv.at[2 * turn + i], sems.at[5 + 2 * turn + i]))
            loads[-1].start()
        for i in range(2):
            loads[i].wait()
            if i == 1:
                play(made, f"c{2 * turn + 1}")

            def content(t, carry):
                r = rows_at(t * WIDE, WIDE)
                squared = sa[at, i, t].reshape(WIDE, 768)
                part = dot_nt(squared, kv[2 * turn + i].reshape(768, 768))
                f5[turn, r, :] = part if i == 0 else f5[turn, r, :] + part
                return carry

            lax.fori_loop(0, 1024 // WIDE, content, 0)

    play(made, "fin")
    play(made, "end")
    load_gy.wait()

    def finish(t, state):
        q = rows_at(t * TILE, TILE)
        gate = jax.nn.sigmoid(sig[q, :])
        carried = f5[0, q, :] + f5[1, q, :]
        st[5, q, :] = low(mid[q, :] + gate * carried)
        passed = wide(xb[q, :]) * gate
        st[6, q, :] = low(passed)
        st[7, q, :] = low(passed * carried * (1.0 - gate))
        return state

    lax.fori_loop(0, 1024 // TILE, finish, 0)
    last = [
        pltpu.make_async_copy(st.at[5], out_o, sems.at[34]),
        pltpu.make_async_copy(st.at[pl.ds(6, 2)], grads_o, sems.at[35]),
    ]
    for copy in last:
        copy.start()
    save_w.wait()
    save_v.wait()
    save_sq.wait()
    for m in range(4):
        pending.pop(m).wait()
    messages.finish()
    for copy in last:
        copy.wait()


ANY = pl.BlockSpec(memory_space=pl.ANY)
ON_CORE = pl.BlockSpec(memory_space=pltpu.VMEM)
LIMIT = 63 * MIB


def forward(proj, final, vectors, kw, vt, docs, x, gy):
    bf, f32 = jnp.bfloat16, jnp.float32
    shape = jax.ShapeDtypeStruct
    return pl.pallas_call(
        forward_kernel,
        out_shape=(
            shape((4, 2, 2, 2, 96, 768), bf), shape((4, 2, 2, 2, 96, 768), bf),
            shape((8, 1024, 768), bf), shape((5, 1024, 768), f32), shape((1024, 768), f32),
            shape((2, 2, 2, 4, 128, 768), bf), shape((4, 1024, 768), bf), shape((2, 1024, 768), bf),
            shape((1024, 768), bf), shape((5, 768, 768), bf), shape((16, 768), f32), shape((1024, 128), f32),
        ),
        in_specs=[ON_CORE] * 6 + [ANY] * 2,
        out_specs=[ANY] * 12,
        scratch_shapes=[
            pltpu.VMEM((5, 768, 768), bf), pltpu.VMEM((4, 2, 2, 2, 96, 768), bf), pltpu.VMEM((2, 2, 2, 4, 128, 768), bf),
            pltpu.VMEM((1024, 768), bf), pltpu.VMEM((8, 1024, 768), bf), pltpu.VMEM((5, 1024, 768), f32),
            pltpu.VMEM((1024, 768), f32), pltpu.VMEM((1024, 768), f32),
            pltpu.VMEM((3, TILE, 768), f32), pltpu.VMEM((16, 768), f32), pltpu.VMEM((8, 768), f32),
            pltpu.VMEM((1024, 128), f32), pltpu.VMEM((2, 2, 2 * SPAN, 768), bf), pltpu.VMEM((128, 768), bf),
            pltpu.SemaphoreType.DMA((37,)), pltpu.SemaphoreType.DMA((10,)), pltpu.SemaphoreType.DMA,
            pltpu.SemaphoreType.DMA((15 * len(PARTS),)),
        ],
        compiler_params=pltpu.CompilerParams(vmem_limit_bytes=LIMIT, collective_id=0, has_side_effects=True),
        name="forward",
    )(proj, final, vectors, kw, vt, docs, x, gy)


def channel_back_kernel(
    kg, vg, wts, acts, sq, act, grads, middle, gy_any, out_row, cols, vecs,
    gm_o, gkv_o, out_o, sums_o,
    kv, sqs, acs, gcg, cc, dh, acc, wg, mid, gy, gm, delta, stage, gate_w, sums, nxt, result, sems, send_sem, recv_sems,
):
    place = Place()
    mp = place.mp
    row, pair = mp % 2, mp // 2
    load_row = pltpu.make_async_copy(out_row, result, sems.at[22])
    load_row.start()
    greet([place.pair])
    messages = Messages(send_sem, recv_sems)
    load_row.wait()
    arrival = messages.send(result, out_o.at[row], out_o.at[1 - row], place.pair)
    keep_row = pltpu.make_async_copy(result, out_o.at[row], sems.at[21])
    keep_row.start()
    order = [2 * pair, 2 * pair + 1, 2 - 2 * pair, 3 - 2 * pair]

    def loads(j):
        m, slot = order[j], j % 2
        copies = [
            pltpu.make_async_copy(kg.at[m], kv.at[0, slot], sems.at[3 * j]),
            pltpu.make_async_copy(vg.at[m], kv.at[1, slot], sems.at[3 * j + 1]),
            pltpu.make_async_copy(act.at[m], acs.at[slot], sems.at[3 * j + 2]),
        ]
        return copies

    load_g = pltpu.make_async_copy(grads, gcg, sems.at[12])
    load_g.start()
    for j in range(2):
        for copy in loads(j):
            copy.start()
    others = [
        pltpu.make_async_copy(sq.at[pl.ds(2 * pair, 2)], sqs, sems.at[13]),
        pltpu.make_async_copy(acts.at[pl.ds(4, 2)], cc, sems.at[14]),
        pltpu.make_async_copy(wts.at[3], wg, sems.at[15]),
        pltpu.make_async_copy(middle, mid, sems.at[16]),
        pltpu.make_async_copy(acts.at[7], delta, sems.at[19]),
        pltpu.make_async_copy(gy_any.at[row], gy, sems.at[17]),
    ]
    for copy in others:
        copy.start()
    load_g.wait()
    waited = False
    stores = []
    for j in range(4):
        slot = j % 2
        for copy in loads(j):
            copy.wait()

        def hidden_back(t, carry):
            r = rows_at(t * WIDE, WIDE)
            active = wide(acs[slot, r, :])
            grad = low(dot(gcg[0, r, :], kv[1, slot]) * (2.0 * active))
            if j < 2:
                dh[j, r, :] = grad
            part = dot_nt(grad, kv[0, slot])
            acc[j // 2, r, :] = part if j % 2 == 0 else acc[j // 2, r, :] + part
            return carry

        lax.fori_loop(0, 1024 // WIDE, hidden_back, 0)
        if j < 2:
            for copy in loads(j + 2):
                copy.start()
            if not waited:
                waited = True
                for copy in others:
                    copy.wait()

            def weights(t, carry):
                c = pl.ds(pl.multiple_of(t * 384, 128), 384)
                spot = pl.ds(t * 4, 4)
                key = low(dot_tn(cc[0, :, c], dh[j]))
                stage[j, spot, 0:96, :] = key.reshape(4, 96, 768)
                value = low(dot_tn(gcg[0, :, c], sqs[j].reshape(1024, 768)))
                stage[j, spot, 96:192, :] = value.reshape(4, 96, 768)
                return carry

            lax.fori_loop(0, 2, weights, 0)

    def gate_weights(t, carry):
        c = pl.ds(pl.multiple_of(t * 384, 128), 384)
        gate_w[c, :] = dot_tn(cc[1, :, c], gcg[1])
        return carry

    lax.fori_loop(0, 2, gate_weights, 0)

    def gate_pack(dp, carry):
        for j in range(2):
            start = pl.multiple_of(96 * dp + 48 * pair + 24 * j, 8)
            piece = jnp.concatenate([gate_w[pl.ds(start, 24), :], jnp.zeros((8, 768), jnp.float32)], axis=0)
            stage[j, dp, 192:224, :] = low(piece)
        return carry

    lax.fori_loop(0, 8, gate_pack, 0)
    store = pltpu.make_async_copy(stage, gkv_o, sems.at[18])
    store.start()
    sums[...] = jnp.zeros_like(sums)
    nxt[...] = jnp.zeros_like(nxt)

    def gate_back(t, carry):
        r = rows_at(t * WIDE, WIDE)
        gm[r, :] = dot_nt(gcg[1, r, :], wg[...])
        return carry

    lax.fori_loop(0, 1024 // WIDE, gate_back, 0)
    gain = vec(vecs, GAIN2)
    key_mix, rec_mix = vec(vecs, BLEND), vec(vecs, BLEND + 1)

    def tokens(n, state):
        q = rows_at((1024 // TILE - 1 - n) * TILE, TILE)
        grad_key, grad_rec = acc[0, q, :] + acc[1, q, :], gm[q, :]
        step = wide(delta[q, :])
        sums[2] += row_sums(grad_key * step)
        sums[3] += row_sums(grad_rec * step)
        grad = grad_key * key_mix + grad_rec * rec_mix
        back = (grad_key + grad_rec - grad) * cols[q, 1:2]
        grad = grad + sooner(back, state)
        scale = cols[q, 7:8]
        normal = (mid[q, :] - cols[q, 6:7]) * scale
        sums[0] += row_sums(grad * normal)
        sums[1] += row_sums(grad)
        gm[q, :] = wide(gy[q, :]) + norm_back(grad * gain, normal, scale)
        return back[0:1]

    lax.fori_loop(0, 1024 // TILE, tokens, jnp.zeros((1, 768), jnp.float32))
    store_gm = pltpu.make_async_copy(gm, gm_o, sems.at[20])
    store_gm.start()
    for i in range(4):
        sums_o[i : i + 1, :] = jnp.sum(sums[i], axis=0, keepdims=True)
    sums_o[4:8, :] = jnp.zeros((4, 768), jnp.float32)
    store.wait()
    store_gm.wait()
    keep_row.wait()
    arrival.wait_recv()
    messages.finish()


def channel_back(kg, vg, wts, acts, sq, act, grads, middle, gy, out_row, cols, vecs):
    bf, f32 = jnp.bfloat16, jnp.float32
    shape = jax.ShapeDtypeStruct
    return pl.pallas_call(
        channel_back_kernel,
        out_shape=(
            shape((1024, 768), f32), shape((2, 8, 224, 768), bf),
            shape((2, 1024, 768), bf), shape((8, 768), f32),
        ),
        in_specs=[ANY] * 10 + [ON_CORE] * 2,
        out_specs=[ANY] * 3 + [ON_CORE],
        scratch_shapes=[
            pltpu.VMEM((2, 2, 768, 768), bf), pltpu.VMEM((2, 8, 128, 768), bf), pltpu.VMEM((2, 1024, 768), bf),
            pltpu.VMEM((2, 1024, 768), bf), pltpu.VMEM((2, 1024, 768), bf), pltpu.VMEM((2, 1024, 768), bf),
            pltpu.VMEM((2, 1024, 768), f32), pltpu.VMEM((768, 768), bf), pltpu.VMEM((1024, 768), f32),
            pltpu.VMEM((1024, 768), bf), pltpu.VMEM((1024, 768), f32), pltpu.VMEM((1024, 768), bf), pltpu.VMEM((2, 8, 224, 768), bf),
            pltpu.VMEM((768, 768), f32), pltpu.VMEM((4, 8, 768), f32), pltpu.VMEM((8, 768), f32),
            pltpu.VMEM((1024, 768), bf),
            pltpu.SemaphoreType.DMA((23,)), pltpu.SemaphoreType.DMA, pltpu.SemaphoreType.DMA((1,)),
        ],
        compiler_params=pltpu.CompilerParams(vmem_limit_bytes=LIMIT, collective_id=1, has_side_effects=True),
        name="channel_back",
    )(kg, vg, wts, acts, sq, act, grads, middle, gy, out_row, cols, vecs)


class Scatter:
    def __init__(self, place, messages, source, load_sem, received, kept, steps, final, orders):
        self.p, self.msg, self.load_sem = place, messages, load_sem
        self.source, self.received, self.kept, self.steps, self.final = source, received, kept, steps, final
        self.orders = orders
        self.parts = len(orders)
        self.waits = []

    def cols(self, part):
        width = self.kept.shape[-1] // self.parts
        return pl.ds(part * width, width)

    def start(self):
        p = self.p
        self.core_wait = self.msg.send(self.source.at[:, :, :, :, 1 - p.core], self.received, self.received, p.sib)
        self.load = pltpu.make_async_copy(self.source.at[:, :, :, :, p.core], self.kept, self.load_sem)
        self.load.start()

    def core(self):
        p = self.p
        self.load.wait()
        self.core_wait.wait_recv()
        n = self.kept.shape[0]
        for i in range(n):
            for j in range(2):
                for y in range(2):
                    for x in range(2):
                        total = wide(self.kept[i, j, y, x]) + wide(self.received[i, j, y, x])
                        self.kept[i, j, y, x] = total.astype(self.kept.dtype)
        self.send(0)

    def index(self, order, step, flip):
        p = self.p
        mine = {"x": p.x, "y": p.y, "j": p.mp % 2}
        picked = {}
        for at, axis in enumerate(order):
            if at < step:
                picked[axis] = mine[axis]
            elif at == step:
                picked[axis] = 1 - mine[axis] if flip else mine[axis]
            else:
                picked[axis] = None
        return picked

    def send(self, step):
        p = self.p
        device = {"x": p.xn, "y": p.yn, "j": p.pair}
        self.waits = []
        for part in range(self.parts):
            order = self.orders[part]
            picked = self.index(order, step, True)
            select = tuple(ALL if picked[a] is None else picked[a] for a in "jyx")
            piece = self.kept.at[(ALL,) + select + (ALL, self.cols(part))]
            target = self.steps[step].at[part]
            self.waits.append(self.msg.send(piece, target, target, device[order[step]]))

    def add(self, step):
        for part in range(self.parts):
            order = self.orders[part]
            self.waits[part].wait_recv()
            picked = self.index(order, step, False)
            free = [a for a in "jyx" if picked[a] is None]
            n = self.kept.shape[0]
            for i in range(n):
                for number in range(2 ** len(free)):
                    bits = {a: (number >> (len(free) - 1 - k)) & 1 for k, a in enumerate(free)}
                    select = tuple(bits[a] if picked[a] is None else picked[a] for a in "jyx")
                    spot = (i,) + select + (ALL, self.cols(part))
                    arrived = self.steps[step][(part, i) + tuple(bits[a] for a in free)]
                    total = wide(self.kept[spot]) + wide(arrived)
                    if step == 2:
                        self.final[i, :, self.cols(part)] = total
                    else:
                        self.kept[spot] = total.astype(self.kept.dtype)
        if step < 2:
            self.send(step + 1)


def scatter_scratch(n, rows, cols, parts, dtype):
    width = cols // parts
    return [
        pltpu.VMEM((n, 2, 2, 2, rows, cols), dtype), pltpu.VMEM((n, 2, 2, 2, rows, cols), dtype),
        pltpu.VMEM((parts, n, 2, 2, rows, width), dtype), pltpu.VMEM((parts, n, 2, rows, width), dtype),
        pltpu.VMEM((parts, n, rows, width), dtype),
    ]


def time_back_kernel(
    wts, acts, kvs, gm_any, x_any, gkv_any, cols, docs, vecs, sums_c,
    ig_o, gkv_o, gt_o, small_o,
    w4, ins, f5, gm, xb, gb, gkvr, delta, grads, split, pack, tables, sums, nxt, small_cut, *scratch,
):
    kv_scratch, s_scratch = scratch[:5], scratch[5:10]
    t_scratch = [scratch[10 + 5 * i : 15 + 5 * i] for i in range(4)]
    sems, send_sem, recv_sems = scratch[30:]
    place_of = Place()
    mp = place_of.mp
    row, pair = mp % 2, mp // 2
    load_w = [
        pltpu.make_async_copy(wts.at[4], w4.at[3], sems.at[1]),
        pltpu.make_async_copy(wts.at[pl.ds(0, 3)], w4.at[pl.ds(0, 3)], sems.at[2]),
    ]
    tile_loads = {}
    for t in reversed(range(1024 // TILE)):
        r = pl.ds(t * TILE, TILE)
        tile_loads[t] = [
            pltpu.make_async_copy(gm_any.at[r], gm.at[r], sems.at[18 + 4 * t]),
            pltpu.make_async_copy(kvs.at[:, r], f5.at[:, r], sems.at[19 + 4 * t]),
            pltpu.make_async_copy(x_any.at[row, r], xb.at[r], sems.at[20 + 4 * t]),
            pltpu.make_async_copy(acts.at[6, r], delta.at[r], sems.at[21 + 4 * t]),
        ]
    load_ins = [pltpu.make_async_copy(acts.at[i], ins.at[i % 2], sems.at[4 + i]) for i in range(4)]
    for copy in load_w[:1] + tile_loads[3] + load_w[1:] + tile_loads[2] + tile_loads[1] + tile_loads[0] + load_ins[:2]:
        copy.start()
    greet([place_of.sib, place_of.xn, place_of.yn, place_of.pair])
    messages = Messages(send_sem, recv_sems)
    channel = Scatter(place_of, messages, gkv_any, sems.at[8], kv_scratch[0], kv_scratch[1], kv_scratch[2:], gkv_o, ("xyj", "yxj"))
    vectors = Scatter(place_of, messages, small_cut, sems.at[9], s_scratch[0], s_scratch[1], s_scratch[2:], small_o, ("xyj",))
    mixing = []
    for i in range(4):
        buffers = t_scratch[i]
        final = gt_o.at[pl.ds(i, 1)]
        order = ("xyj", "yxj")[i % 2]
        mixing.append(Scatter(place_of, messages, pack.at[pl.ds(i, 1)], sems.at[10 + i], buffers[0], buffers[1], buffers[2:], final, (order,)))
    channel.start()
    rate = jnp.exp(vec(vecs, DECAY))
    fade = jnp.exp(-rate)
    place = wide(lax.broadcasted_iota(jnp.int32, (TILE, 1), 0) % SPAN)
    tables[0] = jnp.exp((64.0 - place) * rate)
    tables[1] = jnp.exp((place - 63.0) * rate)
    tables[2] = jnp.exp((place - 127.0) * rate)
    sums[...] = jnp.zeros_like(sums)
    nxt[...] = jnp.zeros_like(nxt)
    gain = vec(vecs, GAIN1)
    own_docs = row_of(docs, row)

    def tile(t):
        base = t * TILE
        r = pl.ds(base, TILE)
        for copy in tile_loads[t]:
            copy.wait()
        gb[r, :] = low(gm[r, :])
        if t == 3:
            load_w[0].wait()
        grads[0] = dot_nt(gb[r, :], w4[3])

        values, gate = f5[1, r, :], f5[2, r, :]
        bonus = jnp.exp(f5[0, r, :] + vec(vecs, FIRST))
        inverse = 1.0 / (f5[4, r, :] + bonus)
        mixed = (f5[3, r, :] + bonus * values) * inverse
        grad_mixed = grads[0] * gate
        gkvr[2, r, :] = low(grad_mixed * mixed * (1.0 - gate))
        grad_top = grad_mixed * inverse
        shrunk = grad_top * tables[0]
        halves(split.at[0], shrunk)
        halves(split.at[1], -shrunk * mixed)
        direct = bonus * grad_top
        own = direct * (values - mixed)
        grads[0] = direct
        grads[1] = own
        sums[0] += row_sums(own)
        grads[3] = grad_top
        edges = [grads[3, i * SPAN : i * SPAN + 1, :] for i in range(TILE // SPAN)]
        time = lax.broadcasted_iota(jnp.int32, (SPAN, SPAN), 0)
        source = lax.broadcasted_iota(jnp.int32, (SPAN, SPAN), 1)
        for i in reversed(range(TILE // SPAN)):
            block = t * (TILE // SPAN) + i
            same = cols[pl.ds(block * SPAN, SPAN), 0:1] == own_docs[:, block * SPAN : (block + 1) * SPAN]
            mask = jnp.where(same & (source > time), 1.0, 0.0).astype(jnp.bfloat16)
            mask = jnp.concatenate([mask, mask], axis=1)
            for k in range(2):
                grads[2 + k, pl.ds(i * SPAN, SPAN), :] = dot(mask, split[k, i])
        for i in reversed(range(TILE // SPAN)):
            begin = base + i * SPAN
            top_in, bottom_in = nxt[1:2, :], nxt[2:3, :]

            q, here = pl.ds(begin, SPAN), pl.ds(i * SPAN, SPAN)
            link = cols[q, 3:4] * tables[2, 0:SPAN, :]
            state_top = grads[2, here, :] * tables[1, 0:SPAN, :] + link * top_in
            state_bottom = grads[3, here, :] * tables[1, 0:SPAN, :] + link * bottom_in
            key_exp = jnp.exp(f5[0, q, :])
            gkvr[0, q, :] = low(grads[1, here, :] + key_exp * (state_top * f5[1, q, :] + state_bottom))
            gkvr[1, q, :] = low(grads[0, here, :] + key_exp * state_top)
            sums[1] += row_sums(state_top * f5[3, q, :] + state_bottom * f5[4, q, :])
            row_top, row_bottom = state_top[0:1], state_bottom[0:1]
            bonus = jnp.exp(f5[0, begin : begin + 1, :] + vec(vecs, FIRST))
            bottom = f5[4, begin : begin + 1, :] + bonus
            mixed = (f5[3, begin : begin + 1, :] + bonus * f5[1, begin : begin + 1, :]) / bottom
            nxt[1:2, :] = fade * row_top + edges[i]
            nxt[2:3, :] = fade * row_bottom - edges[i] * mixed
        if t == 3:
            load_w[1].wait()
        for j in range(3):
            grads[j] = dot_nt(gkvr[j, r, :], w4[j])

        def third(q, state):
            step = wide(delta[q, :])
            grad, whole = 0.0, 0.0
            for j in range(3):
                into = grads[j]
                sums[4 + j] += row_sums(into * step)
                grad += into * vec(vecs, MIX + j)
                whole += into
            back = (whole - grad) * cols[q, 1:2]
            grad = grad + sooner(back, state)
            scale = cols[q, 5:6]
            normal = (wide(xb[q, :]) - cols[q, 4:5]) * scale
            sums[2] += row_sums(grad * normal)
            sums[3] += row_sums(grad)
            xb[q, :] = low(gm[q, :] + norm_back(grad * gain, normal, scale))
            return back[0:1]

        nxt[0:1, :] = third(r, nxt[0:1, :])

    arrivals = []
    keeps = []
    for t in reversed(range(1024 // TILE)):
        tile(t)
        r = pl.ds(t * TILE, TILE)
        done = xb.at[r]
        arrivals.append(messages.send(done, ig_o.at[row, r], ig_o.at[1 - row, r], place_of.pair))
        keeps.append(pltpu.make_async_copy(done, ig_o.at[row, r], sems.at[14 + t]))
        keeps[-1].start()
        if t == 3:
            channel.core()

    def product(slot, right):
        load_ins[slot].wait()
        left = ins.at[slot % 2]
        def body(t, carry):
            c = pl.ds(pl.multiple_of(t * 384, 128), 384)
            f5[0, c, :] = dot_tn(left[:, c], right[...])
            return carry

        lax.fori_loop(0, 2, body, 0)

        def packed(dp, carry):
            for j in range(2):
                start = pl.multiple_of(96 * dp + 48 * pair + 24 * j, 8)
                piece = jnp.concatenate([f5[0, pl.ds(start, 24), :], jnp.zeros((8, 768), jnp.float32)], axis=0)
                pack[slot, j, dp // 4, (dp // 2) % 2, dp % 2] = low(piece)
            return carry

        lax.fori_loop(0, 8, packed, 0)
        if slot < 2:
            load_ins[slot + 2].start()
        mixing[slot].start()

    totals = [jnp.sum(sums[i], axis=0, keepdims=True) for i in range(7)]
    totals[1] = totals[1] * (-rate * fade)
    small = jnp.concatenate([sums_c[0:4, :]] + totals + [jnp.zeros((5, 768), jnp.float32)], axis=0)
    turned = pltpu.roll(small, (768 - 48 * pair) % 768, 1)
    for dp in range(8):
        for j in range(2):
            start = 96 * dp + 24 * j
            piece = turned if start == 0 else pltpu.roll(turned, 768 - start, 1)
            small_cut[0, j, dp // 4, (dp // 2) % 2, dp % 2] = piece[:, :128]
    vectors.start()
    product(0, gkvr.at[0])
    vectors.core()
    channel.add(0)
    product(1, gkvr.at[1])
    mixing[0].core()
    product(2, gkvr.at[2])
    mixing[1].core()
    mixing[0].add(0)
    vectors.add(0)
    product(3, gb)
    mixing[2].core()
    mixing[1].add(0)
    channel.add(1)
    mixing[0].add(1)
    mixing[3].core()
    mixing[2].add(0)
    mixing[1].add(1)
    vectors.add(1)
    mixing[3].add(0)
    mixing[2].add(1)
    mixing[3].add(1)
    channel.add(2)
    vectors.add(2)
    for group in mixing:
        group.add(2)
    for copy in keeps:
        copy.wait()
    for wait in arrivals:
        wait.wait_recv()
    messages.finish()


def time_back(wts, acts, kvs, gm, x, gkv, cols, docs, vecs, sums_c):
    bf, f32 = jnp.bfloat16, jnp.float32
    shape = jax.ShapeDtypeStruct
    return pl.pallas_call(
        time_back_kernel,
        out_shape=(
            shape((2, 1024, 768), bf), shape((1, 224, 768), f32), shape((4, 32, 768), f32), shape((1, 16, 128), f32),
        ),
        in_specs=[ANY] * 6 + [ON_CORE] * 4,
        out_specs=[ANY] + [ON_CORE] * 3,
        scratch_shapes=[
            pltpu.VMEM((4, 768, 768), bf), pltpu.VMEM((2, 1024, 768), bf), pltpu.VMEM((5, 1024, 768), f32),
            pltpu.VMEM((1024, 768), f32), pltpu.VMEM((1024, 768), bf), pltpu.VMEM((1024, 768), bf),
            pltpu.VMEM((3, 1024, 768), bf), pltpu.VMEM((1024, 768), bf), pltpu.VMEM((4, TILE, 768), f32),
            pltpu.VMEM((2, 2, 2 * SPAN, 768), bf),
            pltpu.VMEM((4, 2, 2, 2, 2, 32, 768), bf), pltpu.VMEM((3, TILE, 768), f32), pltpu.VMEM((7, 8, 768), f32),
            pltpu.VMEM((8, 768), f32), pltpu.VMEM((1, 2, 2, 2, 2, 16, 128), f32),
        ]
        + scatter_scratch(1, 224, 768, 2, bf)
        + scatter_scratch(1, 16, 128, 1, f32)
        + scatter_scratch(1, 32, 768, 1, bf) * 4
        + [pltpu.SemaphoreType.DMA((34,)), pltpu.SemaphoreType.DMA, pltpu.SemaphoreType.DMA((32,))],
        compiler_params=pltpu.CompilerParams(vmem_limit_bytes=LIMIT, collective_id=2, has_side_effects=True),
        name="time_back",
    )(wts, acts, kvs, gm, x, gkv, cols, docs, vecs, sums_c)


def results_kernel(
    out_any, ig_any, gkv, gt, small,
    out_o, ig_o, gain1, bias1, gain2, bias2, mix, blend_o, decay, first, grad_mix, grad_out, grad_key, grad_value,
    rows, halves_in, halves_out, sems,
):
    cut = 512
    parts = [(i, pl.ds(j * cut, cut)) for i in range(2) for j in range(1024 // cut)]
    loads = [pltpu.make_async_copy(ig_any.at[i, r], halves_in.at[i, r], sems.at[n]) for n, (i, r) in enumerate(parts)]
    load_out = pltpu.make_async_copy(out_any, rows, sems.at[8])
    for copy in loads + [load_out]:
        copy.start()
    for ref, slot in ((gain2, 0), (bias2, 1), (first, 4), (decay, 5), (gain1, 6), (bias1, 7)):
        ref[...] = small[0, slot, 0:24]
    blend_o[...] = small[0, 2:4, 0:24]
    mix[...] = small[0, 8:11, 0:24]
    for j in range(3):
        grad_mix[j] = gt[j, 0:24, :]
    grad_mix[3] = gkv[0, 192:216, :]
    grad_out[...] = gt[3, 0:24, :]
    grad_key[...] = gkv[0, 0:96, :]
    grad_value[...] = gkv[0, 96:224, :].T[:, 0:96]
    stores = []
    for n, (i, r) in enumerate(parts):
        loads[n].wait()
        halves_out[i, r, :] = wide(halves_in[i, r, :])
        stores.append(pltpu.make_async_copy(halves_out.at[i, r], ig_o.at[i, r], sems.at[4 + n]))
        stores[-1].start()
    load_out.wait()
    stores.append(pltpu.make_async_copy(rows, out_o, sems.at[9]))
    stores[-1].start()
    for copy in stores:
        copy.wait()


def results(out, ig, gkv, gt, small):
    bf, f32 = jnp.bfloat16, jnp.float32
    shape = jax.ShapeDtypeStruct
    vector = shape((24,), f32)
    return pl.pallas_call(
        results_kernel,
        out_shape=(
            shape((2, 1024, 768), bf), shape((2, 1024, 768), f32), vector, vector, vector, vector,
            shape((3, 24), f32), shape((2, 24), f32), vector, vector,
            shape((4, 24, 768), f32), shape((24, 768), f32), shape((96, 768), f32), shape((768, 96), f32),
        ),
        in_specs=[ANY] * 2 + [ON_CORE] * 3,
        out_specs=[ANY] * 2 + [ON_CORE] * 12,
        scratch_shapes=[
            pltpu.VMEM((2, 1024, 768), bf), pltpu.VMEM((2, 1024, 768), bf), pltpu.VMEM((2, 1024, 768), f32),
            pltpu.SemaphoreType.DMA((10,)),
        ],
        compiler_params=pltpu.CompilerParams(vmem_limit_bytes=LIMIT),
        name="results",
    )(out, ig, gkv, gt, small)


def on_device(
    residual_input, article_numbers, upstream_gradient,
    prenorm_scaling, prenorm_offset, postnorm_scaling, postnorm_offset,
    attention_blend, feedforward_blend, forgetting_logrates, present_reward,
    projection_matrices, final_matrix, address_matrix, content_matrix,
):
    vectors = jnp.concatenate(
        [
            prenorm_scaling[None], prenorm_offset[None], postnorm_scaling[None], postnorm_offset[None],
            attention_blend, forgetting_logrates[None], present_reward[None], feedforward_blend,
        ],
        axis=0,
    )
    vectors = jnp.pad(vectors, ((0, 5), (0, 104)))
    kg, vg, acts, kvs, middle, sq, act, grads, out_row, wts, vecs, cols = forward(
        projection_matrices, final_matrix, vectors, address_matrix, content_matrix.T, article_numbers,
        residual_input, upstream_gradient,
    )
    kg, vg, sq = kg.reshape(4, 768, 768), vg.reshape(4, 768, 768), sq.reshape(4, 8, 128, 768)
    gm, gkv, output, sums_c = channel_back(
        kg, vg, wts, acts, sq, act, grads, middle, upstream_gradient, out_row, cols, vecs
    )
    input_grad, gkv, gt, small = time_back(
        wts, acts, kvs, gm, residual_input, gkv.reshape(1, 2, 2, 2, 2, 224, 768), cols, article_numbers, vecs, sums_c
    )
    return results(output, input_grad, gkv, gt, small)


def fits(mesh):
    return dict(mesh.shape) == {"dp": 8, "mp": 4}


def solution(mesh):
    return jax.shard_map(
        on_device if fits(mesh) else general_device,
        mesh=mesh,
        in_specs=(
            P("dp", None, None),
            P("dp", None),
            P("dp", None, None),
            P(("dp", "mp")),
            P(("dp", "mp")),
            P(("dp", "mp")),
            P(("dp", "mp")),
            P(None, ("dp", "mp")),
            P(None, ("dp", "mp")),
            P(("dp", "mp")),
            P(("dp", "mp")),
            P(None, ("dp", "mp"), None),
            P(("dp", "mp"), None),
            P("dp", "mp"),
            P("mp", "dp"),
        ),
        out_specs=(
            P("dp", None, None),
            P("dp", None, None),
            P(("dp", "mp")),
            P(("dp", "mp")),
            P(("dp", "mp")),
            P(("dp", "mp")),
            P(None, ("dp", "mp")),
            P(None, ("dp", "mp")),
            P(("dp", "mp")),
            P(("dp", "mp")),
            P(None, ("dp", "mp"), None),
            P(("dp", "mp"), None),
            P("dp", "mp"),
            P("mp", "dp"),
        ),
        check_vma=False,
    )
```

```python
import functools

import jax
import jax.numpy as jnp
from jax import lax
from jax.experimental import pallas as pl
from jax.experimental.pallas import tpu as pltpu
from jax.sharding import PartitionSpec as P

BLOCK = 64
MICRO = 2


epsilon = 1e-05


def layer_norm(values_in, gain_vec, bias_vec):
    average = jnp.mean(values_in, axis=-1, keepdims=True)
    centered = values_in - average
    variance = jnp.mean(centered * centered, axis=-1, keepdims=True)
    return centered * lax.rsqrt(variance + epsilon) * gain_vec + bias_vec


def shifted(values_in, retain_marker):
    earlier = jnp.concatenate([jnp.zeros_like(values_in[:, :1]), values_in[:, :-1]], axis=1)
    return earlier * retain_marker[:, :, None]


def blend(normed, earlier, factor):
    return normed * factor + earlier * (1.0 - factor)


def project(operand, weights):
    return lax.dot_general(
        operand, weights, (((2,), (0,)), ((), ())), preferred_element_type=jnp.float32
    )


def back_project(gradient, weights):
    return lax.dot_general(
        gradient, weights, (((2,), (1,)), ((), ())), preferred_element_type=jnp.float32
    )


def weight_grad(operand, gradient):
    return lax.dot_general(
        operand, gradient, (((0, 1), (0, 1)), ((), ())), preferred_element_type=jnp.float32
    )


def take_share(array, axis_at, groups, shares, place):
    shape = array.shape
    piece_len = shape[axis_at] // (groups * shares)
    split_shape = shape[:axis_at] + (groups, shares, piece_len) + shape[axis_at + 1 :]
    chosen = lax.dynamic_index_in_dim(
        array.reshape(split_shape), place, axis_at + 1, keepdims=False
    )
    return chosen.reshape(shape[:axis_at] + (groups * piece_len,) + shape[axis_at + 1 :])


def first_piece(stream_f, gain_vec, bias_vec, factors, retain_marker):
    normed = layer_norm(stream_f, gain_vec, bias_vec)
    earlier = shifted(normed, retain_marker)
    return (
        blend(normed, earlier, factors[0]),
        blend(normed, earlier, factors[1]),
        blend(normed, earlier, factors[2]),
    )


def channel_piece(middle, gain_vec, bias_vec, factors, retain_marker):
    normed = layer_norm(middle, gain_vec, bias_vec)
    earlier = shifted(normed, retain_marker)
    return (blend(normed, earlier, factors[0]), blend(normed, earlier, factors[1]))


def time_piece(
    address_series,
    content_series,
    acceptance_gate,
    forgetting_logrates,
    present_reward,
    retain_marker,
    article_labels,
    span_length,
):
    batch_rows, length, feature_count = address_series.shape
    block_count = length // span_length
    decay_rate = jnp.exp(forgetting_logrates)
    position = jnp.arange(span_length, dtype=jnp.float32)[:, None]
    rising = jnp.exp(position * decay_rate)
    sinking = jnp.exp(-position * decay_rate)
    falling = jnp.exp(-(position + 1.0) * decay_rate)
    rising = jnp.concatenate([rising, rising], axis=-1)
    sinking = jnp.concatenate([sinking, sinking], axis=-1)
    falling = jnp.concatenate([falling, falling], axis=-1)
    whole_fade = jnp.exp(-span_length * decay_rate)
    whole_fade = jnp.concatenate([whole_fade, whole_fade], axis=-1)
    key_exp = jnp.exp(address_series)
    weighted = jnp.concatenate([key_exp * content_series, key_exp], axis=-1)
    weighted = weighted.reshape(batch_rows, block_count, span_length, 2 * feature_count)
    block_docs = article_labels.reshape(batch_rows, block_count, span_length)
    causal = jnp.arange(span_length)[:, None] >= jnp.arange(span_length)[None, :]
    same_doc = block_docs[:, :, :, None] == block_docs[:, :, None, :]
    doc_mask = (causal[None, None] & same_doc).astype(jnp.float32)
    partial_value = (
        jnp.einsum("rnji,rnid->rnjd", doc_mask, weighted * rising, precision=lax.Precision.HIGHEST)
        * sinking
    )
    last_docs = block_docs[:, :, -1]
    prior_docs = jnp.concatenate(
        [jnp.full((batch_rows, 1), -1, jnp.int32), last_docs[:, :-1]], axis=1
    )
    linked = (block_docs == prior_docs[:, :, None]).astype(jnp.float32)
    chained = linked[:, :, -1]

    def carry_step(state, pieces):
        tail_state, joined = pieces
        return (tail_state + whole_fade * joined[:, None] * state, state)

    zero_state = jnp.zeros((batch_rows, 2 * feature_count), jnp.float32)
    _, starts = lax.scan(
        carry_step,
        zero_state,
        (jnp.swapaxes(partial_value[:, :, -1], 0, 1), jnp.swapaxes(chained, 0, 1)),
    )
    starts = jnp.swapaxes(starts, 0, 1)
    states = partial_value + falling * linked[..., None] * starts[:, :, None, :]
    states = states.reshape(batch_rows, length, 2 * feature_count)
    entering_memory = shifted(states, retain_marker)
    reward_power = jnp.exp(present_reward + address_series)
    accumulated_dividend = entering_memory[..., :feature_count] + reward_power * content_series
    accumulated_divisor = entering_memory[..., feature_count:] + reward_power
    return jax.nn.sigmoid(acceptance_gate) * (accumulated_dividend / accumulated_divisor)


def general_device(
    residual_input,
    article_numbers,
    upstream_gradient,
    prenorm_scaling,
    prenorm_offset,
    postnorm_scaling,
    postnorm_offset,
    attention_blend,
    feedforward_blend,
    forgetting_logrates,
    present_reward,
    projection_matrices,
    final_matrix,
    address_matrix,
    content_matrix,
):
    batch_rows = residual_input.shape[0] // MICRO
    same_doc = article_numbers[:, 1:] == article_numbers[:, :-1]
    keep_all = jnp.concatenate([jnp.zeros_like(same_doc[:, :1]), same_doc], axis=1).astype(
        jnp.float32
    )
    groups = lax.axis_size("dp")
    shares = lax.axis_size("mp")
    mp_place = lax.axis_index("mp")
    totals = None
    outputs = []
    input_grads = []
    for micro_index in range(MICRO):
        shared = (
            lax.all_gather(prenorm_scaling, ("dp", "mp"), axis=0, tiled=True),
            lax.all_gather(prenorm_offset, ("dp", "mp"), axis=0, tiled=True),
            lax.all_gather(postnorm_scaling, ("dp", "mp"), axis=0, tiled=True),
            lax.all_gather(postnorm_offset, ("dp", "mp"), axis=0, tiled=True),
            lax.all_gather(attention_blend, ("dp", "mp"), axis=1, tiled=True),
            lax.all_gather(feedforward_blend, ("dp", "mp"), axis=1, tiled=True),
            lax.all_gather(forgetting_logrates, ("dp", "mp"), axis=0, tiled=True),
            lax.all_gather(present_reward, ("dp", "mp"), axis=0, tiled=True),
            lax.all_gather(projection_matrices, ("dp", "mp"), axis=1, tiled=True),
            lax.all_gather(final_matrix, ("dp", "mp"), axis=0, tiled=True),
        )
        local = (
            lax.all_gather(address_matrix, "dp", axis=0, tiled=True),
            lax.all_gather(content_matrix, "dp", axis=1, tiled=True),
        )
        fetched = (shared, local)
        shared, local = fetched
        gain_one, bias_one, gain_two, bias_two, tmix_w, cmix_w, decay_w, first_w, mix_w, out_w = (
            shared
        )
        key_w, value_w = local
        mix_part = take_share(mix_w[0:3], 2, groups, shares, mp_place)
        out_part = take_share(out_w, 0, groups, shares, mp_place)
        decay_part = take_share(decay_w, 0, groups, shares, mp_place)
        first_part = take_share(first_w, 0, groups, shares, mp_place)
        lower_row = micro_index * batch_rows
        upper_row = lower_row + batch_rows
        stream_f = residual_input[lower_row:upper_row].astype(jnp.float32)
        retain_marker = keep_all[lower_row:upper_row]
        article_labels = article_numbers[lower_row:upper_row]
        grad_out = upstream_gradient[lower_row:upper_row].astype(jnp.float32)

        def first_local(values_in, gain_vec, bias_vec, factors):
            return first_piece(values_in, gain_vec, bias_vec, factors, retain_marker)

        def time_local(address_series, content_series, acceptance_gate, decay_vec, first_vec):
            return time_piece(
                address_series,
                content_series,
                acceptance_gate,
                decay_vec,
                first_vec,
                retain_marker,
                article_labels,
                BLOCK,
            )

        def channel_local(values_in, gain_vec, bias_vec, factors):
            return channel_piece(values_in, gain_vec, bias_vec, factors, retain_marker)

        mixes, pull_first = jax.vjp(
            first_local,
            stream_f,
            gain_one.astype(jnp.float32),
            bias_one.astype(jnp.float32),
            tmix_w.astype(jnp.float32),
        )
        key_in = mixes[0].astype(jnp.bfloat16)
        value_in = mixes[1].astype(jnp.bfloat16)
        rec_in = mixes[2].astype(jnp.bfloat16)
        address_series = project(key_in, mix_part[0])
        content_series = project(value_in, mix_part[1])
        acceptance_gate = project(rec_in, mix_part[2])
        gated, pull_time = jax.vjp(
            time_local,
            address_series,
            content_series,
            acceptance_gate,
            decay_part.astype(jnp.float32),
            first_part.astype(jnp.float32),
        )
        gated_low = gated.astype(jnp.bfloat16)
        branch = project(gated_low, out_part)
        branch = lax.psum(branch, "mp")
        middle = stream_f + branch
        channel_ins, pull_channel = jax.vjp(
            channel_local,
            middle,
            gain_two.astype(jnp.float32),
            bias_two.astype(jnp.float32),
            cmix_w.astype(jnp.float32),
        )
        ckey_in = channel_ins[0].astype(jnp.bfloat16)
        crec_in = channel_ins[1].astype(jnp.bfloat16)
        hidden = project(ckey_in, key_w)
        active = jax.nn.relu(hidden)
        squared = (active * active).astype(jnp.bfloat16)
        carried = lax.psum(project(squared, value_w).astype(jnp.bfloat16), "mp").astype(jnp.float32)
        gate_sig = jax.nn.sigmoid(project(crec_in, mix_w[3]))
        outputs.append((middle + gate_sig * carried).astype(jnp.bfloat16))
        grad_carried = (grad_out * gate_sig).astype(jnp.bfloat16)
        grad_gate = (grad_out * carried * gate_sig * (1.0 - gate_sig)).astype(jnp.bfloat16)
        grad_value_w = weight_grad(squared, grad_carried)
        grad_hidden = (back_project(grad_carried, value_w) * 2.0 * active).astype(jnp.bfloat16)
        grad_key_w = weight_grad(ckey_in, grad_hidden)
        grad_crec_w = weight_grad(crec_in, grad_gate)
        grad_ckey = lax.psum(back_project(grad_hidden, key_w).astype(jnp.bfloat16), "mp").astype(
            jnp.float32
        )
        grad_crec = back_project(grad_gate, mix_w[3])
        grad_middle, grad_gain_two, grad_bias_two, grad_cmix = pull_channel((grad_ckey, grad_crec))
        grad_middle = grad_middle + grad_out
        grad_branch = grad_middle.astype(jnp.bfloat16)
        grad_out_w = weight_grad(gated_low, grad_branch)
        grad_gated = back_project(grad_branch, out_part)
        grad_keys, grad_values, grad_recept, grad_decay, grad_first = pull_time(grad_gated)
        grad_keys = grad_keys.astype(jnp.bfloat16)
        grad_values = grad_values.astype(jnp.bfloat16)
        grad_recept = grad_recept.astype(jnp.bfloat16)
        grad_mix_three = jnp.stack(
            [
                weight_grad(key_in, grad_keys),
                weight_grad(value_in, grad_values),
                weight_grad(rec_in, grad_recept),
            ]
        )
        grad_ins = (
            back_project(grad_keys, mix_part[0]),
            back_project(grad_values, mix_part[1]),
            back_project(grad_recept, mix_part[2]),
        )
        pulled = pull_first(grad_ins)
        pulled = (
            lax.psum(pulled[0].astype(jnp.bfloat16), "mp").astype(jnp.float32),
            lax.psum(pulled[1].astype(jnp.bfloat16), "mp").astype(jnp.float32),
            lax.psum(pulled[2].astype(jnp.bfloat16), "mp").astype(jnp.float32),
            lax.psum(pulled[3].astype(jnp.bfloat16), "mp").astype(jnp.float32),
        )
        grad_stream, grad_gain_one, grad_bias_one, grad_tmix = pulled
        input_grads.append(grad_stream + grad_middle)
        current = [
            grad_gain_one,
            grad_bias_one,
            grad_gain_two,
            grad_bias_two,
            grad_tmix,
            grad_cmix,
            grad_decay,
            grad_first,
            grad_mix_three,
            grad_crec_w,
            grad_out_w,
            grad_key_w,
            grad_value_w,
        ]
        totals = (
            current
            if totals is None
            else [earlier + latest for earlier, latest in zip(totals, current)]
        )

    def pick(gradient, axis_at):
        return take_share(gradient, axis_at, groups, shares, mp_place)

    split_grads = (
        lax.psum_scatter(pick(totals[0], 0), "dp", scatter_dimension=0, tiled=True),
        lax.psum_scatter(pick(totals[1], 0), "dp", scatter_dimension=0, tiled=True),
        lax.psum_scatter(pick(totals[2], 0), "dp", scatter_dimension=0, tiled=True),
        lax.psum_scatter(pick(totals[3], 0), "dp", scatter_dimension=0, tiled=True),
        lax.psum_scatter(pick(totals[4], 1), "dp", scatter_dimension=1, tiled=True),
        lax.psum_scatter(pick(totals[5], 1), "dp", scatter_dimension=1, tiled=True),
        lax.psum_scatter(totals[6], "dp", scatter_dimension=0, tiled=True),
        lax.psum_scatter(totals[7], "dp", scatter_dimension=0, tiled=True),
        lax.psum_scatter(totals[10], "dp", scatter_dimension=0, tiled=True),
    )
    feature_count = totals[9].shape[0]
    share_mask = jax.nn.one_hot(mp_place, shares, dtype=jnp.float32)
    three_full = (
        totals[8].reshape(3, feature_count, groups, 1, feature_count // (groups * shares))
        * share_mask[None, None, None, :, None]
    )
    three_full = three_full.reshape(3, feature_count, feature_count)
    crec_grad = totals[9] * (mp_place == 0).astype(jnp.float32)
    mix_grad = lax.psum_scatter(
        jnp.concatenate([three_full, crec_grad[None]], axis=0),
        ("dp", "mp"),
        scatter_dimension=1,
        tiled=True,
    )
    shared_grads = (
        split_grads[0],
        split_grads[1],
        split_grads[2],
        split_grads[3],
        split_grads[4],
        split_grads[5],
        split_grads[6],
        split_grads[7],
        mix_grad,
        split_grads[8],
    )
    channel_grads = (
        lax.psum_scatter(totals[11], "dp", scatter_dimension=0, tiled=True),
        lax.psum_scatter(totals[12], "dp", scatter_dimension=1, tiled=True),
    )
    output = jnp.concatenate(outputs, axis=0)
    input_grad = jnp.concatenate(input_grads, axis=0)
    return (
        output,
        input_grad,
        shared_grads[0],
        shared_grads[1],
        shared_grads[2],
        shared_grads[3],
        shared_grads[4],
        shared_grads[5],
        shared_grads[6],
        shared_grads[7],
        shared_grads[8],
        shared_grads[9],
        channel_grads[0],
        channel_grads[1],
    )


MESH = pl.DeviceIdType.MESH
MIB = 2**20

class Place:
    def __init__(self):
        self.dp = lax.axis_index("dp")
        self.mp = lax.axis_index("mp")
        self.core = self.dp % 2
        self.x = (self.dp // 2) % 2
        self.y = self.dp // 4
        self.sib = (self.dp + 1 - 2 * self.core, self.mp)
        self.xn = (self.dp + 2 - 4 * self.x, self.mp)
        self.yn = (self.dp + 4 - 8 * self.y, self.mp)
        self.up_z = (self.mp + 1) % 4
        self.down_z = (self.mp + 3) % 4
        self.far_z = (self.mp + 2) % 4
        self.up = (self.dp, self.up_z)
        self.down = (self.dp, self.down_z)
        self.pair = (self.dp, self.mp + 1 - 2 * (self.mp % 2))
        self.across = (self.dp + 6 - 4 * self.x - 8 * self.y, self.mp)


def greet(devices):
    barrier = pltpu.get_barrier_semaphore()
    for device in devices:
        pl.semaphore_signal(barrier, inc=1, device_id=device, device_id_type=MESH)
    pl.semaphore_wait(barrier, len(devices))


class Messages:
    def __init__(self, send_sem, recv_sems):
        self.send_sem, self.recv_sems, self.count, self.sent = send_sem, recv_sems, 0, []

    def send(self, source, target, arrival, device, when=None):
        index = self.count
        self.count += 1
        copy = pltpu.make_async_remote_copy(source, target, self.send_sem, self.recv_sems.at[index], device_id=device, device_id_type=MESH)
        only(when, copy.start)
        self.sent.append((when, copy))
        return pltpu.make_async_remote_copy(arrival, arrival, self.send_sem, self.recv_sems.at[index], device_id=device, device_id_type=MESH)

    def finish(self):
        for when, copy in self.sent:
            only(when, copy.wait_send)
        self.sent = []


def only(when, action):
    if when is None:
        action()
    else:
        pl.when(when)(action)


ALL = slice(None)


class Stream:
    def __init__(self, place, messages, order, piece, own, twin_sem):
        self.p, self.msg, self.order, self.piece, self.own, self.twin_sem = place, messages, order, piece, own, twin_sem
        p = place
        self.first = order.replace("z", "")[0]
        self.z_leads = order[0] == "z"
        self.a, self.b = (p.x, p.y) if self.first == "x" else (p.y, p.x)
        self.na, self.nb = (p.xn, p.yn) if self.first == "x" else (p.yn, p.xn)
        self.base = messages.count
        messages.count += 15

    def at(self, col, other, slab, core=None):
        a = self.a if col == 0 else 1 - self.a
        b = 1 - self.b if other else self.b
        y, x = (b, a) if self.first == "x" else (a, b)
        return self.piece(y, x, self.p.core if core is None else core, slab)

    def slab(self, j):
        m = self.p.mp
        if j == 0:
            return m
        flip = (m >= 2).astype(jnp.int32)
        near = m + flip * (3 - 2 * m)
        picked = j - (j <= near).astype(jnp.int32)
        return picked + flip * (3 - 2 * picked)

    def rank(self, m, slab):
        flip = (m >= 2).astype(jnp.int32)
        near = m + flip * (3 - 2 * m)
        picked = slab + flip * (3 - 2 * slab)
        return picked - (picked > near).astype(jnp.int32) + 1

    def index(self, kind, col, j):
        if self.z_leads:
            return self.base + {"z": j - 1, "a": 3 + j, "b": 7 + 4 * col + j}[kind]
        return self.base + {"z": 3 * col + j - 1, "a": 6, "b": 7 + 4 * col + j}[kind]

    def copy(self, piece, index, device, when=None, source=None):
        copy = pltpu.make_async_remote_copy(
            piece if source is None else source, piece, self.msg.send_sem, self.msg.recv_sems.at[index],
            device_id=device, device_id_type=MESH,
        )
        only(when, copy.start)
        self.msg.sent.append((when, copy))

    def twin(self, col, other, slab, source=None):
        piece = self.at(col, other, slab)
        sem = self.twin_sem(slab)
        copy = pltpu.make_async_remote_copy(
            piece if source is None else source, piece, self.msg.send_sem, sem,
            device_id=self.p.sib, device_id_type=MESH,
        )
        copy.start()
        self.msg.sent.append((None, copy))

    def send_z(self, col, j, source=None):
        m = self.p.mp
        slab = self.slab(j)
        piece = self.at(col, 0, slab)
        if j == 0:
            self.copy(piece, self.index("z", col, 1) + self.rank(m + 1, slab) - 1, self.p.up, m < 3, source)
            self.copy(piece, self.index("z", col, 1) + self.rank(m - 1, slab) - 1, self.p.down, m > 0, source)
            return
        target = m - 1 + 2 * (slab < m).astype(jnp.int32)
        safe = (target + 4) % 4
        self.copy(piece, self.index("z", col, 1) + self.rank(target, slab) - 1, (self.p.dp, safe), (target >= 0) & (target <= 3))

    def send_a(self, j, source=None):
        self.copy(self.at(0, 0, self.slab(j)), self.index("a", 0, j), self.na, source=source)

    def send_b(self, col, j, source=None):
        self.copy(self.at(col, 0, self.slab(j)), self.index("b", col, j), self.nb, source=source)

    def event(self, kind, col, j):
        if kind == "o":
            self.send_z(0, 0, self.own)
            self.send_a(0, self.own)
            self.send_b(0, 0, self.own)
            self.twin(0, 0, self.p.mp, self.own)
            return
        slab = self.slab(j)
        piece = self.at(1 if kind == "a" else col, kind == "b", slab)
        sem = self.msg.recv_sems.at[self.index(kind, col, j)]
        pltpu.make_async_remote_copy(piece, piece, self.msg.send_sem, sem, device_id=self.na, device_id_type=MESH).wait_recv()
        if kind == "z":
            self.send_z(col, j)
            if self.z_leads:
                self.send_a(j)
            self.send_b(col, j)
            self.twin(col, 0, slab)
        elif kind == "a":
            if not self.z_leads:
                self.send_z(1, 0)
            self.send_b(1, j)
            self.twin(1, 0, slab)
        else:
            self.twin(col, 1, slab)


PARTS = (
    ("t", 0, 48, "zxy"),
    ("t", 48, 32, "zyx"),
    ("t", 80, 48, "xzy"),
    ("k", 0, 96, "yzx"),
    ("v", 0, 96, "zxy"),
)
EVENTS = {
    "own": ("0o00", "1o00", "2o00", ),
    "relayA": ("0z01", "3o00", "1b00", "1z01", "1a00", "0a01", "0z02", "0z03", "1z02", "0b01", "1z03", "3a00", "0b11", "0a02", "0a03", "2a00", "1b02", "1a01", "0a00", "2z01", "0b00", "0b03", "1b01", "1a02", "1a03", "4o00", "3z12", "0b12", "2b00", "1b10", "2z11", "1b12", "1b11", "0b02", "3b10", "3b00", "0b10", "0b13", "2z03", "4z01", "1b13", "1b03", "3z11", "2z12", ),
    "a0.0": ("2z13", ),
    "a0.1": ("3z01", "2z02", ),
    "a0.2": (),
    "a1.0": ("4z03", ),
    "a1.1": (),
    "a1.2": (),
    "a2.0": ("4b00", "4a01", "4z02", "2b10", ),
    "a2.1": ("2b11", ),
    "a2.2": ("2b12", ),
    "a3.0": ("3z13", ),
    "a3.1": (),
    "a3.2": ("2b01", "4b01", ),
    "relayB": ("4a00", "3b11", "3z02", "2b03", "2b13", "3b12", "2b02", ),
    "b0.0": (),
    "b0.1": ("3z03", ),
    "b1.0": (),
    "b1.1": ("4a02", "4b11", "4b02", ),
    "b2.0": (),
    "b2.1": ("4b10", ),
    "b3.0": ("4a03", "4b03", ),
    "b3.1": ("3b02", "3b01", "3b13", ),
    "h0": ("3b03", ),
    "h1": (),
    "h2": ("4b12", ),
    "h3": (),
    "c0": (),
    "c1": ("4b13", ),
    "c2": (),
    "c3": (),
    "fin": (),
    "end": (),
}


def streams(place, messages, twin_sems, pk, kw, vt, tw, kg, vg):
    def piece_of(name, start, rows):
        if name == "t":
            return lambda y, x, c, m: tw.at[y, x, c, m, pl.ds(start, rows)]
        array = kg if name == "k" else vg
        return lambda y, x, c, m: array.at[m, y, x, c, pl.ds(start, rows)]

    made = []
    for name, start, rows, order in PARTS:
        own = {"t": pk, "k": kw, "v": vt}[name].at[pl.ds(start, rows)]
        if name == "t":
            twin = lambda slab, i=start // 80: twin_sems.at[i]
        else:
            twin = lambda slab, i=2 if name == "k" else 6: twin_sems.at[i + slab]
        made.append(Stream(place, messages, order, piece_of(name, start, rows), own, twin))
    return made


def play(made, marker):
    for event in EVENTS[marker]:
        made[int(event[0])].event(event[1], int(event[2]), int(event[3]))


def greet_all(p):
    barrier = pltpu.get_barrier_semaphore()
    for device in (p.sib, p.xn, p.yn):
        pl.semaphore_signal(barrier, inc=1, device_id=device, device_id_type=MESH)
    only(p.mp < 3, lambda: pl.semaphore_signal(barrier, inc=1, device_id=p.up, device_id_type=MESH))
    only(p.mp > 0, lambda: pl.semaphore_signal(barrier, inc=1, device_id=p.down, device_id_type=MESH))
    pl.semaphore_wait(barrier, 3 + (p.mp < 3).astype(jnp.int32) + (p.mp > 0).astype(jnp.int32))


TILE = 256
SPAN = 128
WIDE = 512


def dot(a, b):
    return jnp.dot(a, b, preferred_element_type=jnp.float32)


def dot_nt(a, b):
    return lax.dot_general(a, b, (((1,), (1,)), ((), ())), preferred_element_type=jnp.float32)


def dot_tn(a, b):
    return lax.dot_general(a, b, (((0,), (0,)), ((), ())), preferred_element_type=jnp.float32)


def low(values):
    return values.astype(jnp.bfloat16)


def wide(values):
    return values.astype(jnp.float32)


def row_sums(values):
    rows, width = values.shape
    return jnp.sum(values.reshape(rows // 8, 8, width), axis=0)


def standardise(values):
    centered = values - jnp.mean(values, axis=-1, keepdims=True)
    variance = jnp.mean(centered * centered, axis=-1, keepdims=True)
    scale = lax.rsqrt(variance + epsilon)
    return centered * scale, scale


def norm_back(grad, normal, scale):
    mean_grad = jnp.mean(grad, axis=-1, keepdims=True)
    mean_both = jnp.mean(grad * normal, axis=-1, keepdims=True)
    return scale * (grad - mean_grad - normal * mean_both)


def later(values, first_row):
    row = lax.broadcasted_iota(jnp.int32, values.shape, 0)
    return jnp.where(row == 0, first_row, pltpu.roll(values, 1, 0))


def sooner(values, last_row):
    rows = values.shape[0]
    row = lax.broadcasted_iota(jnp.int32, values.shape, 0)
    return jnp.where(row == rows - 1, last_row, pltpu.roll(values, rows - 1, 0))


def halves(target, values):
    for span in range(values.shape[0] // SPAN):
        part = values[span * SPAN : (span + 1) * SPAN]
        high = low(part)
        target[span, 0:SPAN, :] = high
        target[span, SPAN : 2 * SPAN, :] = low(part - wide(high))


GAIN1, BIAS1, GAIN2, BIAS2, MIX, DECAY, FIRST, BLEND = 0, 1, 2, 3, 4, 7, 8, 9


def vec(ref, index):
    return ref[index : index + 1, :]


def rows_at(start, count):
    return pl.ds(pl.multiple_of(start, 128), count)


def pack_block(p, proj, final, vectors, pk):
    spread = jnp.concatenate([wide(vectors[...]), jnp.zeros((16, 256), jnp.float32)], axis=1)
    spread = pltpu.roll(spread, 24 * ((4 * p.dp + p.mp) % 16), 1)
    spread = jnp.concatenate([spread[:8], spread[8:]], axis=1)
    rows = [wide(proj[0]), wide(proj[1]), wide(proj[2]), spread, wide(proj[3]), wide(final[...])]
    pk[...] = low(jnp.concatenate(rows, axis=0))


def row_of(docs, row):
    return wide(jnp.where(row == 0, docs[0:1, :], docs[1:2, :]))


def describe(docs, row, cols):
    own = row_of(docs, row)
    lane = lax.broadcasted_iota(jnp.int32, own.shape, 1)
    keep = jnp.where((lane > 0) & (own == pltpu.roll(own, 1, 1)), 1.0, 0.0)
    spans = own.shape[1] // SPAN
    none = jnp.zeros((1, SPAN), jnp.float32)
    for i in range(spans):
        part = own[:, i * SPAN : (i + 1) * SPAN]
        before = after = none
        if i > 0:
            before = jnp.where(part == own[:, i * SPAN - 1 : i * SPAN], 1.0, 0.0)
        if i < spans - 1:
            after = jnp.where(part == own[:, (i + 1) * SPAN : (i + 1) * SPAN + 1], 1.0, 0.0)
        rows = [part, keep[:, i * SPAN : (i + 1) * SPAN], before, after, jnp.zeros((SPAN - 4, SPAN), jnp.float32)]
        cols[i * SPAN : (i + 1) * SPAN, :] = jnp.concatenate(rows, axis=0).T


def forward_kernel(
    proj, final, vectors, kw, vt, docs, x_any, gy_any,
    kg, vg, acts, kvs, middle_o, sq_o, act_o, grads_o, out_o, wts_o, vecs_o, cols_o,
    w5, kv, sa, xb, st, f5, mid, sig, tables, vecs, prev, cols, split, pk, sems, twin_sems, send_sem, recv_sems,
):
    place_of = Place()
    p = place_of
    row = p.mp % 2
    load_x = pltpu.make_async_copy(x_any.at[row], xb, sems.at[0])
    load_x.start()
    pack_block(p, proj, final, vectors, pk)
    keep = [
        pltpu.make_async_copy(pk, sa.at[p.y, p.x, p.core, p.mp], sems.at[26]),
        pltpu.make_async_copy(kw, kg.at[p.mp, p.y, p.x, p.core], sems.at[27]),
        pltpu.make_async_copy(vt, vg.at[p.mp, p.y, p.x, p.core], sems.at[28]),
    ]
    for copy in keep:
        copy.start()
    greet_all(place_of)
    messages = Messages(send_sem, recv_sems)
    made = streams(place_of, messages, twin_sems, pk, kw, vt, sa, kg, vg)

    def twins(i, half):
        pltpu.make_async_copy(half, half, twin_sems.at[i]).wait()

    def time_twins(i):
        twins(i, sa.at[:, :, 1 - p.core, :, (pl.ds(0, 80), pl.ds(80, 48))[i]])

    prev[...] = jnp.zeros_like(prev)
    play(made, "own")
    describe(docs, row, cols)
    own_docs = row_of(docs, row)
    play(made, "relayA")
    for copy in keep:
        copy.wait()
    time_twins(0)

    def relay(half, first_row, count, slots):
        def body(i, total):
            core, m = i // 2, 2 * (i % 2)
            pair = 8 * half + i
            spot = half, i // 4, core % 2
            rows = pl.ds(first_row, count)
            one, two = wide(sa[spot + (m, rows)]), wide(sa[spot + (m + 1, rows)])
            for n, j in enumerate(slots):
                piece = jnp.concatenate([one[24 * n : 24 * n + 24], two[24 * n : 24 * n + 24]], axis=0)
                w5[j, pl.ds(pl.multiple_of(48 * pair, 16), 48), :] = low(piece)
            return total + one[count - 8 :] + two[count - 8 :]

        return lax.fori_loop(0, 8, body, jnp.zeros((8, 768), jnp.float32))

    left, right = relay(0, 0, 80, (0, 1, 2)), relay(1, 0, 80, (0, 1, 2))
    vecs[0:8, :] = jnp.concatenate([left[:, :384], right[:, :384]], axis=1)
    vecs[8:16, :] = jnp.concatenate([left[:, 384:], right[:, 384:]], axis=1)
    save_v = pltpu.make_async_copy(vecs, vecs_o, sems.at[11])
    save_v.start()

    rate = jnp.exp(vec(vecs, DECAY))
    fade = jnp.exp(-rate)
    place = wide(lax.broadcasted_iota(jnp.int32, (TILE, 1), 0) % SPAN)
    tables[0] = jnp.exp((place - 64.0) * rate)
    tables[1] = jnp.exp((65.0 - place) * rate)
    tables[2] = jnp.exp(-place * rate)
    load_x.wait()
    tiles = [(t, t * TILE, pl.ds(t * TILE, TILE)) for t in range(1024 // TILE)]
    for t, base, r in tiles:
        play(made, f"a{t}.0")

        def first(q, last):
            x = wide(xb[q, :])
            mean = jnp.mean(x, axis=-1, keepdims=True)
            centered = x - mean
            scale = lax.rsqrt(jnp.mean(centered * centered, axis=-1, keepdims=True) + epsilon)
            cols[q, 4:5] = mean
            cols[q, 5:6] = scale
            normed = centered * scale * vec(vecs, GAIN1) + vec(vecs, BIAS1)
            earlier = later(normed, last) * cols[q, 1:2]
            delta = normed - earlier
            for j in range(3):
                st[j, q, :] = low(earlier + delta * vec(vecs, MIX + j))
            st[6, q, :] = low(delta)
            return normed[TILE - 1 :]

        prev[0:1, :] = first(r, prev[0:1, :])
        for j in range(3):
            f5[j, r, :] = dot(st[j, r, :], w5[j])
        play(made, f"a{t}.1")

        key_exp = jnp.exp(f5[0, r, :])
        f5[2, r, :] = jax.nn.sigmoid(f5[2, r, :])
        grown = key_exp * tables[0]
        halves(split.at[0], grown * f5[1, r, :])
        halves(split.at[1], grown)
        time = lax.broadcasted_iota(jnp.int32, (SPAN, SPAN), 0)
        source = lax.broadcasted_iota(jnp.int32, (SPAN, SPAN), 1)
        for i in range(TILE // SPAN):
            block = t * (TILE // SPAN) + i
            same = cols[pl.ds(block * SPAN, SPAN), 0:1] == own_docs[:, block * SPAN : (block + 1) * SPAN]
            mask = jnp.where(same & (source < time), 1.0, 0.0).astype(jnp.bfloat16)
            mask = jnp.concatenate([mask, mask], axis=1)
            for k in range(2):
                f5[3 + k, pl.ds(block * SPAN, SPAN), :] = dot(mask, split[k, i])
        play(made, f"a{t}.2")
        for i in range(TILE // SPAN):
            begin = base + i * SPAN
            top_in, bottom_in = prev[2:3, :], prev[3:4, :]

            q = pl.ds(begin, SPAN)
            values = f5[1, q, :]
            link = cols[q, 2:3] * tables[2, 0:SPAN, :]
            top = f5[3, q, :] * tables[1, 0:SPAN, :] + link * top_in
            bottom = f5[4, q, :] * tables[1, 0:SPAN, :] + link * bottom_in
            f5[3, q, :] = top
            f5[4, q, :] = bottom
            bonus = jnp.exp(f5[0, q, :] + vec(vecs, FIRST))
            st[3, q, :] = low(f5[2, q, :] * ((top + bonus * values) / (bottom + bonus)))
            end = begin + SPAN - 1
            key_exp = jnp.exp(f5[0, end : end + 1, :])
            prev[2:3, :] = fade * f5[3, end : end + 1, :] + key_exp * f5[1, end : end + 1, :]
            prev[3:4, :] = fade * f5[4, end : end + 1, :] + key_exp
    saves = [pltpu.make_async_copy(f5, kvs, sems.at[16])]
    saves[0].start()
    play(made, "relayB")
    time_twins(1)
    relay(0, 80, 48, (3, 4))
    relay(1, 80, 48, (3, 4))
    save_w = pltpu.make_async_copy(w5, wts_o, sems.at[10])
    save_w.start()
    for t, base, r in tiles:
        play(made, f"b{t}.0")
        mid[r, :] = dot(st[3, r, :], w5[4])

        def fourth(q, last):
            middle = wide(xb[q, :]) + mid[q, :]
            mid[q, :] = middle
            mean = jnp.mean(middle, axis=-1, keepdims=True)
            centered = middle - mean
            scale = lax.rsqrt(jnp.mean(centered * centered, axis=-1, keepdims=True) + epsilon)
            cols[q, 6:7] = mean
            cols[q, 7:8] = scale
            normed = centered * scale * vec(vecs, GAIN2) + vec(vecs, BIAS2)
            earlier = later(normed, last) * cols[q, 1:2]
            delta = normed - earlier
            for j in range(2):
                st[4 + j, q, :] = low(earlier + delta * vec(vecs, BLEND + j))
            st[7, q, :] = low(delta)
            return normed[TILE - 1 :]

        prev[1:2, :] = fourth(r, prev[1:2, :])
        play(made, f"b{t}.1")
        sig[r, :] = dot(st[5, r, :], w5[3])
        saves += [
            pltpu.make_async_copy(st.at[:, r], acts.at[:, r], sems.at[12 + t]),
            pltpu.make_async_copy(mid.at[r], middle_o.at[r], sems.at[20 + t]),
        ]
        for copy in saves[-2:]:
            copy.start()
    saves.append(pltpu.make_async_copy(cols, cols_o, sems.at[36]))
    saves[-1].start()
    load_gy = pltpu.make_async_copy(gy_any.at[row], xb, sems.at[24])
    load_gy.start()
    messages.finish()

    def load_kv(m, which, array):
        target = kv.at[m]
        return pltpu.make_async_copy(array.at[m], target, sems.at[4 * which + 1 + m])

    pending = {}
    for m in range(4):
        play(made, f"h{m}")
        if m == 0:
            for slab in range(4):
                twins(2 + slab, kg.at[slab, :, :, 1 - p.core])
                load_kv(slab, 0, kg).start()
        load_kv(m, 0, kg).wait()
        if m == 0:
            for copy in saves:
                copy.wait()

        def hidden(t, carry):
            r = rows_at(t * WIDE, WIDE)
            active = jnp.maximum(dot(st[4, r, :], kv[m].reshape(768, 768)), 0.0)
            squared = low(active * active)
            spot = m // 2, m % 2, t
            sa[spot] = squared.reshape(4, 128, 768)
            st[m, r, :] = low(active)
            return carry

        lax.fori_loop(0, 1024 // WIDE, hidden, 0)
        pending[m] = pltpu.make_async_copy(st.at[m], act_o.at[m], sems.at[29 + m])
        pending[m].start()
    save_sq = pltpu.make_async_copy(sa, sq_o, sems.at[33])
    save_sq.start()
    pair = p.mp // 2
    for turn in range(2):
        play(made, f"c{2 * turn}")
        at = pair if turn == 0 else 1 - pair
        loads = []
        for i in range(2):
            slab = 2 * at + i
            twins(6 + slab, vg.at[slab, :, :, 1 - p.core])
            loads.append(pltpu.make_async_copy(vg.at[slab], kv.at[2 * turn + i], sems.at[5 + 2 * turn + i]))
            loads[-1].start()
        for i in range(2):
            loads[i].wait()
            if i == 1:
                play(made, f"c{2 * turn + 1}")

            def content(t, carry):
                r = rows_at(t * WIDE, WIDE)
                squared = sa[at, i, t].reshape(WIDE, 768)
                part = dot_nt(squared, kv[2 * turn + i].reshape(768, 768))
                f5[turn, r, :] = part if i == 0 else f5[turn, r, :] + part
                return carry

            lax.fori_loop(0, 1024 // WIDE, content, 0)

    play(made, "fin")
    play(made, "end")
    load_gy.wait()

    last = []
    for t, _, q in tiles:
        gate = jax.nn.sigmoid(sig[q, :])
        carried = f5[0, q, :] + f5[1, q, :]
        st[5, q, :] = low(mid[q, :] + gate * carried)
        passed = wide(xb[q, :]) * gate
        st[6, q, :] = low(passed)
        st[7, q, :] = low(passed * carried * (1.0 - gate))
        last += [
            pltpu.make_async_copy(st.at[5, q], out_o.at[q], sems.at[37 + t]),
            pltpu.make_async_copy(st.at[pl.ds(6, 2), q], grads_o.at[:, q], sems.at[41 + t]),
        ]
        for copy in last[-2:]:
            copy.start()
    save_w.wait()
    save_v.wait()
    save_sq.wait()
    for m in range(4):
        pending.pop(m).wait()
    messages.finish()
    for copy in last:
        copy.wait()


ANY = pl.BlockSpec(memory_space=pl.ANY)
ON_CORE = pl.BlockSpec(memory_space=pltpu.VMEM)
LIMIT = 63 * MIB


def forward(proj, final, vectors, kw, vt, docs, x, gy):
    bf, f32 = jnp.bfloat16, jnp.float32
    shape = jax.ShapeDtypeStruct
    return pl.pallas_call(
        forward_kernel,
        out_shape=(
            shape((4, 2, 2, 2, 96, 768), bf), shape((4, 2, 2, 2, 96, 768), bf),
            shape((8, 1024, 768), bf), shape((5, 1024, 768), f32), shape((1024, 768), f32),
            shape((2, 2, 2, 4, 128, 768), bf), shape((4, 1024, 768), bf), shape((2, 1024, 768), bf),
            shape((1024, 768), bf), shape((5, 768, 768), bf), shape((16, 768), f32), shape((1024, 128), f32),
        ),
        in_specs=[ON_CORE] * 6 + [ANY] * 2,
        out_specs=[ANY] * 12,
        scratch_shapes=[
            pltpu.VMEM((5, 768, 768), bf), pltpu.VMEM((4, 2, 2, 2, 96, 768), bf), pltpu.VMEM((2, 2, 2, 4, 128, 768), bf),
            pltpu.VMEM((1024, 768), bf), pltpu.VMEM((8, 1024, 768), bf), pltpu.VMEM((5, 1024, 768), f32),
            pltpu.VMEM((1024, 768), f32), pltpu.VMEM((1024, 768), f32),
            pltpu.VMEM((3, TILE, 768), f32), pltpu.VMEM((16, 768), f32), pltpu.VMEM((8, 768), f32),
            pltpu.VMEM((1024, 128), f32), pltpu.VMEM((2, 2, 2 * SPAN, 768), bf), pltpu.VMEM((128, 768), bf),
            pltpu.SemaphoreType.DMA((45,)), pltpu.SemaphoreType.DMA((10,)), pltpu.SemaphoreType.DMA,
            pltpu.SemaphoreType.DMA((15 * len(PARTS),)),
        ],
        compiler_params=pltpu.CompilerParams(vmem_limit_bytes=LIMIT, collective_id=0, has_side_effects=True),
        name="forward",
    )(proj, final, vectors, kw, vt, docs, x, gy)


class Scatter:
    def __init__(self, place, messages, source, received, kept, steps, final, orders):
        self.p, self.msg = place, messages
        self.source, self.received, self.kept, self.steps, self.final = source, received, kept, steps, final
        self.orders = orders
        self.parts = len(orders)
        self.core_waits, self.waits = {}, []

    def cols(self, part):
        width = self.kept.shape[-1] // self.parts
        return pl.ds(part * width, width)

    def start(self, j):
        p = self.p
        target = self.received.at[:, j]
        self.core_waits[j] = self.msg.send(self.source.at[:, j, :, :, 1 - p.core], target, target, p.sib)

    def core(self, j):
        p = self.p
        self.core_waits[j].wait_recv()
        for i in range(self.kept.shape[0]):
            for y in range(2):
                for x in range(2):
                    total = wide(self.source[i, j, y, x, p.core]) + wide(self.received[i, j, y, x])
                    self.kept[i, j, y, x] = total.astype(self.kept.dtype)
        self.send(0, j)

    def index(self, order, step, flip):
        p = self.p
        mine = {"x": p.x, "y": p.y, "j": p.mp % 2}
        picked = {}
        for at, axis in enumerate(order):
            if at < step:
                picked[axis] = mine[axis]
            elif at == step:
                picked[axis] = 1 - mine[axis] if flip else mine[axis]
            else:
                picked[axis] = None
        return picked

    def send(self, step, j=None):
        p = self.p
        device = {"x": p.xn, "y": p.yn, "j": p.pair}
        if step > 0:
            self.waits = []
        for part in range(self.parts):
            order = self.orders[part]
            picked = self.index(order, step, True)
            target = self.steps[step].at[part]
            if j is not None:
                picked["j"] = j
                target = self.steps[step].at[part, :, j]
            select = tuple(ALL if picked[a] is None else picked[a] for a in "jyx")
            piece = self.kept.at[(ALL,) + select + (ALL, self.cols(part))]
            self.waits.append(self.msg.send(piece, target, target, device[order[step]]))

    def add(self, step, last=False):
        for wait in self.waits:
            wait.wait_recv()
        for part in range(self.parts):
            picked = self.index(self.orders[part], step, False)
            free = [a for a in "jyx" if picked[a] is None]
            for i in range(self.kept.shape[0]):
                for number in range(2 ** len(free)):
                    bits = {a: (number >> (len(free) - 1 - k)) & 1 for k, a in enumerate(free)}
                    select = tuple(bits[a] if picked[a] is None else picked[a] for a in "jyx")
                    spot = (i,) + select + (ALL, self.cols(part))
                    arrived = self.steps[step][(part, i) + tuple(bits[a] for a in free)]
                    total = wide(self.kept[spot]) + wide(arrived)
                    if step == 2:
                        self.final[i, :, self.cols(part)] = total
                    else:
                        self.kept[spot] = total.astype(self.kept.dtype)
        if step < 2 and not last:
            self.send(step + 1)


class Plane:
    def __init__(self, place, messages, source, received, kept, arrived, last, final):
        self.p, self.msg = place, messages
        self.source, self.received, self.kept, self.arrived, self.last, self.final = source, received, kept, arrived, last, final

    def start(self):
        p = self.p
        self.wait = self.msg.send(self.source.at[:, :, :, 1 - p.core], self.received, self.received, p.sib)

    def core(self):
        p, kept = self.p, self.kept
        self.wait.wait_recv()
        for j in range(2):
            for y in range(2):
                for x in range(2):
                    total = wide(self.source[j, y, x, p.core]) + wide(self.received[j, y, x])
                    kept[j, y, x] = total.astype(kept.dtype)
        pieces = (
            (kept.at[:, 1 - p.y, 1 - p.x], p.across), (kept.at[:, p.y, 1 - p.x], p.xn), (kept.at[:, 1 - p.y, p.x], p.yn),
        )
        self.waits = [
            self.msg.send(piece, self.arrived.at[n], self.arrived.at[n], device) for n, (piece, device) in enumerate(pieces)
        ]

    def plane(self):
        p, kept = self.p, self.kept
        for wait in self.waits:
            wait.wait_recv()
        for j in range(2):
            total = wide(kept[j, p.y, p.x])
            for n in range(3):
                total += wide(self.arrived[n, j])
            kept[j, p.y, p.x] = total.astype(kept.dtype)
        self.wait = self.msg.send(kept.at[1 - p.mp % 2, p.y, p.x], self.last, self.last, p.pair)

    def z(self):
        p = self.p
        self.wait.wait_recv()
        self.final[...] = wide(self.kept[p.mp % 2, p.y, p.x]) + wide(self.last[...])


def plane_scratch(rows, cols, dtype):
    return [
        pltpu.VMEM((2, 2, 2, rows, cols), dtype), pltpu.VMEM((2, 2, 2, rows, cols), dtype),
        pltpu.VMEM((3, 2, rows, cols), dtype), pltpu.VMEM((rows, cols), dtype),
    ]


def channel_back_kernel(
    kg, vg, wts, acts, sq, act, grads, middle, gy_any, out_row, cols, vecs,
    gm_o, kept_o, out_o, sums_o,
    kv, sqs, acs, gcg, cc, dh, acc, wg, mid, gy, gm, delta, stage, gate_w, sums, nxt, result, received, kept, first_step, sems, send_sem, recv_sems,
):
    place = Place()
    mp = place.mp
    row, pair = mp % 2, mp // 2
    load_row = pltpu.make_async_copy(out_row, result, sems.at[22])
    load_row.start()
    greet([place.sib, place.xn, place.yn, place.pair])
    messages = Messages(send_sem, recv_sems)
    load_row.wait()
    channel = Scatter(place, messages, stage, received, kept, [first_step], None, ("xyj", "yxj"))
    arrival = messages.send(result, out_o.at[row], out_o.at[1 - row], place.pair)
    keep_row = pltpu.make_async_copy(result, out_o.at[row], sems.at[21])
    keep_row.start()
    order = [2 * pair, 2 * pair + 1, 2 - 2 * pair, 3 - 2 * pair]

    def loads(j):
        m, slot = order[j], j % 2
        copies = [
            pltpu.make_async_copy(kg.at[m], kv.at[0, slot], sems.at[3 * j]),
            pltpu.make_async_copy(vg.at[m], kv.at[1, slot], sems.at[3 * j + 1]),
            pltpu.make_async_copy(act.at[m], acs.at[slot], sems.at[3 * j + 2]),
        ]
        return copies

    load_g = pltpu.make_async_copy(grads, gcg, sems.at[12])
    load_g.start()
    for j in range(2):
        for copy in loads(j):
            copy.start()
    others = [
        pltpu.make_async_copy(sq.at[pl.ds(2 * pair, 2)], sqs, sems.at[13]),
        pltpu.make_async_copy(acts.at[pl.ds(4, 2)], cc, sems.at[14]),
        pltpu.make_async_copy(wts.at[3], wg, sems.at[15]),
        pltpu.make_async_copy(middle, mid, sems.at[16]),
        pltpu.make_async_copy(acts.at[7], delta, sems.at[19]),
        pltpu.make_async_copy(gy_any.at[row], gy, sems.at[17]),
    ]
    for copy in others:
        copy.start()
    load_g.wait()
    others[1].wait()

    def gate_weights(t, carry):
        c = pl.ds(pl.multiple_of(t * 384, 128), 384)
        gate_w[c, :] = dot_tn(cc[1, :, c], gcg[1])
        return carry

    lax.fori_loop(0, 2, gate_weights, 0)

    def gate_pack(dp, carry):
        for j in range(2):
            start = pl.multiple_of(96 * dp + 48 * pair + 24 * j, 8)
            piece = jnp.concatenate([gate_w[pl.ds(start, 24), :], jnp.zeros((8, 768), jnp.float32)], axis=0)
            stage[0, j, dp // 4, (dp // 2) % 2, dp % 2, 192:224, :] = low(piece)
        return carry

    lax.fori_loop(0, 8, gate_pack, 0)
    for j in range(4):
        slot = j % 2
        for copy in loads(j):
            copy.wait()

        def hidden_back(t, carry):
            r = rows_at(t * WIDE, WIDE)
            active = wide(acs[slot, r, :])
            grad = low(dot(gcg[0, r, :], kv[1, slot]) * (2.0 * active))
            if j < 2:
                dh[j, r, :] = grad
            part = dot_nt(grad, kv[0, slot])
            acc[j // 2, r, :] = part if j % 2 == 0 else acc[j // 2, r, :] + part
            return carry

        lax.fori_loop(0, 1024 // WIDE, hidden_back, 0)
        if j < 2:
            for copy in loads(j + 2):
                copy.start()
            if j == 0:
                others[0].wait()
            else:
                channel.core(0)

            def weights(t, carry):
                c = pl.ds(pl.multiple_of(t * 384, 128), 384)
                key = low(dot_tn(cc[0, :, c], dh[j]))
                stage[0, j, t, :, :, 0:96, :] = key.reshape(2, 2, 96, 768)
                value = low(dot_tn(gcg[0, :, c], sqs[j].reshape(1024, 768)))
                stage[0, j, t, :, :, 96:192, :] = value.reshape(2, 2, 96, 768)
                return carry

            lax.fori_loop(0, 2, weights, 0)
            channel.start(j)
        elif j == 2:
            channel.core(1)
            for copy in others[2:]:
                copy.wait()

    sums[...] = jnp.zeros_like(sums)
    nxt[...] = jnp.zeros_like(nxt)

    def gate_back(t, carry):
        r = rows_at(t * WIDE, WIDE)
        gm[r, :] = dot_nt(gcg[1, r, :], wg[...])
        return carry

    lax.fori_loop(0, 1024 // WIDE, gate_back, 0)
    gain = vec(vecs, GAIN2)
    key_mix, rec_mix = vec(vecs, BLEND), vec(vecs, BLEND + 1)

    def tokens(n, state):
        q = rows_at((1024 // TILE - 1 - n) * TILE, TILE)
        grad_key, grad_rec = acc[0, q, :] + acc[1, q, :], gm[q, :]
        step = wide(delta[q, :])
        sums[2] += row_sums(grad_key * step)
        sums[3] += row_sums(grad_rec * step)
        grad = grad_key * key_mix + grad_rec * rec_mix
        back = (grad_key + grad_rec - grad) * cols[q, 1:2]
        grad = grad + sooner(back, state)
        scale = cols[q, 7:8]
        normal = (mid[q, :] - cols[q, 6:7]) * scale
        sums[0] += row_sums(grad * normal)
        sums[1] += row_sums(grad)
        gm[q, :] = wide(gy[q, :]) + norm_back(grad * gain, normal, scale)
        return back[0:1]

    lax.fori_loop(0, 1024 // TILE, tokens, jnp.zeros((1, 768), jnp.float32))
    store_gm = pltpu.make_async_copy(gm, gm_o, sems.at[20])
    store_gm.start()
    for i in range(4):
        sums_o[i : i + 1, :] = jnp.sum(sums[i], axis=0, keepdims=True)
    sums_o[4:8, :] = jnp.zeros((4, 768), jnp.float32)
    channel.add(0, last=True)
    store = pltpu.make_async_copy(kept, kept_o, sems.at[18])
    store.start()
    store.wait()
    store_gm.wait()
    keep_row.wait()
    arrival.wait_recv()
    messages.finish()


def channel_back(kg, vg, wts, acts, sq, act, grads, middle, gy, out_row, cols, vecs):
    bf, f32 = jnp.bfloat16, jnp.float32
    shape = jax.ShapeDtypeStruct
    return pl.pallas_call(
        channel_back_kernel,
        out_shape=(
            shape((1024, 768), f32), shape((1, 2, 2, 2, 224, 768), bf),
            shape((2, 1024, 768), bf), shape((8, 768), f32),
        ),
        in_specs=[ANY] * 10 + [ON_CORE] * 2,
        out_specs=[ANY] * 3 + [ON_CORE],
        scratch_shapes=[
            pltpu.VMEM((2, 2, 768, 768), bf), pltpu.VMEM((2, 8, 128, 768), bf), pltpu.VMEM((2, 1024, 768), bf),
            pltpu.VMEM((2, 1024, 768), bf), pltpu.VMEM((2, 1024, 768), bf), pltpu.VMEM((2, 1024, 768), bf),
            pltpu.VMEM((2, 1024, 768), f32), pltpu.VMEM((768, 768), bf), pltpu.VMEM((1024, 768), f32),
            pltpu.VMEM((1024, 768), bf), pltpu.VMEM((1024, 768), f32), pltpu.VMEM((1024, 768), bf), pltpu.VMEM((1, 2, 2, 2, 2, 224, 768), bf),
            pltpu.VMEM((768, 768), f32), pltpu.VMEM((4, 8, 768), f32), pltpu.VMEM((8, 768), f32),
            pltpu.VMEM((1024, 768), bf), pltpu.VMEM((1, 2, 2, 2, 224, 768), bf), pltpu.VMEM((1, 2, 2, 2, 224, 768), bf),
            pltpu.VMEM((2, 1, 2, 2, 224, 384), bf),
            pltpu.SemaphoreType.DMA((23,)), pltpu.SemaphoreType.DMA, pltpu.SemaphoreType.DMA((7,)),
        ],
        compiler_params=pltpu.CompilerParams(vmem_limit_bytes=LIMIT, collective_id=1, has_side_effects=True),
        name="channel_back",
    )(kg, vg, wts, acts, sq, act, grads, middle, gy, out_row, cols, vecs)


def time_back_kernel(
    wts, acts, kvs, gm_any, x_any, kept_any, cols, docs, vecs, sums_c,
    ig_o, gkv_o, gt_o, small_o,
    w4, ins, f5, gm, xb, gb, gkvr, delta, grads, split, pack, tables, sums, nxt, small_cut, *scratch,
):
    kept, second_step, third_step = scratch[:3]
    s_scratch = scratch[3:7]
    t_scratch = [scratch[7 + 4 * i : 11 + 4 * i] for i in range(4)]
    sems, send_sem, recv_sems = scratch[23:]
    place_of = Place()
    mp = place_of.mp
    row, pair = mp % 2, mp // 2
    load_kept = pltpu.make_async_copy(kept_any, kept, sems.at[8])
    load_kept.start()
    load_w = [
        pltpu.make_async_copy(wts.at[4], w4.at[3], sems.at[1]),
        pltpu.make_async_copy(wts.at[pl.ds(0, 3)], w4.at[pl.ds(0, 3)], sems.at[2]),
    ]
    tile_loads = {}
    for t in reversed(range(1024 // TILE)):
        r = pl.ds(t * TILE, TILE)
        tile_loads[t] = [
            pltpu.make_async_copy(gm_any.at[r], gm.at[r], sems.at[18 + 4 * t]),
            pltpu.make_async_copy(kvs.at[:, r], f5.at[:, r], sems.at[19 + 4 * t]),
            pltpu.make_async_copy(x_any.at[row, r], xb.at[r], sems.at[20 + 4 * t]),
            pltpu.make_async_copy(acts.at[6, r], delta.at[r], sems.at[21 + 4 * t]),
        ]
    load_ins = [pltpu.make_async_copy(acts.at[i], ins.at[i % 2], sems.at[4 + i]) for i in range(4)]
    for copy in load_w[:1] + tile_loads[3] + load_w[1:] + tile_loads[2] + tile_loads[1] + tile_loads[0] + load_ins[:2]:
        copy.start()
    greet([place_of.sib, place_of.xn, place_of.yn, place_of.across, place_of.pair])
    messages = Messages(send_sem, recv_sems)
    channel = Scatter(place_of, messages, None, None, kept, [None, second_step, third_step], gkv_o, ("xyj", "yxj"))
    vectors = Plane(place_of, messages, small_cut.at[0], *s_scratch, small_o.at[0])
    mixing = [Plane(place_of, messages, pack.at[i], *t_scratch[i], gt_o.at[i]) for i in range(4)]
    load_kept.wait()
    channel.send(1)
    rate = jnp.exp(vec(vecs, DECAY))
    fade = jnp.exp(-rate)
    place = wide(lax.broadcasted_iota(jnp.int32, (TILE, 1), 0) % SPAN)
    tables[0] = jnp.exp((64.0 - place) * rate)
    tables[1] = jnp.exp((place - 63.0) * rate)
    tables[2] = jnp.exp((place - 127.0) * rate)
    sums[...] = jnp.zeros_like(sums)
    nxt[...] = jnp.zeros_like(nxt)
    gain = vec(vecs, GAIN1)
    own_docs = row_of(docs, row)

    def tile(t):
        base = t * TILE
        r = pl.ds(base, TILE)
        for copy in tile_loads[t]:
            copy.wait()
        gb[r, :] = low(gm[r, :])
        if t == 3:
            load_w[0].wait()
        grads[0] = dot_nt(gb[r, :], w4[3])

        values, gate = f5[1, r, :], f5[2, r, :]
        bonus = jnp.exp(f5[0, r, :] + vec(vecs, FIRST))
        inverse = 1.0 / (f5[4, r, :] + bonus)
        mixed = (f5[3, r, :] + bonus * values) * inverse
        grad_mixed = grads[0] * gate
        gkvr[2, r, :] = low(grad_mixed * mixed * (1.0 - gate))
        grad_top = grad_mixed * inverse
        shrunk = grad_top * tables[0]
        halves(split.at[0], shrunk)
        halves(split.at[1], -shrunk * mixed)
        direct = bonus * grad_top
        own = direct * (values - mixed)
        grads[0] = direct
        grads[1] = own
        sums[0] += row_sums(own)
        grads[3] = grad_top
        edges = [grads[3, i * SPAN : i * SPAN + 1, :] for i in range(TILE // SPAN)]
        time = lax.broadcasted_iota(jnp.int32, (SPAN, SPAN), 0)
        source = lax.broadcasted_iota(jnp.int32, (SPAN, SPAN), 1)
        for i in reversed(range(TILE // SPAN)):
            block = t * (TILE // SPAN) + i
            same = cols[pl.ds(block * SPAN, SPAN), 0:1] == own_docs[:, block * SPAN : (block + 1) * SPAN]
            mask = jnp.where(same & (source > time), 1.0, 0.0).astype(jnp.bfloat16)
            mask = jnp.concatenate([mask, mask], axis=1)
            for k in range(2):
                grads[2 + k, pl.ds(i * SPAN, SPAN), :] = dot(mask, split[k, i])
        for i in reversed(range(TILE // SPAN)):
            begin = base + i * SPAN
            top_in, bottom_in = nxt[1:2, :], nxt[2:3, :]

            q, here = pl.ds(begin, SPAN), pl.ds(i * SPAN, SPAN)
            link = cols[q, 3:4] * tables[2, 0:SPAN, :]
            state_top = grads[2, here, :] * tables[1, 0:SPAN, :] + link * top_in
            state_bottom = grads[3, here, :] * tables[1, 0:SPAN, :] + link * bottom_in
            key_exp = jnp.exp(f5[0, q, :])
            gkvr[0, q, :] = low(grads[1, here, :] + key_exp * (state_top * f5[1, q, :] + state_bottom))
            gkvr[1, q, :] = low(grads[0, here, :] + key_exp * state_top)
            sums[1] += row_sums(state_top * f5[3, q, :] + state_bottom * f5[4, q, :])
            row_top, row_bottom = state_top[0:1], state_bottom[0:1]
            bonus = jnp.exp(f5[0, begin : begin + 1, :] + vec(vecs, FIRST))
            bottom = f5[4, begin : begin + 1, :] + bonus
            mixed = (f5[3, begin : begin + 1, :] + bonus * f5[1, begin : begin + 1, :]) / bottom
            nxt[1:2, :] = fade * row_top + edges[i]
            nxt[2:3, :] = fade * row_bottom - edges[i] * mixed
        if t == 3:
            load_w[1].wait()
        for j in range(3):
            grads[j] = dot_nt(gkvr[j, r, :], w4[j])

        def third(q, state):
            step = wide(delta[q, :])
            grad, whole = 0.0, 0.0
            for j in range(3):
                into = grads[j]
                sums[4 + j] += row_sums(into * step)
                grad += into * vec(vecs, MIX + j)
                whole += into
            back = (whole - grad) * cols[q, 1:2]
            grad = grad + sooner(back, state)
            scale = cols[q, 5:6]
            normal = (wide(xb[q, :]) - cols[q, 4:5]) * scale
            sums[2] += row_sums(grad * normal)
            sums[3] += row_sums(grad)
            xb[q, :] = low(gm[q, :] + norm_back(grad * gain, normal, scale))
            return back[0:1]

        nxt[0:1, :] = third(r, nxt[0:1, :])

    arrivals = []
    keeps = []
    for t in reversed(range(1024 // TILE)):
        tile(t)
        r = pl.ds(t * TILE, TILE)
        done = xb.at[r]
        arrivals.append(messages.send(done, ig_o.at[row, r], ig_o.at[1 - row, r], place_of.pair))
        keeps.append(pltpu.make_async_copy(done, ig_o.at[row, r], sems.at[14 + t]))
        keeps[-1].start()
        if t == 2:
            channel.add(1)

    def product(slot, right):
        load_ins[slot].wait()
        left = ins.at[slot % 2]
        def body(t, carry):
            c = pl.ds(pl.multiple_of(t * 384, 128), 384)
            f5[0, c, :] = dot_tn(left[:, c], right[...])
            return carry

        lax.fori_loop(0, 2, body, 0)

        def packed(dp, carry):
            for j in range(2):
                start = pl.multiple_of(96 * dp + 48 * pair + 24 * j, 8)
                piece = jnp.concatenate([f5[0, pl.ds(start, 24), :], jnp.zeros((8, 768), jnp.float32)], axis=0)
                pack[slot, j, dp // 4, (dp // 2) % 2, dp % 2] = low(piece)
            return carry

        lax.fori_loop(0, 8, packed, 0)
        if slot < 2:
            load_ins[slot + 2].start()
        mixing[slot].start()

    totals = [jnp.sum(sums[i], axis=0, keepdims=True) for i in range(7)]
    totals[1] = totals[1] * (-rate * fade)
    small = jnp.concatenate([sums_c[0:4, :]] + totals + [jnp.zeros((5, 768), jnp.float32)], axis=0)
    turned = pltpu.roll(small, (768 - 48 * pair) % 768, 1)
    for dp in range(8):
        for j in range(2):
            start = 96 * dp + 24 * j
            piece = turned if start == 0 else pltpu.roll(turned, 768 - start, 1)
            small_cut[0, j, dp // 4, (dp // 2) % 2, dp % 2] = piece[:, :128]
    vectors.start()
    product(0, gkvr.at[0])
    vectors.core()
    product(1, gkvr.at[1])
    mixing[0].core()
    product(2, gkvr.at[2])
    mixing[1].core()
    mixing[0].plane()
    vectors.plane()
    product(3, gb)
    mixing[2].core()
    mixing[1].plane()
    mixing[3].core()
    mixing[2].plane()
    channel.add(2)
    vectors.z()
    mixing[0].z()
    mixing[1].z()
    mixing[3].plane()
    mixing[2].z()
    mixing[3].z()
    for copy in keeps:
        copy.wait()
    for wait in arrivals:
        wait.wait_recv()
    messages.finish()


def time_back(wts, acts, kvs, gm, x, kept, cols, docs, vecs, sums_c):
    bf, f32 = jnp.bfloat16, jnp.float32
    shape = jax.ShapeDtypeStruct
    return pl.pallas_call(
        time_back_kernel,
        out_shape=(
            shape((2, 1024, 768), bf), shape((1, 224, 768), f32), shape((4, 32, 768), f32), shape((1, 16, 128), f32),
        ),
        in_specs=[ANY] * 6 + [ON_CORE] * 4,
        out_specs=[ANY] + [ON_CORE] * 3,
        scratch_shapes=[
            pltpu.VMEM((4, 768, 768), bf), pltpu.VMEM((2, 1024, 768), bf), pltpu.VMEM((5, 1024, 768), f32),
            pltpu.VMEM((1024, 768), f32), pltpu.VMEM((1024, 768), bf), pltpu.VMEM((1024, 768), bf),
            pltpu.VMEM((3, 1024, 768), bf), pltpu.VMEM((1024, 768), bf), pltpu.VMEM((4, TILE, 768), f32),
            pltpu.VMEM((2, 2, 2 * SPAN, 768), bf),
            pltpu.VMEM((4, 2, 2, 2, 2, 32, 768), bf), pltpu.VMEM((3, TILE, 768), f32), pltpu.VMEM((7, 8, 768), f32),
            pltpu.VMEM((8, 768), f32), pltpu.VMEM((1, 2, 2, 2, 2, 16, 128), f32),
        ]
        + [pltpu.VMEM((1, 2, 2, 2, 224, 768), bf), pltpu.VMEM((2, 1, 2, 224, 384), bf), pltpu.VMEM((2, 1, 224, 384), bf)]
        + plane_scratch(16, 128, f32)
        + plane_scratch(32, 768, bf) * 4
        + [pltpu.SemaphoreType.DMA((34,)), pltpu.SemaphoreType.DMA, pltpu.SemaphoreType.DMA((36,))],
        compiler_params=pltpu.CompilerParams(vmem_limit_bytes=LIMIT, collective_id=2, has_side_effects=True),
        name="time_back",
    )(wts, acts, kvs, gm, x, kept, cols, docs, vecs, sums_c)


def results_kernel(
    out_any, ig_any, gkv_any, gt_any, small,
    out_o, ig_o, gain1, bias1, gain2, bias2, mix, blend_o, decay, first, grad_mix, grad_out, grad_key, grad_value,
    rows, halves_in, halves_out, gkv, gt, sems,
):
    cut = 256
    parts = [(i, pl.ds(j * cut, cut)) for i in range(2) for j in range(1024 // cut)]
    loads = [pltpu.make_async_copy(ig_any.at[i, r], halves_in.at[i, r], sems.at[n]) for n, (i, r) in enumerate(parts)]
    load_out = [pltpu.make_async_copy(out_any.at[i], rows.at[i], sems.at[16 + i]) for i in range(2)]
    load_w = [pltpu.make_async_copy(gkv_any, gkv, sems.at[18]), pltpu.make_async_copy(gt_any, gt, sems.at[19])]
    for copy in loads[:4] + load_w + loads[4:] + load_out:
        copy.start()
    for ref, slot in ((gain2, 0), (bias2, 1), (first, 4), (decay, 5), (gain1, 6), (bias1, 7)):
        ref[...] = small[0, slot, 0:24]
    blend_o[...] = small[0, 2:4, 0:24]
    mix[...] = small[0, 8:11, 0:24]
    stores = []

    def store(source, target):
        copy = pltpu.make_async_copy(source, target, sems.at[20 + len(stores)])
        copy.start()
        stores.append(copy)

    for n, (i, r) in enumerate(parts):
        loads[n].wait()
        halves_out[i, r, :] = wide(halves_in[i, r, :])
        store(halves_out.at[i, r], ig_o.at[i, r])
        if n == 3:
            for copy in load_w:
                copy.wait()
            store(gt.at[pl.ds(0, 3), pl.ds(0, 24)], grad_mix.at[pl.ds(0, 3)])
            store(gkv.at[0, pl.ds(192, 24)], grad_mix.at[3])
            store(gt.at[3, pl.ds(0, 24)], grad_out)
            store(gkv.at[0, pl.ds(0, 96)], grad_key)
            store(gkv.at[0, pl.ds(96, 96)], grad_value)
    for i in range(2):
        load_out[i].wait()
        store(rows.at[i], out_o.at[i])
    for copy in stores:
        copy.wait()


def results(out, ig, gkv, gt, small):
    bf, f32 = jnp.bfloat16, jnp.float32
    shape = jax.ShapeDtypeStruct
    vector = shape((24,), f32)
    return pl.pallas_call(
        results_kernel,
        out_shape=(
            shape((2, 1024, 768), bf), shape((2, 1024, 768), f32), vector, vector, vector, vector,
            shape((3, 24), f32), shape((2, 24), f32), vector, vector,
            shape((4, 24, 768), f32), shape((24, 768), f32), shape((96, 768), f32), shape((96, 768), f32),
        ),
        in_specs=[ANY] * 4 + [ON_CORE],
        out_specs=[ANY] * 2 + [ON_CORE] * 8 + [ANY] * 4,
        scratch_shapes=[
            pltpu.VMEM((2, 1024, 768), bf), pltpu.VMEM((2, 1024, 768), bf), pltpu.VMEM((2, 1024, 768), f32),
            pltpu.VMEM((1, 224, 768), f32), pltpu.VMEM((4, 32, 768), f32), pltpu.SemaphoreType.DMA((40,)),
        ],
        compiler_params=pltpu.CompilerParams(vmem_limit_bytes=LIMIT),
        name="results",
    )(out, ig, gkv, gt, small)


def on_device(
    residual_input, article_numbers, upstream_gradient,
    prenorm_scaling, prenorm_offset, postnorm_scaling, postnorm_offset,
    attention_blend, feedforward_blend, forgetting_logrates, present_reward,
    projection_matrices, final_matrix, address_matrix, content_matrix,
):
    vectors = jnp.concatenate(
        [
            prenorm_scaling[None], prenorm_offset[None], postnorm_scaling[None], postnorm_offset[None],
            attention_blend, forgetting_logrates[None], present_reward[None], feedforward_blend,
        ],
        axis=0,
    )
    vectors = jnp.pad(vectors, ((0, 5), (0, 104)))
    kg, vg, acts, kvs, middle, sq, act, grads, out_row, wts, vecs, cols = forward(
        projection_matrices, final_matrix, vectors, address_matrix, content_matrix.T, article_numbers,
        residual_input, upstream_gradient,
    )
    kg, vg, sq = kg.reshape(4, 768, 768), vg.reshape(4, 768, 768), sq.reshape(4, 8, 128, 768)
    gm, kept, output, sums_c = channel_back(
        kg, vg, wts, acts, sq, act, grads, middle, upstream_gradient, out_row, cols, vecs
    )
    input_grad, gkv, gt, small = time_back(
        wts, acts, kvs, gm, residual_input, kept, cols, article_numbers, vecs, sums_c
    )
    *others, grad_value = results(output, input_grad, gkv, gt, small)
    return (*others, grad_value.T)


def fits(mesh):
    return dict(mesh.shape) == {"dp": 8, "mp": 4}


def solution(mesh):
    return jax.shard_map(
        on_device if fits(mesh) else general_device,
        mesh=mesh,
        in_specs=(
            P("dp", None, None),
            P("dp", None),
            P("dp", None, None),
            P(("dp", "mp")),
            P(("dp", "mp")),
            P(("dp", "mp")),
            P(("dp", "mp")),
            P(None, ("dp", "mp")),
            P(None, ("dp", "mp")),
            P(("dp", "mp")),
            P(("dp", "mp")),
            P(None, ("dp", "mp"), None),
            P(("dp", "mp"), None),
            P("dp", "mp"),
            P("mp", "dp"),
        ),
        out_specs=(
            P("dp", None, None),
            P("dp", None, None),
            P(("dp", "mp")),
            P(("dp", "mp")),
            P(("dp", "mp")),
            P(("dp", "mp")),
            P(None, ("dp", "mp")),
            P(None, ("dp", "mp")),
            P(("dp", "mp")),
            P(("dp", "mp")),
            P(None, ("dp", "mp"), None),
            P(("dp", "mp"), None),
            P("dp", "mp"),
            P("mp", "dp"),
        ),
        check_vma=False,
    )
```

```python
import functools

import jax
import jax.numpy as jnp
from jax import lax
from jax.experimental import pallas as pl
from jax.experimental.pallas import tpu as pltpu
from jax.sharding import PartitionSpec as P

BLOCK = 64
MICRO = 2


epsilon = 1e-05


def layer_norm(values_in, gain_vec, bias_vec):
    average = jnp.mean(values_in, axis=-1, keepdims=True)
    centered = values_in - average
    variance = jnp.mean(centered * centered, axis=-1, keepdims=True)
    return centered * lax.rsqrt(variance + epsilon) * gain_vec + bias_vec


def shifted(values_in, retain_marker):
    earlier = jnp.concatenate([jnp.zeros_like(values_in[:, :1]), values_in[:, :-1]], axis=1)
    return earlier * retain_marker[:, :, None]


def blend(normed, earlier, factor):
    return normed * factor + earlier * (1.0 - factor)


def project(operand, weights):
    return lax.dot_general(
        operand, weights, (((2,), (0,)), ((), ())), preferred_element_type=jnp.float32
    )


def back_project(gradient, weights):
    return lax.dot_general(
        gradient, weights, (((2,), (1,)), ((), ())), preferred_element_type=jnp.float32
    )


def weight_grad(operand, gradient):
    return lax.dot_general(
        operand, gradient, (((0, 1), (0, 1)), ((), ())), preferred_element_type=jnp.float32
    )


def take_share(array, axis_at, groups, shares, place):
    shape = array.shape
    piece_len = shape[axis_at] // (groups * shares)
    split_shape = shape[:axis_at] + (groups, shares, piece_len) + shape[axis_at + 1 :]
    chosen = lax.dynamic_index_in_dim(
        array.reshape(split_shape), place, axis_at + 1, keepdims=False
    )
    return chosen.reshape(shape[:axis_at] + (groups * piece_len,) + shape[axis_at + 1 :])


def first_piece(stream_f, gain_vec, bias_vec, factors, retain_marker):
    normed = layer_norm(stream_f, gain_vec, bias_vec)
    earlier = shifted(normed, retain_marker)
    return (
        blend(normed, earlier, factors[0]),
        blend(normed, earlier, factors[1]),
        blend(normed, earlier, factors[2]),
    )


def channel_piece(middle, gain_vec, bias_vec, factors, retain_marker):
    normed = layer_norm(middle, gain_vec, bias_vec)
    earlier = shifted(normed, retain_marker)
    return (blend(normed, earlier, factors[0]), blend(normed, earlier, factors[1]))


def time_piece(
    address_series,
    content_series,
    acceptance_gate,
    forgetting_logrates,
    present_reward,
    retain_marker,
    article_labels,
    span_length,
):
    batch_rows, length, feature_count = address_series.shape
    block_count = length // span_length
    decay_rate = jnp.exp(forgetting_logrates)
    position = jnp.arange(span_length, dtype=jnp.float32)[:, None]
    rising = jnp.exp(position * decay_rate)
    sinking = jnp.exp(-position * decay_rate)
    falling = jnp.exp(-(position + 1.0) * decay_rate)
    rising = jnp.concatenate([rising, rising], axis=-1)
    sinking = jnp.concatenate([sinking, sinking], axis=-1)
    falling = jnp.concatenate([falling, falling], axis=-1)
    whole_fade = jnp.exp(-span_length * decay_rate)
    whole_fade = jnp.concatenate([whole_fade, whole_fade], axis=-1)
    key_exp = jnp.exp(address_series)
    weighted = jnp.concatenate([key_exp * content_series, key_exp], axis=-1)
    weighted = weighted.reshape(batch_rows, block_count, span_length, 2 * feature_count)
    block_docs = article_labels.reshape(batch_rows, block_count, span_length)
    causal = jnp.arange(span_length)[:, None] >= jnp.arange(span_length)[None, :]
    same_doc = block_docs[:, :, :, None] == block_docs[:, :, None, :]
    doc_mask = (causal[None, None] & same_doc).astype(jnp.float32)
    partial_value = (
        jnp.einsum("rnji,rnid->rnjd", doc_mask, weighted * rising, precision=lax.Precision.HIGHEST)
        * sinking
    )
    last_docs = block_docs[:, :, -1]
    prior_docs = jnp.concatenate(
        [jnp.full((batch_rows, 1), -1, jnp.int32), last_docs[:, :-1]], axis=1
    )
    linked = (block_docs == prior_docs[:, :, None]).astype(jnp.float32)
    chained = linked[:, :, -1]

    def carry_step(state, pieces):
        tail_state, joined = pieces
        return (tail_state + whole_fade * joined[:, None] * state, state)

    zero_state = jnp.zeros((batch_rows, 2 * feature_count), jnp.float32)
    _, starts = lax.scan(
        carry_step,
        zero_state,
        (jnp.swapaxes(partial_value[:, :, -1], 0, 1), jnp.swapaxes(chained, 0, 1)),
    )
    starts = jnp.swapaxes(starts, 0, 1)
    states = partial_value + falling * linked[..., None] * starts[:, :, None, :]
    states = states.reshape(batch_rows, length, 2 * feature_count)
    entering_memory = shifted(states, retain_marker)
    reward_power = jnp.exp(present_reward + address_series)
    accumulated_dividend = entering_memory[..., :feature_count] + reward_power * content_series
    accumulated_divisor = entering_memory[..., feature_count:] + reward_power
    return jax.nn.sigmoid(acceptance_gate) * (accumulated_dividend / accumulated_divisor)


def general_device(
    residual_input,
    article_numbers,
    upstream_gradient,
    prenorm_scaling,
    prenorm_offset,
    postnorm_scaling,
    postnorm_offset,
    attention_blend,
    feedforward_blend,
    forgetting_logrates,
    present_reward,
    projection_matrices,
    final_matrix,
    address_matrix,
    content_matrix,
):
    batch_rows = residual_input.shape[0] // MICRO
    same_doc = article_numbers[:, 1:] == article_numbers[:, :-1]
    keep_all = jnp.concatenate([jnp.zeros_like(same_doc[:, :1]), same_doc], axis=1).astype(
        jnp.float32
    )
    groups = lax.axis_size("dp")
    shares = lax.axis_size("mp")
    mp_place = lax.axis_index("mp")
    totals = None
    outputs = []
    input_grads = []
    for micro_index in range(MICRO):
        shared = (
            lax.all_gather(prenorm_scaling, ("dp", "mp"), axis=0, tiled=True),
            lax.all_gather(prenorm_offset, ("dp", "mp"), axis=0, tiled=True),
            lax.all_gather(postnorm_scaling, ("dp", "mp"), axis=0, tiled=True),
            lax.all_gather(postnorm_offset, ("dp", "mp"), axis=0, tiled=True),
            lax.all_gather(attention_blend, ("dp", "mp"), axis=1, tiled=True),
            lax.all_gather(feedforward_blend, ("dp", "mp"), axis=1, tiled=True),
            lax.all_gather(forgetting_logrates, ("dp", "mp"), axis=0, tiled=True),
            lax.all_gather(present_reward, ("dp", "mp"), axis=0, tiled=True),
            lax.all_gather(projection_matrices, ("dp", "mp"), axis=1, tiled=True),
            lax.all_gather(final_matrix, ("dp", "mp"), axis=0, tiled=True),
        )
        local = (
            lax.all_gather(address_matrix, "dp", axis=0, tiled=True),
            lax.all_gather(content_matrix, "dp", axis=1, tiled=True),
        )
        fetched = (shared, local)
        shared, local = fetched
        gain_one, bias_one, gain_two, bias_two, tmix_w, cmix_w, decay_w, first_w, mix_w, out_w = (
            shared
        )
        key_w, value_w = local
        mix_part = take_share(mix_w[0:3], 2, groups, shares, mp_place)
        out_part = take_share(out_w, 0, groups, shares, mp_place)
        decay_part = take_share(decay_w, 0, groups, shares, mp_place)
        first_part = take_share(first_w, 0, groups, shares, mp_place)
        lower_row = micro_index * batch_rows
        upper_row = lower_row + batch_rows
        stream_f = residual_input[lower_row:upper_row].astype(jnp.float32)
        retain_marker = keep_all[lower_row:upper_row]
        article_labels = article_numbers[lower_row:upper_row]
        grad_out = upstream_gradient[lower_row:upper_row].astype(jnp.float32)

        def first_local(values_in, gain_vec, bias_vec, factors):
            return first_piece(values_in, gain_vec, bias_vec, factors, retain_marker)

        def time_local(address_series, content_series, acceptance_gate, decay_vec, first_vec):
            return time_piece(
                address_series,
                content_series,
                acceptance_gate,
                decay_vec,
                first_vec,
                retain_marker,
                article_labels,
                BLOCK,
            )

        def channel_local(values_in, gain_vec, bias_vec, factors):
            return channel_piece(values_in, gain_vec, bias_vec, factors, retain_marker)

        mixes, pull_first = jax.vjp(
            first_local,
            stream_f,
            gain_one.astype(jnp.float32),
            bias_one.astype(jnp.float32),
            tmix_w.astype(jnp.float32),
        )
        key_in = mixes[0].astype(jnp.bfloat16)
        value_in = mixes[1].astype(jnp.bfloat16)
        rec_in = mixes[2].astype(jnp.bfloat16)
        address_series = project(key_in, mix_part[0])
        content_series = project(value_in, mix_part[1])
        acceptance_gate = project(rec_in, mix_part[2])
        gated, pull_time = jax.vjp(
            time_local,
            address_series,
            content_series,
            acceptance_gate,
            decay_part.astype(jnp.float32),
            first_part.astype(jnp.float32),
        )
        gated_low = gated.astype(jnp.bfloat16)
        branch = project(gated_low, out_part)
        branch = lax.psum(branch, "mp")
        middle = stream_f + branch
        channel_ins, pull_channel = jax.vjp(
            channel_local,
            middle,
            gain_two.astype(jnp.float32),
            bias_two.astype(jnp.float32),
            cmix_w.astype(jnp.float32),
        )
        ckey_in = channel_ins[0].astype(jnp.bfloat16)
        crec_in = channel_ins[1].astype(jnp.bfloat16)
        hidden = project(ckey_in, key_w)
        active = jax.nn.relu(hidden)
        squared = (active * active).astype(jnp.bfloat16)
        carried = lax.psum(project(squared, value_w).astype(jnp.bfloat16), "mp").astype(jnp.float32)
        gate_sig = jax.nn.sigmoid(project(crec_in, mix_w[3]))
        outputs.append((middle + gate_sig * carried).astype(jnp.bfloat16))
        grad_carried = (grad_out * gate_sig).astype(jnp.bfloat16)
        grad_gate = (grad_out * carried * gate_sig * (1.0 - gate_sig)).astype(jnp.bfloat16)
        grad_value_w = weight_grad(squared, grad_carried)
        grad_hidden = (back_project(grad_carried, value_w) * 2.0 * active).astype(jnp.bfloat16)
        grad_key_w = weight_grad(ckey_in, grad_hidden)
        grad_crec_w = weight_grad(crec_in, grad_gate)
        grad_ckey = lax.psum(back_project(grad_hidden, key_w).astype(jnp.bfloat16), "mp").astype(
            jnp.float32
        )
        grad_crec = back_project(grad_gate, mix_w[3])
        grad_middle, grad_gain_two, grad_bias_two, grad_cmix = pull_channel((grad_ckey, grad_crec))
        grad_middle = grad_middle + grad_out
        grad_branch = grad_middle.astype(jnp.bfloat16)
        grad_out_w = weight_grad(gated_low, grad_branch)
        grad_gated = back_project(grad_branch, out_part)
        grad_keys, grad_values, grad_recept, grad_decay, grad_first = pull_time(grad_gated)
        grad_keys = grad_keys.astype(jnp.bfloat16)
        grad_values = grad_values.astype(jnp.bfloat16)
        grad_recept = grad_recept.astype(jnp.bfloat16)
        grad_mix_three = jnp.stack(
            [
                weight_grad(key_in, grad_keys),
                weight_grad(value_in, grad_values),
                weight_grad(rec_in, grad_recept),
            ]
        )
        grad_ins = (
            back_project(grad_keys, mix_part[0]),
            back_project(grad_values, mix_part[1]),
            back_project(grad_recept, mix_part[2]),
        )
        pulled = pull_first(grad_ins)
        pulled = (
            lax.psum(pulled[0].astype(jnp.bfloat16), "mp").astype(jnp.float32),
            lax.psum(pulled[1].astype(jnp.bfloat16), "mp").astype(jnp.float32),
            lax.psum(pulled[2].astype(jnp.bfloat16), "mp").astype(jnp.float32),
            lax.psum(pulled[3].astype(jnp.bfloat16), "mp").astype(jnp.float32),
        )
        grad_stream, grad_gain_one, grad_bias_one, grad_tmix = pulled
        input_grads.append(grad_stream + grad_middle)
        current = [
            grad_gain_one,
            grad_bias_one,
            grad_gain_two,
            grad_bias_two,
            grad_tmix,
            grad_cmix,
            grad_decay,
            grad_first,
            grad_mix_three,
            grad_crec_w,
            grad_out_w,
            grad_key_w,
            grad_value_w,
        ]
        totals = (
            current
            if totals is None
            else [earlier + latest for earlier, latest in zip(totals, current)]
        )

    def pick(gradient, axis_at):
        return take_share(gradient, axis_at, groups, shares, mp_place)

    split_grads = (
        lax.psum_scatter(pick(totals[0], 0), "dp", scatter_dimension=0, tiled=True),
        lax.psum_scatter(pick(totals[1], 0), "dp", scatter_dimension=0, tiled=True),
        lax.psum_scatter(pick(totals[2], 0), "dp", scatter_dimension=0, tiled=True),
        lax.psum_scatter(pick(totals[3], 0), "dp", scatter_dimension=0, tiled=True),
        lax.psum_scatter(pick(totals[4], 1), "dp", scatter_dimension=1, tiled=True),
        lax.psum_scatter(pick(totals[5], 1), "dp", scatter_dimension=1, tiled=True),
        lax.psum_scatter(totals[6], "dp", scatter_dimension=0, tiled=True),
        lax.psum_scatter(totals[7], "dp", scatter_dimension=0, tiled=True),
        lax.psum_scatter(totals[10], "dp", scatter_dimension=0, tiled=True),
    )
    feature_count = totals[9].shape[0]
    share_mask = jax.nn.one_hot(mp_place, shares, dtype=jnp.float32)
    three_full = (
        totals[8].reshape(3, feature_count, groups, 1, feature_count // (groups * shares))
        * share_mask[None, None, None, :, None]
    )
    three_full = three_full.reshape(3, feature_count, feature_count)
    crec_grad = totals[9] * (mp_place == 0).astype(jnp.float32)
    mix_grad = lax.psum_scatter(
        jnp.concatenate([three_full, crec_grad[None]], axis=0),
        ("dp", "mp"),
        scatter_dimension=1,
        tiled=True,
    )
    shared_grads = (
        split_grads[0],
        split_grads[1],
        split_grads[2],
        split_grads[3],
        split_grads[4],
        split_grads[5],
        split_grads[6],
        split_grads[7],
        mix_grad,
        split_grads[8],
    )
    channel_grads = (
        lax.psum_scatter(totals[11], "dp", scatter_dimension=0, tiled=True),
        lax.psum_scatter(totals[12], "dp", scatter_dimension=1, tiled=True),
    )
    output = jnp.concatenate(outputs, axis=0)
    input_grad = jnp.concatenate(input_grads, axis=0)
    return (
        output,
        input_grad,
        shared_grads[0],
        shared_grads[1],
        shared_grads[2],
        shared_grads[3],
        shared_grads[4],
        shared_grads[5],
        shared_grads[6],
        shared_grads[7],
        shared_grads[8],
        shared_grads[9],
        channel_grads[0],
        channel_grads[1],
    )


MESH = pl.DeviceIdType.MESH
MIB = 2**20

class Place:
    def __init__(self):
        self.dp = lax.axis_index("dp")
        self.mp = lax.axis_index("mp")
        self.core = self.dp % 2
        self.x = (self.dp // 2) % 2
        self.y = self.dp // 4
        self.sib = (self.dp + 1 - 2 * self.core, self.mp)
        self.xn = (self.dp + 2 - 4 * self.x, self.mp)
        self.yn = (self.dp + 4 - 8 * self.y, self.mp)
        self.up_z = (self.mp + 1) % 4
        self.down_z = (self.mp + 3) % 4
        self.far_z = (self.mp + 2) % 4
        self.up = (self.dp, self.up_z)
        self.down = (self.dp, self.down_z)
        self.pair = (self.dp, self.mp + 1 - 2 * (self.mp % 2))
        self.across = (self.dp + 6 - 4 * self.x - 8 * self.y, self.mp)


def greet(devices):
    barrier = pltpu.get_barrier_semaphore()
    for device in devices:
        pl.semaphore_signal(barrier, inc=1, device_id=device, device_id_type=MESH)
    pl.semaphore_wait(barrier, len(devices))


class Messages:
    def __init__(self, send_sem, recv_sems):
        self.send_sem, self.recv_sems, self.count, self.sent = send_sem, recv_sems, 0, []

    def send(self, source, target, arrival, device, when=None):
        index = self.count
        self.count += 1
        copy = pltpu.make_async_remote_copy(source, target, self.send_sem, self.recv_sems.at[index], device_id=device, device_id_type=MESH)
        only(when, copy.start)
        self.sent.append((when, copy))
        return pltpu.make_async_remote_copy(arrival, arrival, self.send_sem, self.recv_sems.at[index], device_id=device, device_id_type=MESH)

    def finish(self):
        for when, copy in self.sent:
            only(when, copy.wait_send)
        self.sent = []


def only(when, action):
    if when is None:
        action()
    else:
        pl.when(when)(action)


ALL = slice(None)


class Stream:
    def __init__(self, place, messages, order, piece, own, twin_sem):
        self.p, self.msg, self.order, self.piece, self.own, self.twin_sem = place, messages, order, piece, own, twin_sem
        p = place
        self.first = order.replace("z", "")[0]
        self.z_leads = order[0] == "z"
        self.a, self.b = (p.x, p.y) if self.first == "x" else (p.y, p.x)
        self.na, self.nb = (p.xn, p.yn) if self.first == "x" else (p.yn, p.xn)
        self.base = messages.count
        messages.count += 15

    def at(self, col, other, slab, core=None):
        a = self.a if col == 0 else 1 - self.a
        b = 1 - self.b if other else self.b
        y, x = (b, a) if self.first == "x" else (a, b)
        return self.piece(y, x, self.p.core if core is None else core, slab)

    def slab(self, j):
        m = self.p.mp
        if j == 0:
            return m
        flip = (m >= 2).astype(jnp.int32)
        near = m + flip * (3 - 2 * m)
        picked = j - (j <= near).astype(jnp.int32)
        return picked + flip * (3 - 2 * picked)

    def rank(self, m, slab):
        flip = (m >= 2).astype(jnp.int32)
        near = m + flip * (3 - 2 * m)
        picked = slab + flip * (3 - 2 * slab)
        return picked - (picked > near).astype(jnp.int32) + 1

    def index(self, kind, col, j):
        if self.z_leads:
            return self.base + {"z": j - 1, "a": 3 + j, "b": 7 + 4 * col + j}[kind]
        return self.base + {"z": 3 * col + j - 1, "a": 6, "b": 7 + 4 * col + j}[kind]

    def copy(self, piece, index, device, when=None, source=None):
        copy = pltpu.make_async_remote_copy(
            piece if source is None else source, piece, self.msg.send_sem, self.msg.recv_sems.at[index],
            device_id=device, device_id_type=MESH,
        )
        only(when, copy.start)
        self.msg.sent.append((when, copy))

    def twin(self, col, other, slab, source=None):
        piece = self.at(col, other, slab)
        sem = self.twin_sem(slab)
        copy = pltpu.make_async_remote_copy(
            piece if source is None else source, piece, self.msg.send_sem, sem,
            device_id=self.p.sib, device_id_type=MESH,
        )
        copy.start()
        self.msg.sent.append((None, copy))

    def send_z(self, col, j, source=None):
        m = self.p.mp
        slab = self.slab(j)
        piece = self.at(col, 0, slab)
        if j == 0:
            self.copy(piece, self.index("z", col, 1) + self.rank(m + 1, slab) - 1, self.p.up, m < 3, source)
            self.copy(piece, self.index("z", col, 1) + self.rank(m - 1, slab) - 1, self.p.down, m > 0, source)
            return
        target = m - 1 + 2 * (slab < m).astype(jnp.int32)
        safe = (target + 4) % 4
        self.copy(piece, self.index("z", col, 1) + self.rank(target, slab) - 1, (self.p.dp, safe), (target >= 0) & (target <= 3))

    def send_a(self, j, source=None):
        self.copy(self.at(0, 0, self.slab(j)), self.index("a", 0, j), self.na, source=source)

    def send_b(self, col, j, source=None):
        self.copy(self.at(col, 0, self.slab(j)), self.index("b", col, j), self.nb, source=source)

    def event(self, kind, col, j):
        if kind == "o":
            self.send_z(0, 0, self.own)
            self.send_a(0, self.own)
            self.send_b(0, 0, self.own)
            self.twin(0, 0, self.p.mp, self.own)
            return
        slab = self.slab(j)
        piece = self.at(1 if kind == "a" else col, kind == "b", slab)
        sem = self.msg.recv_sems.at[self.index(kind, col, j)]
        pltpu.make_async_remote_copy(piece, piece, self.msg.send_sem, sem, device_id=self.na, device_id_type=MESH).wait_recv()
        if kind == "z":
            self.send_z(col, j)
            if self.z_leads:
                self.send_a(j)
            self.send_b(col, j)
            self.twin(col, 0, slab)
        elif kind == "a":
            if not self.z_leads:
                self.send_z(1, 0)
            self.send_b(1, j)
            self.twin(1, 0, slab)
        else:
            self.twin(col, 1, slab)


PARTS = (
    ("t", 0, 48, "zxy"),
    ("t", 48, 32, "zyx"),
    ("t", 80, 48, "xzy"),
    ("k", 0, 96, "yzx"),
    ("v", 0, 96, "zxy"),
)
EVENTS = {
    "own": ("0o00", "1o00", "2o00", ),
    "relayA": ("0z01", "3o00", "1b00", "1z01", "1a00", "0a01", "0z02", "0z03", "1z02", "0b01", "1z03", "3a00", "0b11", "0a02", "0a03", "2a00", "1b02", "1a01", "0a00", "2z01", "0b00", "0b03", "1b01", "1a02", "1a03", "4o00", "3z12", "0b12", "2b00", "1b10", "2z11", "1b12", "1b11", "0b02", "3b10", "3b00", "0b10", "0b13", "2z03", "4z01", "1b13", "1b03", "3z11", "2z12", ),
    "a0.0": ("2z13", ),
    "a0.1": ("3z01", "2z02", ),
    "a0.2": (),
    "a1.0": ("4z03", ),
    "a1.1": (),
    "a1.2": (),
    "a2.0": ("4b00", "4a01", "4z02", "2b10", ),
    "a2.1": ("2b11", ),
    "a2.2": ("2b12", ),
    "a3.0": ("3z13", ),
    "a3.1": (),
    "a3.2": ("2b01", "4b01", ),
    "relayB": ("4a00", "3b11", "3z02", "2b03", "2b13", "3b12", "2b02", ),
    "b0.0": (),
    "b0.1": ("3z03", ),
    "b1.0": (),
    "b1.1": ("4a02", "4b11", "4b02", ),
    "b2.0": (),
    "b2.1": ("4b10", ),
    "b3.0": ("4a03", "4b03", ),
    "b3.1": ("3b02", "3b01", "3b13", ),
    "h0": ("3b03", ),
    "h1": (),
    "h2": ("4b12", ),
    "h3": (),
    "c0": (),
    "c1": ("4b13", ),
    "c2": (),
    "c3": (),
    "fin": (),
    "end": (),
}


def streams(place, messages, twin_sems, pk, kw, vt, tw, kg, vg):
    def piece_of(name, start, rows):
        if name == "t":
            return lambda y, x, c, m: tw.at[y, x, c, m, pl.ds(start, rows)]
        array = kg if name == "k" else vg
        return lambda y, x, c, m: array.at[m, y, x, c, pl.ds(start, rows)]

    made = []
    for name, start, rows, order in PARTS:
        own = {"t": pk, "k": kw, "v": vt}[name].at[pl.ds(start, rows)]
        if name == "t":
            twin = lambda slab, i=start // 80: twin_sems.at[i]
        else:
            twin = lambda slab, i=2 if name == "k" else 6: twin_sems.at[i + slab]
        made.append(Stream(place, messages, order, piece_of(name, start, rows), own, twin))
    return made


def play(made, marker):
    for event in EVENTS[marker]:
        made[int(event[0])].event(event[1], int(event[2]), int(event[3]))


def greet_all(p):
    barrier = pltpu.get_barrier_semaphore()
    for device in (p.sib, p.xn, p.yn):
        pl.semaphore_signal(barrier, inc=1, device_id=device, device_id_type=MESH)
    only(p.mp < 3, lambda: pl.semaphore_signal(barrier, inc=1, device_id=p.up, device_id_type=MESH))
    only(p.mp > 0, lambda: pl.semaphore_signal(barrier, inc=1, device_id=p.down, device_id_type=MESH))
    pl.semaphore_wait(barrier, 3 + (p.mp < 3).astype(jnp.int32) + (p.mp > 0).astype(jnp.int32))


TILE = 256
SPAN = 128
WIDE = 512


def dot(a, b):
    return jnp.dot(a, b, preferred_element_type=jnp.float32)


def dot_nt(a, b):
    return lax.dot_general(a, b, (((1,), (1,)), ((), ())), preferred_element_type=jnp.float32)


def dot_tn(a, b):
    return lax.dot_general(a, b, (((0,), (0,)), ((), ())), preferred_element_type=jnp.float32)


def low(values):
    return values.astype(jnp.bfloat16)


def wide(values):
    return values.astype(jnp.float32)


def row_sums(values):
    rows, width = values.shape
    return jnp.sum(values.reshape(rows // 8, 8, width), axis=0)


def standardise(values):
    centered = values - jnp.mean(values, axis=-1, keepdims=True)
    variance = jnp.mean(centered * centered, axis=-1, keepdims=True)
    scale = lax.rsqrt(variance + epsilon)
    return centered * scale, scale


def norm_back(grad, normal, scale):
    mean_grad = jnp.mean(grad, axis=-1, keepdims=True)
    mean_both = jnp.mean(grad * normal, axis=-1, keepdims=True)
    return scale * (grad - mean_grad - normal * mean_both)


def later(values, first_row):
    row = lax.broadcasted_iota(jnp.int32, values.shape, 0)
    return jnp.where(row == 0, first_row, pltpu.roll(values, 1, 0))


def sooner(values, last_row):
    rows = values.shape[0]
    row = lax.broadcasted_iota(jnp.int32, values.shape, 0)
    return jnp.where(row == rows - 1, last_row, pltpu.roll(values, rows - 1, 0))


def halves(target, values):
    for span in range(values.shape[0] // SPAN):
        part = values[span * SPAN : (span + 1) * SPAN]
        high = low(part)
        target[span, 0:SPAN, :] = high
        target[span, SPAN : 2 * SPAN, :] = low(part - wide(high))


GAIN1, BIAS1, GAIN2, BIAS2, MIX, DECAY, FIRST, BLEND = 0, 1, 2, 3, 4, 7, 8, 9


def vec(ref, index):
    return ref[index : index + 1, :]


def rows_at(start, count):
    return pl.ds(pl.multiple_of(start, 128), count)


def pack_block(p, proj, final, vectors, pk):
    spread = jnp.concatenate([wide(vectors[...]), jnp.zeros((16, 256), jnp.float32)], axis=1)
    spread = pltpu.roll(spread, 24 * ((4 * p.dp + p.mp) % 16), 1)
    spread = jnp.concatenate([spread[:8], spread[8:]], axis=1)
    rows = [wide(proj[0]), wide(proj[1]), wide(proj[2]), spread, wide(proj[3]), wide(final[...])]
    pk[...] = low(jnp.concatenate(rows, axis=0))


def row_of(docs, row):
    return wide(jnp.where(row == 0, docs[0:1, :], docs[1:2, :]))


def describe(docs, row, cols):
    own = row_of(docs, row)
    lane = lax.broadcasted_iota(jnp.int32, own.shape, 1)
    keep = jnp.where((lane > 0) & (own == pltpu.roll(own, 1, 1)), 1.0, 0.0)
    spans = own.shape[1] // SPAN
    none = jnp.zeros((1, SPAN), jnp.float32)
    for i in range(spans):
        part = own[:, i * SPAN : (i + 1) * SPAN]
        before = after = none
        if i > 0:
            before = jnp.where(part == own[:, i * SPAN - 1 : i * SPAN], 1.0, 0.0)
        if i < spans - 1:
            after = jnp.where(part == own[:, (i + 1) * SPAN : (i + 1) * SPAN + 1], 1.0, 0.0)
        rows = [part, keep[:, i * SPAN : (i + 1) * SPAN], before, after, jnp.zeros((SPAN - 4, SPAN), jnp.float32)]
        cols[i * SPAN : (i + 1) * SPAN, :] = jnp.concatenate(rows, axis=0).T


def forward_kernel(
    proj, final, vectors, kw, vt, docs, x_any, gy_any,
    kg, vg, acts, kvs, middle_o, sq_o, act_o, grads_o, out_o, wts_o, vecs_o, cols_o,
    w5, kv, sa, xb, st, f5, mid, sig, tables, vecs, prev, cols, split, pk, sems, twin_sems, send_sem, recv_sems,
):
    place_of = Place()
    p = place_of
    row = p.mp % 2
    load_x = pltpu.make_async_copy(x_any.at[row], xb, sems.at[0])
    load_x.start()
    pack_block(p, proj, final, vectors, pk)
    keep = [
        pltpu.make_async_copy(pk, sa.at[p.y, p.x, p.core, p.mp], sems.at[26]),
        pltpu.make_async_copy(kw, kg.at[p.mp, p.y, p.x, p.core], sems.at[27]),
        pltpu.make_async_copy(vt, vg.at[p.mp, p.y, p.x, p.core], sems.at[28]),
    ]
    for copy in keep:
        copy.start()
    greet_all(place_of)
    messages = Messages(send_sem, recv_sems)
    made = streams(place_of, messages, twin_sems, pk, kw, vt, sa, kg, vg)

    def twins(i, half):
        pltpu.make_async_copy(half, half, twin_sems.at[i]).wait()

    def time_twins(i):
        twins(i, sa.at[:, :, 1 - p.core, :, (pl.ds(0, 80), pl.ds(80, 48))[i]])

    prev[...] = jnp.zeros_like(prev)
    play(made, "own")
    describe(docs, row, cols)
    own_docs = row_of(docs, row)
    play(made, "relayA")
    for copy in keep:
        copy.wait()
    time_twins(0)

    def relay(half, first_row, count, slots):
        def body(i, total):
            core, m = i // 2, 2 * (i % 2)
            pair = 8 * half + i
            spot = half, i // 4, core % 2
            rows = pl.ds(first_row, count)
            one, two = wide(sa[spot + (m, rows)]), wide(sa[spot + (m + 1, rows)])
            for n, j in enumerate(slots):
                piece = jnp.concatenate([one[24 * n : 24 * n + 24], two[24 * n : 24 * n + 24]], axis=0)
                w5[j, pl.ds(pl.multiple_of(48 * pair, 16), 48), :] = low(piece)
            return total + one[count - 8 :] + two[count - 8 :]

        return lax.fori_loop(0, 8, body, jnp.zeros((8, 768), jnp.float32))

    left, right = relay(0, 0, 80, (0, 1, 2)), relay(1, 0, 80, (0, 1, 2))
    vecs[0:8, :] = jnp.concatenate([left[:, :384], right[:, :384]], axis=1)
    vecs[8:16, :] = jnp.concatenate([left[:, 384:], right[:, 384:]], axis=1)
    save_v = pltpu.make_async_copy(vecs, vecs_o, sems.at[11])
    save_v.start()

    rate = jnp.exp(vec(vecs, DECAY))
    fade = jnp.exp(-rate)
    place = wide(lax.broadcasted_iota(jnp.int32, (TILE, 1), 0) % SPAN)
    tables[0] = jnp.exp((place - 64.0) * rate)
    tables[1] = jnp.exp((65.0 - place) * rate)
    tables[2] = jnp.exp(-place * rate)
    load_x.wait()
    tiles = [(t, t * TILE, pl.ds(t * TILE, TILE)) for t in range(1024 // TILE)]
    for t, base, r in tiles:
        play(made, f"a{t}.0")

        def first(q, last):
            x = wide(xb[q, :])
            mean = jnp.mean(x, axis=-1, keepdims=True)
            centered = x - mean
            scale = lax.rsqrt(jnp.mean(centered * centered, axis=-1, keepdims=True) + epsilon)
            cols[q, 4:5] = mean
            cols[q, 5:6] = scale
            normed = centered * scale * vec(vecs, GAIN1) + vec(vecs, BIAS1)
            earlier = later(normed, last) * cols[q, 1:2]
            delta = normed - earlier
            for j in range(3):
                st[j, q, :] = low(earlier + delta * vec(vecs, MIX + j))
            st[6, q, :] = low(delta)
            return normed[TILE - 1 :]

        prev[0:1, :] = first(r, prev[0:1, :])
        for j in range(3):
            f5[j, r, :] = dot(st[j, r, :], w5[j])
        play(made, f"a{t}.1")

        key_exp = jnp.exp(f5[0, r, :])
        f5[2, r, :] = jax.nn.sigmoid(f5[2, r, :])
        grown = key_exp * tables[0]
        halves(split.at[0], grown * f5[1, r, :])
        halves(split.at[1], grown)
        time = lax.broadcasted_iota(jnp.int32, (SPAN, SPAN), 0)
        source = lax.broadcasted_iota(jnp.int32, (SPAN, SPAN), 1)
        for i in range(TILE // SPAN):
            block = t * (TILE // SPAN) + i
            same = cols[pl.ds(block * SPAN, SPAN), 0:1] == own_docs[:, block * SPAN : (block + 1) * SPAN]
            mask = jnp.where(same & (source < time), 1.0, 0.0).astype(jnp.bfloat16)
            mask = jnp.concatenate([mask, mask], axis=1)
            for k in range(2):
                f5[3 + k, pl.ds(block * SPAN, SPAN), :] = dot(mask, split[k, i])
        play(made, f"a{t}.2")
        for i in range(TILE // SPAN):
            begin = base + i * SPAN
            top_in, bottom_in = prev[2:3, :], prev[3:4, :]

            q = pl.ds(begin, SPAN)
            values = f5[1, q, :]
            link = cols[q, 2:3] * tables[2, 0:SPAN, :]
            top = f5[3, q, :] * tables[1, 0:SPAN, :] + link * top_in
            bottom = f5[4, q, :] * tables[1, 0:SPAN, :] + link * bottom_in
            f5[3, q, :] = top
            f5[4, q, :] = bottom
            bonus = jnp.exp(f5[0, q, :] + vec(vecs, FIRST))
            st[3, q, :] = low(f5[2, q, :] * ((top + bonus * values) / (bottom + bonus)))
            end = begin + SPAN - 1
            key_exp = jnp.exp(f5[0, end : end + 1, :])
            prev[2:3, :] = fade * f5[3, end : end + 1, :] + key_exp * f5[1, end : end + 1, :]
            prev[3:4, :] = fade * f5[4, end : end + 1, :] + key_exp
    saves = [pltpu.make_async_copy(f5, kvs, sems.at[16])]
    saves[0].start()
    play(made, "relayB")
    time_twins(1)
    relay(0, 80, 48, (3, 4))
    relay(1, 80, 48, (3, 4))
    save_w = pltpu.make_async_copy(w5, wts_o, sems.at[10])
    save_w.start()
    for t, base, r in tiles:
        play(made, f"b{t}.0")
        mid[r, :] = dot(st[3, r, :], w5[4])

        def fourth(q, last):
            middle = wide(xb[q, :]) + mid[q, :]
            mid[q, :] = middle
            mean = jnp.mean(middle, axis=-1, keepdims=True)
            centered = middle - mean
            scale = lax.rsqrt(jnp.mean(centered * centered, axis=-1, keepdims=True) + epsilon)
            cols[q, 6:7] = mean
            cols[q, 7:8] = scale
            normed = centered * scale * vec(vecs, GAIN2) + vec(vecs, BIAS2)
            earlier = later(normed, last) * cols[q, 1:2]
            delta = normed - earlier
            for j in range(2):
                st[4 + j, q, :] = low(earlier + delta * vec(vecs, BLEND + j))
            st[7, q, :] = low(delta)
            return normed[TILE - 1 :]

        prev[1:2, :] = fourth(r, prev[1:2, :])
        play(made, f"b{t}.1")
        sig[r, :] = dot(st[5, r, :], w5[3])
        saves += [
            pltpu.make_async_copy(st.at[:, r], acts.at[:, r], sems.at[12 + t]),
            pltpu.make_async_copy(mid.at[r], middle_o.at[r], sems.at[20 + t]),
        ]
        for copy in saves[-2:]:
            copy.start()
    saves.append(pltpu.make_async_copy(cols, cols_o, sems.at[36]))
    saves[-1].start()
    load_gy = pltpu.make_async_copy(gy_any.at[row], xb, sems.at[24])
    load_gy.start()
    messages.finish()

    def load_kv(m, which, array):
        target = kv.at[m]
        return pltpu.make_async_copy(array.at[m], target, sems.at[4 * which + 1 + m])

    pending = {}
    for m in range(4):
        play(made, f"h{m}")
        if m == 0:
            for slab in range(4):
                twins(2 + slab, kg.at[slab, :, :, 1 - p.core])
                load_kv(slab, 0, kg).start()
        load_kv(m, 0, kg).wait()
        if m == 0:
            for copy in saves:
                copy.wait()

        def hidden(t, carry):
            r = rows_at(t * WIDE, WIDE)
            active = jnp.maximum(dot(st[4, r, :], kv[m].reshape(768, 768)), 0.0)
            squared = low(active * active)
            spot = m // 2, m % 2, t
            sa[spot] = squared.reshape(4, 128, 768)
            st[m, r, :] = low(active)
            return carry

        lax.fori_loop(0, 1024 // WIDE, hidden, 0)
        pending[m] = pltpu.make_async_copy(st.at[m], act_o.at[m], sems.at[29 + m])
        pending[m].start()
    save_sq = pltpu.make_async_copy(sa, sq_o, sems.at[33])
    save_sq.start()
    pair = p.mp // 2
    for turn in range(2):
        play(made, f"c{2 * turn}")
        at = pair if turn == 0 else 1 - pair
        loads = []
        for i in range(2):
            slab = 2 * at + i
            twins(6 + slab, vg.at[slab, :, :, 1 - p.core])
            loads.append(pltpu.make_async_copy(vg.at[slab], kv.at[2 * turn + i], sems.at[5 + 2 * turn + i]))
            loads[-1].start()
        for i in range(2):
            loads[i].wait()
            if i == 1:
                play(made, f"c{2 * turn + 1}")

            def content(t, carry):
                r = rows_at(t * WIDE, WIDE)
                squared = sa[at, i, t].reshape(WIDE, 768)
                part = dot_nt(squared, kv[2 * turn + i].reshape(768, 768))
                f5[turn, r, :] = part if i == 0 else f5[turn, r, :] + part
                return carry

            lax.fori_loop(0, 1024 // WIDE, content, 0)

    play(made, "fin")
    play(made, "end")
    load_gy.wait()

    last = []
    for t, _, q in tiles:
        gate = jax.nn.sigmoid(sig[q, :])
        carried = f5[0, q, :] + f5[1, q, :]
        st[5, q, :] = low(mid[q, :] + gate * carried)
        passed = wide(xb[q, :]) * gate
        st[6, q, :] = low(passed)
        st[7, q, :] = low(passed * carried * (1.0 - gate))
        last += [
            pltpu.make_async_copy(st.at[5, q], out_o.at[q], sems.at[37 + t]),
            pltpu.make_async_copy(st.at[pl.ds(6, 2), q], grads_o.at[:, q], sems.at[41 + t]),
        ]
        for copy in last[-2:]:
            copy.start()
    save_w.wait()
    save_v.wait()
    save_sq.wait()
    for m in range(4):
        pending.pop(m).wait()
    messages.finish()
    for copy in last:
        copy.wait()


ANY = pl.BlockSpec(memory_space=pl.ANY)
ON_CORE = pl.BlockSpec(memory_space=pltpu.VMEM)
LIMIT = 63 * MIB


def forward(proj, final, vectors, kw, vt, docs, x, gy):
    bf, f32 = jnp.bfloat16, jnp.float32
    shape = jax.ShapeDtypeStruct
    return pl.pallas_call(
        forward_kernel,
        out_shape=(
            shape((4, 2, 2, 2, 96, 768), bf), shape((4, 2, 2, 2, 96, 768), bf),
            shape((8, 1024, 768), bf), shape((5, 1024, 768), f32), shape((1024, 768), f32),
            shape((2, 2, 2, 4, 128, 768), bf), shape((4, 1024, 768), bf), shape((2, 1024, 768), bf),
            shape((1024, 768), bf), shape((5, 768, 768), bf), shape((16, 768), f32), shape((1024, 128), f32),
        ),
        in_specs=[ON_CORE] * 6 + [ANY] * 2,
        out_specs=[ANY] * 12,
        scratch_shapes=[
            pltpu.VMEM((5, 768, 768), bf), pltpu.VMEM((4, 2, 2, 2, 96, 768), bf), pltpu.VMEM((2, 2, 2, 4, 128, 768), bf),
            pltpu.VMEM((1024, 768), bf), pltpu.VMEM((8, 1024, 768), bf), pltpu.VMEM((5, 1024, 768), f32),
            pltpu.VMEM((1024, 768), f32), pltpu.VMEM((1024, 768), f32),
            pltpu.VMEM((3, TILE, 768), f32), pltpu.VMEM((16, 768), f32), pltpu.VMEM((8, 768), f32),
            pltpu.VMEM((1024, 128), f32), pltpu.VMEM((2, 2, 2 * SPAN, 768), bf), pltpu.VMEM((128, 768), bf),
            pltpu.SemaphoreType.DMA((45,)), pltpu.SemaphoreType.DMA((10,)), pltpu.SemaphoreType.DMA,
            pltpu.SemaphoreType.DMA((15 * len(PARTS),)),
        ],
        compiler_params=pltpu.CompilerParams(vmem_limit_bytes=LIMIT, collective_id=0, has_side_effects=True),
        name="forward",
    )(proj, final, vectors, kw, vt, docs, x, gy)


class Scatter:
    def __init__(self, place, messages, source, received, kept, steps, final, orders):
        self.p, self.msg = place, messages
        self.source, self.received, self.kept, self.steps, self.final = source, received, kept, steps, final
        self.orders = orders
        self.parts = len(orders)
        self.core_waits, self.waits = {}, []

    def cols(self, part):
        width = self.kept.shape[-1] // self.parts
        return pl.ds(part * width, width)

    def start(self, j):
        p = self.p
        target = self.received.at[:, j]
        self.core_waits[j] = self.msg.send(self.source.at[:, j, :, :, 1 - p.core], target, target, p.sib)

    def core(self, j):
        p = self.p
        self.core_waits[j].wait_recv()
        for i in range(self.kept.shape[0]):
            for y in range(2):
                for x in range(2):
                    self.kept[i, j, y, x] = self.source[i, j, y, x, p.core] + self.received[i, j, y, x]
        self.send(0, j)

    def index(self, order, step, flip):
        p = self.p
        mine = {"x": p.x, "y": p.y, "j": p.mp % 2}
        picked = {}
        for at, axis in enumerate(order):
            if at < step:
                picked[axis] = mine[axis]
            elif at == step:
                picked[axis] = 1 - mine[axis] if flip else mine[axis]
            else:
                picked[axis] = None
        return picked

    def send(self, step, j=None):
        p = self.p
        device = {"x": p.xn, "y": p.yn, "j": p.pair}
        if step > 0:
            self.waits = []
        for part in range(self.parts):
            order = self.orders[part]
            picked = self.index(order, step, True)
            target = self.steps[step].at[part]
            if j is not None:
                picked["j"] = j
                target = self.steps[step].at[part, :, j]
            select = tuple(ALL if picked[a] is None else picked[a] for a in "jyx")
            piece = self.kept.at[(ALL,) + select + (ALL, self.cols(part))]
            self.waits.append(self.msg.send(piece, target, target, device[order[step]]))

    def add(self, step, last=False):
        for wait in self.waits:
            wait.wait_recv()
        for part in range(self.parts):
            picked = self.index(self.orders[part], step, False)
            free = [a for a in "jyx" if picked[a] is None]
            for i in range(self.kept.shape[0]):
                for number in range(2 ** len(free)):
                    bits = {a: (number >> (len(free) - 1 - k)) & 1 for k, a in enumerate(free)}
                    select = tuple(bits[a] if picked[a] is None else picked[a] for a in "jyx")
                    spot = (i,) + select + (ALL, self.cols(part))
                    arrived = self.steps[step][(part, i) + tuple(bits[a] for a in free)]
                    if step == 2:
                        self.final[i, :, self.cols(part)] = wide(self.kept[spot]) + wide(arrived)
                    else:
                        self.kept[spot] = self.kept[spot] + arrived
        if step < 2 and not last:
            self.send(step + 1)


class Plane:
    def __init__(self, place, messages, source, received, kept, arrived, last, final):
        self.p, self.msg = place, messages
        self.source, self.received, self.kept, self.arrived, self.last, self.final = source, received, kept, arrived, last, final

    def start(self):
        p = self.p
        self.wait = self.msg.send(self.source.at[:, :, :, 1 - p.core], self.received, self.received, p.sib)

    def core(self):
        p, kept = self.p, self.kept
        self.wait.wait_recv()
        for j in range(2):
            for y in range(2):
                for x in range(2):
                    kept[j, y, x] = self.source[j, y, x, p.core] + self.received[j, y, x]
        pieces = (
            (kept.at[:, 1 - p.y, 1 - p.x], p.across), (kept.at[:, p.y, 1 - p.x], p.xn), (kept.at[:, 1 - p.y, p.x], p.yn),
        )
        self.waits = [
            self.msg.send(piece, self.arrived.at[n], self.arrived.at[n], device) for n, (piece, device) in enumerate(pieces)
        ]

    def plane(self):
        p, kept = self.p, self.kept
        for wait in self.waits:
            wait.wait_recv()
        for j in range(2):
            total = wide(kept[j, p.y, p.x])
            for n in range(3):
                total += wide(self.arrived[n, j])
            kept[j, p.y, p.x] = total.astype(kept.dtype)
        self.wait = self.msg.send(kept.at[1 - p.mp % 2, p.y, p.x], self.last, self.last, p.pair)

    def z(self):
        p = self.p
        self.wait.wait_recv()
        self.final[...] = wide(self.kept[p.mp % 2, p.y, p.x]) + wide(self.last[...])


def plane_scratch(rows, cols, dtype):
    return [
        pltpu.VMEM((2, 2, 2, rows, cols), dtype), pltpu.VMEM((2, 2, 2, rows, cols), dtype),
        pltpu.VMEM((3, 2, rows, cols), dtype), pltpu.VMEM((rows, cols), dtype),
    ]


def channel_back_kernel(
    kg, vg, wts, acts, sq, act, grads, middle, gy_any, out_row, cols, vecs,
    gm_o, kept_o, out_o, sums_o,
    kv, sqs, acs, gcg, cc, dh, acc, wg, mid, gy, gm, delta, stage, gate_w, sums, nxt, result, received, kept, first_step, sems, send_sem, recv_sems,
):
    place = Place()
    mp = place.mp
    row, pair = mp % 2, mp // 2
    load_row = pltpu.make_async_copy(out_row, result, sems.at[22])
    load_row.start()
    greet([place.sib, place.xn, place.yn, place.pair])
    messages = Messages(send_sem, recv_sems)
    load_row.wait()
    channel = Scatter(place, messages, stage, received, kept, [first_step], None, ("xyj", "yxj"))
    arrival = messages.send(result, out_o.at[row], out_o.at[1 - row], place.pair)
    keep_row = pltpu.make_async_copy(result, out_o.at[row], sems.at[21])
    keep_row.start()
    order = [2 * pair, 2 * pair + 1, 2 - 2 * pair, 3 - 2 * pair]

    def loads(j):
        m, slot = order[j], j % 2
        copies = [
            pltpu.make_async_copy(kg.at[m], kv.at[0, slot], sems.at[3 * j]),
            pltpu.make_async_copy(vg.at[m], kv.at[1, slot], sems.at[3 * j + 1]),
            pltpu.make_async_copy(act.at[m], acs.at[slot], sems.at[3 * j + 2]),
        ]
        return copies

    load_g = pltpu.make_async_copy(grads, gcg, sems.at[12])
    load_g.start()
    others = [
        pltpu.make_async_copy(sq.at[pl.ds(2 * pair, 2)], sqs, sems.at[13]),
        pltpu.make_async_copy(acts.at[pl.ds(4, 2)], cc, sems.at[14]),
        pltpu.make_async_copy(wts.at[3], wg, sems.at[15]),
        pltpu.make_async_copy(middle, mid, sems.at[16]),
        pltpu.make_async_copy(acts.at[7], delta, sems.at[19]),
        pltpu.make_async_copy(gy_any.at[row], gy, sems.at[17]),
    ]
    for copy in [others[1]] + loads(0) + [others[0]] + loads(1) + others[2:]:
        copy.start()
    load_g.wait()
    others[1].wait()

    def gate_weights(t, carry):
        c = pl.ds(pl.multiple_of(t * 384, 128), 384)
        gate_w[c, :] = dot_tn(cc[1, :, c], gcg[1])
        return carry

    lax.fori_loop(0, 2, gate_weights, 0)

    def gate_pack(dp, carry):
        for j in range(2):
            start = pl.multiple_of(96 * dp + 48 * pair + 24 * j, 8)
            piece = jnp.concatenate([gate_w[pl.ds(start, 24), :], jnp.zeros((8, 768), jnp.float32)], axis=0)
            stage[0, j, dp // 4, (dp // 2) % 2, dp % 2, 192:224, :] = low(piece)
        return carry

    lax.fori_loop(0, 8, gate_pack, 0)
    for j in range(4):
        slot = j % 2
        for copy in loads(j):
            copy.wait()

        def hidden_back(t, carry):
            r = rows_at(t * WIDE, WIDE)
            active = wide(acs[slot, r, :])
            grad = low(dot(gcg[0, r, :], kv[1, slot]) * (2.0 * active))
            if j < 2:
                dh[j, r, :] = grad
            part = dot_nt(grad, kv[0, slot])
            acc[j // 2, r, :] = part if j % 2 == 0 else acc[j // 2, r, :] + part
            return carry

        lax.fori_loop(0, 1024 // WIDE, hidden_back, 0)
        if j < 2:
            for copy in loads(j + 2):
                copy.start()
            if j == 0:
                others[0].wait()
            else:
                channel.core(0)

            def weights(t, carry):
                c = pl.ds(pl.multiple_of(t * 384, 128), 384)
                key = low(dot_tn(cc[0, :, c], dh[j]))
                stage[0, j, t, :, :, 0:96, :] = key.reshape(2, 2, 96, 768)
                value = low(dot_tn(gcg[0, :, c], sqs[j].reshape(1024, 768)))
                stage[0, j, t, :, :, 96:192, :] = value.reshape(2, 2, 96, 768)
                return carry

            lax.fori_loop(0, 2, weights, 0)
            channel.start(j)
        elif j == 2:
            channel.core(1)
            for copy in others[2:]:
                copy.wait()

    sums[...] = jnp.zeros_like(sums)
    nxt[...] = jnp.zeros_like(nxt)

    def gate_back(t, carry):
        r = rows_at(t * WIDE, WIDE)
        gm[r, :] = dot_nt(gcg[1, r, :], wg[...])
        return carry

    lax.fori_loop(0, 1024 // WIDE, gate_back, 0)
    gain = vec(vecs, GAIN2)
    key_mix, rec_mix = vec(vecs, BLEND), vec(vecs, BLEND + 1)

    def tokens(n, state):
        q = rows_at((1024 // TILE - 1 - n) * TILE, TILE)
        grad_key, grad_rec = acc[0, q, :] + acc[1, q, :], gm[q, :]
        step = wide(delta[q, :])
        sums[2] += row_sums(grad_key * step)
        sums[3] += row_sums(grad_rec * step)
        grad = grad_key * key_mix + grad_rec * rec_mix
        back = (grad_key + grad_rec - grad) * cols[q, 1:2]
        grad = grad + sooner(back, state)
        scale = cols[q, 7:8]
        normal = (mid[q, :] - cols[q, 6:7]) * scale
        sums[0] += row_sums(grad * normal)
        sums[1] += row_sums(grad)
        gm[q, :] = wide(gy[q, :]) + norm_back(grad * gain, normal, scale)
        return back[0:1]

    lax.fori_loop(0, 1024 // TILE, tokens, jnp.zeros((1, 768), jnp.float32))
    store_gm = pltpu.make_async_copy(gm, gm_o, sems.at[20])
    store_gm.start()
    for i in range(4):
        sums_o[i : i + 1, :] = jnp.sum(sums[i], axis=0, keepdims=True)
    sums_o[4:8, :] = jnp.zeros((4, 768), jnp.float32)
    channel.add(0, last=True)
    store = pltpu.make_async_copy(kept, kept_o, sems.at[18])
    store.start()
    store.wait()
    store_gm.wait()
    keep_row.wait()
    arrival.wait_recv()
    messages.finish()


def channel_back(kg, vg, wts, acts, sq, act, grads, middle, gy, out_row, cols, vecs):
    bf, f32 = jnp.bfloat16, jnp.float32
    shape = jax.ShapeDtypeStruct
    return pl.pallas_call(
        channel_back_kernel,
        out_shape=(
            shape((1024, 768), f32), shape((1, 2, 2, 2, 224, 768), bf),
            shape((2, 1024, 768), bf), shape((8, 768), f32),
        ),
        in_specs=[ANY] * 10 + [ON_CORE] * 2,
        out_specs=[ANY] * 3 + [ON_CORE],
        scratch_shapes=[
            pltpu.VMEM((2, 2, 768, 768), bf), pltpu.VMEM((2, 8, 128, 768), bf), pltpu.VMEM((2, 1024, 768), bf),
            pltpu.VMEM((2, 1024, 768), bf), pltpu.VMEM((2, 1024, 768), bf), pltpu.VMEM((2, 1024, 768), bf),
            pltpu.VMEM((2, 1024, 768), f32), pltpu.VMEM((768, 768), bf), pltpu.VMEM((1024, 768), f32),
            pltpu.VMEM((1024, 768), bf), pltpu.VMEM((1024, 768), f32), pltpu.VMEM((1024, 768), bf), pltpu.VMEM((1, 2, 2, 2, 2, 224, 768), bf),
            pltpu.VMEM((768, 768), f32), pltpu.VMEM((4, 8, 768), f32), pltpu.VMEM((8, 768), f32),
            pltpu.VMEM((1024, 768), bf), pltpu.VMEM((1, 2, 2, 2, 224, 768), bf), pltpu.VMEM((1, 2, 2, 2, 224, 768), bf),
            pltpu.VMEM((2, 1, 2, 2, 224, 384), bf),
            pltpu.SemaphoreType.DMA((23,)), pltpu.SemaphoreType.DMA, pltpu.SemaphoreType.DMA((7,)),
        ],
        compiler_params=pltpu.CompilerParams(vmem_limit_bytes=LIMIT, collective_id=1, has_side_effects=True),
        name="channel_back",
    )(kg, vg, wts, acts, sq, act, grads, middle, gy, out_row, cols, vecs)


def time_back_kernel(
    wts, acts, kvs, gm_any, x_any, kept_any, cols, docs, vecs, sums_c,
    ig_o, gkv_o, gt_o, small_o,
    w4, ins, f5, gm, xb, gb, gkvr, delta, grads, split, pack, tables, sums, nxt, small_cut, *scratch,
):
    kept, second_step, third_step = scratch[:3]
    s_scratch = scratch[3:7]
    t_scratch = [scratch[7 + 4 * i : 11 + 4 * i] for i in range(4)]
    sems, send_sem, recv_sems = scratch[23:]
    place_of = Place()
    mp = place_of.mp
    row, pair = mp % 2, mp // 2
    load_kept = pltpu.make_async_copy(kept_any, kept, sems.at[8])
    load_w = [
        pltpu.make_async_copy(wts.at[4], w4.at[3], sems.at[1]),
        pltpu.make_async_copy(wts.at[pl.ds(0, 3)], w4.at[pl.ds(0, 3)], sems.at[2]),
    ]
    tile_loads = {}
    for t in reversed(range(1024 // TILE)):
        r = pl.ds(t * TILE, TILE)
        tile_loads[t] = [
            pltpu.make_async_copy(gm_any.at[r], gm.at[r], sems.at[18 + 4 * t]),
            pltpu.make_async_copy(kvs.at[:, r], f5.at[:, r], sems.at[19 + 4 * t]),
            pltpu.make_async_copy(x_any.at[row, r], xb.at[r], sems.at[20 + 4 * t]),
            pltpu.make_async_copy(acts.at[6, r], delta.at[r], sems.at[21 + 4 * t]),
        ]
    load_ins = [pltpu.make_async_copy(acts.at[i], ins.at[i % 2], sems.at[4 + i]) for i in range(4)]
    for copy in load_w[:1] + tile_loads[3] + load_w[1:] + [load_kept] + tile_loads[2] + tile_loads[1] + tile_loads[0] + load_ins[:2]:
        copy.start()
    greet([place_of.sib, place_of.xn, place_of.yn, place_of.across, place_of.pair])
    messages = Messages(send_sem, recv_sems)
    channel = Scatter(place_of, messages, None, None, kept, [None, second_step, third_step], gkv_o, ("xyj", "yxj"))
    vectors = Plane(place_of, messages, small_cut.at[0], *s_scratch, small_o.at[0])
    mixing = [Plane(place_of, messages, pack.at[i], *t_scratch[i], gt_o.at[i]) for i in range(4)]
    rate = jnp.exp(vec(vecs, DECAY))
    fade = jnp.exp(-rate)
    place = wide(lax.broadcasted_iota(jnp.int32, (TILE, 1), 0) % SPAN)
    tables[0] = jnp.exp((64.0 - place) * rate)
    tables[1] = jnp.exp((place - 63.0) * rate)
    tables[2] = jnp.exp((place - 127.0) * rate)
    sums[...] = jnp.zeros_like(sums)
    nxt[...] = jnp.zeros_like(nxt)
    gain = vec(vecs, GAIN1)
    own_docs = row_of(docs, row)

    def tile(t):
        base = t * TILE
        r = pl.ds(base, TILE)
        for copy in tile_loads[t]:
            copy.wait()
        gb[r, :] = low(gm[r, :])
        if t == 3:
            load_w[0].wait()
        grads[0] = dot_nt(gb[r, :], w4[3])

        values, gate = f5[1, r, :], f5[2, r, :]
        bonus = jnp.exp(f5[0, r, :] + vec(vecs, FIRST))
        inverse = 1.0 / (f5[4, r, :] + bonus)
        mixed = (f5[3, r, :] + bonus * values) * inverse
        grad_mixed = grads[0] * gate
        gkvr[2, r, :] = low(grad_mixed * mixed * (1.0 - gate))
        grad_top = grad_mixed * inverse
        shrunk = grad_top * tables[0]
        halves(split.at[0], shrunk)
        halves(split.at[1], -shrunk * mixed)
        direct = bonus * grad_top
        own = direct * (values - mixed)
        grads[0] = direct
        grads[1] = own
        sums[0] += row_sums(own)
        grads[3] = grad_top
        edges = [grads[3, i * SPAN : i * SPAN + 1, :] for i in range(TILE // SPAN)]
        time = lax.broadcasted_iota(jnp.int32, (SPAN, SPAN), 0)
        source = lax.broadcasted_iota(jnp.int32, (SPAN, SPAN), 1)
        for i in reversed(range(TILE // SPAN)):
            block = t * (TILE // SPAN) + i
            same = cols[pl.ds(block * SPAN, SPAN), 0:1] == own_docs[:, block * SPAN : (block + 1) * SPAN]
            mask = jnp.where(same & (source > time), 1.0, 0.0).astype(jnp.bfloat16)
            mask = jnp.concatenate([mask, mask], axis=1)
            for k in range(2):
                grads[2 + k, pl.ds(i * SPAN, SPAN), :] = dot(mask, split[k, i])
        for i in reversed(range(TILE // SPAN)):
            begin = base + i * SPAN
            top_in, bottom_in = nxt[1:2, :], nxt[2:3, :]

            q, here = pl.ds(begin, SPAN), pl.ds(i * SPAN, SPAN)
            link = cols[q, 3:4] * tables[2, 0:SPAN, :]
            state_top = grads[2, here, :] * tables[1, 0:SPAN, :] + link * top_in
            state_bottom = grads[3, here, :] * tables[1, 0:SPAN, :] + link * bottom_in
            key_exp = jnp.exp(f5[0, q, :])
            gkvr[0, q, :] = low(grads[1, here, :] + key_exp * (state_top * f5[1, q, :] + state_bottom))
            gkvr[1, q, :] = low(grads[0, here, :] + key_exp * state_top)
            sums[1] += row_sums(state_top * f5[3, q, :] + state_bottom * f5[4, q, :])
            row_top, row_bottom = state_top[0:1], state_bottom[0:1]
            bonus = jnp.exp(f5[0, begin : begin + 1, :] + vec(vecs, FIRST))
            bottom = f5[4, begin : begin + 1, :] + bonus
            mixed = (f5[3, begin : begin + 1, :] + bonus * f5[1, begin : begin + 1, :]) / bottom
            nxt[1:2, :] = fade * row_top + edges[i]
            nxt[2:3, :] = fade * row_bottom - edges[i] * mixed
        if t == 3:
            load_w[1].wait()
        for j in range(3):
            grads[j] = dot_nt(gkvr[j, r, :], w4[j])

        def third(q, state):
            step = wide(delta[q, :])
            grad, whole = 0.0, 0.0
            for j in range(3):
                into = grads[j]
                sums[4 + j] += row_sums(into * step)
                grad += into * vec(vecs, MIX + j)
                whole += into
            back = (whole - grad) * cols[q, 1:2]
            grad = grad + sooner(back, state)
            scale = cols[q, 5:6]
            normal = (wide(xb[q, :]) - cols[q, 4:5]) * scale
            sums[2] += row_sums(grad * normal)
            sums[3] += row_sums(grad)
            xb[q, :] = low(gm[q, :] + norm_back(grad * gain, normal, scale))
            return back[0:1]

        nxt[0:1, :] = third(r, nxt[0:1, :])

    arrivals = []
    keeps = []
    for t in reversed(range(1024 // TILE)):
        tile(t)
        r = pl.ds(t * TILE, TILE)
        done = xb.at[r]
        arrivals.append(messages.send(done, ig_o.at[row, r], ig_o.at[1 - row, r], place_of.pair))
        keeps.append(pltpu.make_async_copy(done, ig_o.at[row, r], sems.at[14 + t]))
        keeps[-1].start()
        if t == 3:
            load_kept.wait()
            channel.send(1)
        elif t == 1:
            channel.add(1)

    def product(slot, right):
        load_ins[slot].wait()
        left = ins.at[slot % 2]
        def body(t, carry):
            c = pl.ds(pl.multiple_of(t * 384, 128), 384)
            f5[0, c, :] = dot_tn(left[:, c], right[...])
            return carry

        lax.fori_loop(0, 2, body, 0)

        def packed(dp, carry):
            for j in range(2):
                start = pl.multiple_of(96 * dp + 48 * pair + 24 * j, 8)
                piece = jnp.concatenate([f5[0, pl.ds(start, 24), :], jnp.zeros((8, 768), jnp.float32)], axis=0)
                pack[slot, j, dp // 4, (dp // 2) % 2, dp % 2] = low(piece)
            return carry

        lax.fori_loop(0, 8, packed, 0)
        if slot < 2:
            load_ins[slot + 2].start()
        mixing[slot].start()

    totals = [jnp.sum(sums[i], axis=0, keepdims=True) for i in range(7)]
    totals[1] = totals[1] * (-rate * fade)
    small = jnp.concatenate([sums_c[0:4, :]] + totals + [jnp.zeros((5, 768), jnp.float32)], axis=0)
    turned = pltpu.roll(small, (768 - 48 * pair) % 768, 1)
    for dp in range(8):
        for j in range(2):
            start = 96 * dp + 24 * j
            piece = turned if start == 0 else pltpu.roll(turned, 768 - start, 1)
            small_cut[0, j, dp // 4, (dp // 2) % 2, dp % 2] = piece[:, :128]
    vectors.start()
    product(0, gkvr.at[0])
    vectors.core()
    product(1, gkvr.at[1])
    mixing[0].core()
    product(2, gkvr.at[2])
    mixing[1].core()
    mixing[0].plane()
    vectors.plane()
    product(3, gb)
    mixing[2].core()
    mixing[1].plane()
    mixing[3].core()
    mixing[2].plane()
    channel.add(2)
    vectors.z()
    mixing[0].z()
    mixing[1].z()
    mixing[3].plane()
    mixing[2].z()
    mixing[3].z()
    for copy in keeps:
        copy.wait()
    for wait in arrivals:
        wait.wait_recv()
    messages.finish()


def time_back(wts, acts, kvs, gm, x, kept, cols, docs, vecs, sums_c):
    bf, f32 = jnp.bfloat16, jnp.float32
    shape = jax.ShapeDtypeStruct
    return pl.pallas_call(
        time_back_kernel,
        out_shape=(
            shape((2, 1024, 768), bf), shape((1, 224, 768), f32), shape((4, 32, 768), f32), shape((1, 16, 128), f32),
        ),
        in_specs=[ANY] * 6 + [ON_CORE] * 4,
        out_specs=[ANY] + [ON_CORE] * 3,
        scratch_shapes=[
            pltpu.VMEM((4, 768, 768), bf), pltpu.VMEM((2, 1024, 768), bf), pltpu.VMEM((5, 1024, 768), f32),
            pltpu.VMEM((1024, 768), f32), pltpu.VMEM((1024, 768), bf), pltpu.VMEM((1024, 768), bf),
            pltpu.VMEM((3, 1024, 768), bf), pltpu.VMEM((1024, 768), bf), pltpu.VMEM((4, TILE, 768), f32),
            pltpu.VMEM((2, 2, 2 * SPAN, 768), bf),
            pltpu.VMEM((4, 2, 2, 2, 2, 32, 768), bf), pltpu.VMEM((3, TILE, 768), f32), pltpu.VMEM((7, 8, 768), f32),
            pltpu.VMEM((8, 768), f32), pltpu.VMEM((1, 2, 2, 2, 2, 16, 128), f32),
        ]
        + [pltpu.VMEM((1, 2, 2, 2, 224, 768), bf), pltpu.VMEM((2, 1, 2, 224, 384), bf), pltpu.VMEM((2, 1, 224, 384), bf)]
        + plane_scratch(16, 128, f32)
        + plane_scratch(32, 768, bf) * 4
        + [pltpu.SemaphoreType.DMA((34,)), pltpu.SemaphoreType.DMA, pltpu.SemaphoreType.DMA((36,))],
        compiler_params=pltpu.CompilerParams(vmem_limit_bytes=LIMIT, collective_id=2, has_side_effects=True),
        name="time_back",
    )(wts, acts, kvs, gm, x, kept, cols, docs, vecs, sums_c)


def results_kernel(
    out_any, ig_any, gkv_any, gt_any, small,
    out_o, ig_o, gain1, bias1, gain2, bias2, mix, blend_o, decay, first, grad_mix, grad_out, grad_key, grad_value,
    rows, halves_in, halves_out, gkv, gt, sems,
):
    cut = 256
    parts = [(i, pl.ds(j * cut, cut)) for i in range(2) for j in range(1024 // cut)]
    loads = [pltpu.make_async_copy(ig_any.at[i, r], halves_in.at[i, r], sems.at[n]) for n, (i, r) in enumerate(parts)]
    load_out = [pltpu.make_async_copy(out_any.at[i], rows.at[i], sems.at[16 + i]) for i in range(2)]
    load_w = [pltpu.make_async_copy(gkv_any, gkv, sems.at[18]), pltpu.make_async_copy(gt_any, gt, sems.at[19])]
    for copy in loads[:4] + load_w + loads[4:] + load_out:
        copy.start()
    for ref, slot in ((gain2, 0), (bias2, 1), (first, 4), (decay, 5), (gain1, 6), (bias1, 7)):
        ref[...] = small[0, slot, 0:24]
    blend_o[...] = small[0, 2:4, 0:24]
    mix[...] = small[0, 8:11, 0:24]
    stores = []

    def store(source, target):
        copy = pltpu.make_async_copy(source, target, sems.at[20 + len(stores)])
        copy.start()
        stores.append(copy)

    for n, (i, r) in enumerate(parts):
        loads[n].wait()
        halves_out[i, r, :] = wide(halves_in[i, r, :])
        store(halves_out.at[i, r], ig_o.at[i, r])
        if n == 3:
            for copy in load_w:
                copy.wait()
            store(gt.at[pl.ds(0, 3), pl.ds(0, 24)], grad_mix.at[pl.ds(0, 3)])
            store(gkv.at[0, pl.ds(192, 24)], grad_mix.at[3])
            store(gt.at[3, pl.ds(0, 24)], grad_out)
            store(gkv.at[0, pl.ds(0, 96)], grad_key)
            store(gkv.at[0, pl.ds(96, 96)], grad_value)
    for i in range(2):
        load_out[i].wait()
        store(rows.at[i], out_o.at[i])
    for copy in stores:
        copy.wait()


def results(out, ig, gkv, gt, small):
    bf, f32 = jnp.bfloat16, jnp.float32
    shape = jax.ShapeDtypeStruct
    vector = shape((24,), f32)
    return pl.pallas_call(
        results_kernel,
        out_shape=(
            shape((2, 1024, 768), bf), shape((2, 1024, 768), f32), vector, vector, vector, vector,
            shape((3, 24), f32), shape((2, 24), f32), vector, vector,
            shape((4, 24, 768), f32), shape((24, 768), f32), shape((96, 768), f32), shape((96, 768), f32),
        ),
        in_specs=[ANY] * 4 + [ON_CORE],
        out_specs=[ANY] * 2 + [ON_CORE] * 8 + [ANY] * 4,
        scratch_shapes=[
            pltpu.VMEM((2, 1024, 768), bf), pltpu.VMEM((2, 1024, 768), bf), pltpu.VMEM((2, 1024, 768), f32),
            pltpu.VMEM((1, 224, 768), f32), pltpu.VMEM((4, 32, 768), f32), pltpu.SemaphoreType.DMA((40,)),
        ],
        compiler_params=pltpu.CompilerParams(vmem_limit_bytes=LIMIT),
        name="results",
    )(out, ig, gkv, gt, small)


def on_device(
    residual_input, article_numbers, upstream_gradient,
    prenorm_scaling, prenorm_offset, postnorm_scaling, postnorm_offset,
    attention_blend, feedforward_blend, forgetting_logrates, present_reward,
    projection_matrices, final_matrix, address_matrix, content_matrix,
):
    pieces = (
        prenorm_scaling[None], prenorm_offset[None], postnorm_scaling[None], postnorm_offset[None],
        attention_blend, forgetting_logrates[None], present_reward[None], feedforward_blend,
    )
    vectors, first_row = 0.0, 0
    for piece in pieces:
        count, lanes = piece.shape
        vectors = vectors + jnp.pad(piece, ((first_row, 16 - first_row - count), (0, 128 - lanes)))
        first_row += count
    vectors = vectors.astype(jnp.bfloat16)
    kg, vg, acts, kvs, middle, sq, act, grads, out_row, wts, vecs, cols = forward(
        projection_matrices, final_matrix, vectors, address_matrix, content_matrix.T, article_numbers,
        residual_input, upstream_gradient,
    )
    kg, vg, sq = kg.reshape(4, 768, 768), vg.reshape(4, 768, 768), sq.reshape(4, 8, 128, 768)
    gm, kept, output, sums_c = channel_back(
        kg, vg, wts, acts, sq, act, grads, middle, upstream_gradient, out_row, cols, vecs
    )
    input_grad, gkv, gt, small = time_back(
        wts, acts, kvs, gm, residual_input, kept, cols, article_numbers, vecs, sums_c
    )
    *others, grad_value = results(output, input_grad, gkv, gt, small)
    return (*others, grad_value.T)


def fits(mesh):
    return dict(mesh.shape) == {"dp": 8, "mp": 4}


def solution(mesh):
    return jax.shard_map(
        on_device if fits(mesh) else general_device,
        mesh=mesh,
        in_specs=(
            P("dp", None, None),
            P("dp", None),
            P("dp", None, None),
            P(("dp", "mp")),
            P(("dp", "mp")),
            P(("dp", "mp")),
            P(("dp", "mp")),
            P(None, ("dp", "mp")),
            P(None, ("dp", "mp")),
            P(("dp", "mp")),
            P(("dp", "mp")),
            P(None, ("dp", "mp"), None),
            P(("dp", "mp"), None),
            P("dp", "mp"),
            P("mp", "dp"),
        ),
        out_specs=(
            P("dp", None, None),
            P("dp", None, None),
            P(("dp", "mp")),
            P(("dp", "mp")),
            P(("dp", "mp")),
            P(("dp", "mp")),
            P(None, ("dp", "mp")),
            P(None, ("dp", "mp")),
            P(("dp", "mp")),
            P(("dp", "mp")),
            P(None, ("dp", "mp"), None),
            P(("dp", "mp"), None),
            P("dp", "mp"),
            P("mp", "dp"),
        ),
        check_vma=False,
    )
```

```python
import functools

import jax
import jax.numpy as jnp
from jax import lax
from jax.experimental import pallas as pl
from jax.experimental.pallas import tpu as pltpu
from jax.sharding import PartitionSpec as P

BLOCK = 64
MICRO = 2


epsilon = 1e-05


def layer_norm(values_in, gain_vec, bias_vec):
    average = jnp.mean(values_in, axis=-1, keepdims=True)
    centered = values_in - average
    variance = jnp.mean(centered * centered, axis=-1, keepdims=True)
    return centered * lax.rsqrt(variance + epsilon) * gain_vec + bias_vec


def shifted(values_in, retain_marker):
    earlier = jnp.concatenate([jnp.zeros_like(values_in[:, :1]), values_in[:, :-1]], axis=1)
    return earlier * retain_marker[:, :, None]


def blend(normed, earlier, factor):
    return normed * factor + earlier * (1.0 - factor)


def project(operand, weights):
    return lax.dot_general(
        operand, weights, (((2,), (0,)), ((), ())), preferred_element_type=jnp.float32
    )


def back_project(gradient, weights):
    return lax.dot_general(
        gradient, weights, (((2,), (1,)), ((), ())), preferred_element_type=jnp.float32
    )


def weight_grad(operand, gradient):
    return lax.dot_general(
        operand, gradient, (((0, 1), (0, 1)), ((), ())), preferred_element_type=jnp.float32
    )


def take_share(array, axis_at, groups, shares, place):
    shape = array.shape
    piece_len = shape[axis_at] // (groups * shares)
    split_shape = shape[:axis_at] + (groups, shares, piece_len) + shape[axis_at + 1 :]
    chosen = lax.dynamic_index_in_dim(
        array.reshape(split_shape), place, axis_at + 1, keepdims=False
    )
    return chosen.reshape(shape[:axis_at] + (groups * piece_len,) + shape[axis_at + 1 :])


def first_piece(stream_f, gain_vec, bias_vec, factors, retain_marker):
    normed = layer_norm(stream_f, gain_vec, bias_vec)
    earlier = shifted(normed, retain_marker)
    return (
        blend(normed, earlier, factors[0]),
        blend(normed, earlier, factors[1]),
        blend(normed, earlier, factors[2]),
    )


def channel_piece(middle, gain_vec, bias_vec, factors, retain_marker):
    normed = layer_norm(middle, gain_vec, bias_vec)
    earlier = shifted(normed, retain_marker)
    return (blend(normed, earlier, factors[0]), blend(normed, earlier, factors[1]))


def time_piece(
    address_series,
    content_series,
    acceptance_gate,
    forgetting_logrates,
    present_reward,
    retain_marker,
    article_labels,
    span_length,
):
    batch_rows, length, feature_count = address_series.shape
    block_count = length // span_length
    decay_rate = jnp.exp(forgetting_logrates)
    position = jnp.arange(span_length, dtype=jnp.float32)[:, None]
    rising = jnp.exp(position * decay_rate)
    sinking = jnp.exp(-position * decay_rate)
    falling = jnp.exp(-(position + 1.0) * decay_rate)
    rising = jnp.concatenate([rising, rising], axis=-1)
    sinking = jnp.concatenate([sinking, sinking], axis=-1)
    falling = jnp.concatenate([falling, falling], axis=-1)
    whole_fade = jnp.exp(-span_length * decay_rate)
    whole_fade = jnp.concatenate([whole_fade, whole_fade], axis=-1)
    key_exp = jnp.exp(address_series)
    weighted = jnp.concatenate([key_exp * content_series, key_exp], axis=-1)
    weighted = weighted.reshape(batch_rows, block_count, span_length, 2 * feature_count)
    block_docs = article_labels.reshape(batch_rows, block_count, span_length)
    causal = jnp.arange(span_length)[:, None] >= jnp.arange(span_length)[None, :]
    same_doc = block_docs[:, :, :, None] == block_docs[:, :, None, :]
    doc_mask = (causal[None, None] & same_doc).astype(jnp.float32)
    partial_value = (
        jnp.einsum("rnji,rnid->rnjd", doc_mask, weighted * rising, precision=lax.Precision.HIGHEST)
        * sinking
    )
    last_docs = block_docs[:, :, -1]
    prior_docs = jnp.concatenate(
        [jnp.full((batch_rows, 1), -1, jnp.int32), last_docs[:, :-1]], axis=1
    )
    linked = (block_docs == prior_docs[:, :, None]).astype(jnp.float32)
    chained = linked[:, :, -1]

    def carry_step(state, pieces):
        tail_state, joined = pieces
        return (tail_state + whole_fade * joined[:, None] * state, state)

    zero_state = jnp.zeros((batch_rows, 2 * feature_count), jnp.float32)
    _, starts = lax.scan(
        carry_step,
        zero_state,
        (jnp.swapaxes(partial_value[:, :, -1], 0, 1), jnp.swapaxes(chained, 0, 1)),
    )
    starts = jnp.swapaxes(starts, 0, 1)
    states = partial_value + falling * linked[..., None] * starts[:, :, None, :]
    states = states.reshape(batch_rows, length, 2 * feature_count)
    entering_memory = shifted(states, retain_marker)
    reward_power = jnp.exp(present_reward + address_series)
    accumulated_dividend = entering_memory[..., :feature_count] + reward_power * content_series
    accumulated_divisor = entering_memory[..., feature_count:] + reward_power
    return jax.nn.sigmoid(acceptance_gate) * (accumulated_dividend / accumulated_divisor)


def general_device(
    residual_input,
    article_numbers,
    upstream_gradient,
    prenorm_scaling,
    prenorm_offset,
    postnorm_scaling,
    postnorm_offset,
    attention_blend,
    feedforward_blend,
    forgetting_logrates,
    present_reward,
    projection_matrices,
    final_matrix,
    address_matrix,
    content_matrix,
):
    batch_rows = residual_input.shape[0] // MICRO
    same_doc = article_numbers[:, 1:] == article_numbers[:, :-1]
    keep_all = jnp.concatenate([jnp.zeros_like(same_doc[:, :1]), same_doc], axis=1).astype(
        jnp.float32
    )
    groups = lax.axis_size("dp")
    shares = lax.axis_size("mp")
    mp_place = lax.axis_index("mp")
    totals = None
    outputs = []
    input_grads = []
    for micro_index in range(MICRO):
        shared = (
            lax.all_gather(prenorm_scaling, ("dp", "mp"), axis=0, tiled=True),
            lax.all_gather(prenorm_offset, ("dp", "mp"), axis=0, tiled=True),
            lax.all_gather(postnorm_scaling, ("dp", "mp"), axis=0, tiled=True),
            lax.all_gather(postnorm_offset, ("dp", "mp"), axis=0, tiled=True),
            lax.all_gather(attention_blend, ("dp", "mp"), axis=1, tiled=True),
            lax.all_gather(feedforward_blend, ("dp", "mp"), axis=1, tiled=True),
            lax.all_gather(forgetting_logrates, ("dp", "mp"), axis=0, tiled=True),
            lax.all_gather(present_reward, ("dp", "mp"), axis=0, tiled=True),
            lax.all_gather(projection_matrices, ("dp", "mp"), axis=1, tiled=True),
            lax.all_gather(final_matrix, ("dp", "mp"), axis=0, tiled=True),
        )
        local = (
            lax.all_gather(address_matrix, "dp", axis=0, tiled=True),
            lax.all_gather(content_matrix, "dp", axis=1, tiled=True),
        )
        fetched = (shared, local)
        shared, local = fetched
        gain_one, bias_one, gain_two, bias_two, tmix_w, cmix_w, decay_w, first_w, mix_w, out_w = (
            shared
        )
        key_w, value_w = local
        mix_part = take_share(mix_w[0:3], 2, groups, shares, mp_place)
        out_part = take_share(out_w, 0, groups, shares, mp_place)
        decay_part = take_share(decay_w, 0, groups, shares, mp_place)
        first_part = take_share(first_w, 0, groups, shares, mp_place)
        lower_row = micro_index * batch_rows
        upper_row = lower_row + batch_rows
        stream_f = residual_input[lower_row:upper_row].astype(jnp.float32)
        retain_marker = keep_all[lower_row:upper_row]
        article_labels = article_numbers[lower_row:upper_row]
        grad_out = upstream_gradient[lower_row:upper_row].astype(jnp.float32)

        def first_local(values_in, gain_vec, bias_vec, factors):
            return first_piece(values_in, gain_vec, bias_vec, factors, retain_marker)

        def time_local(address_series, content_series, acceptance_gate, decay_vec, first_vec):
            return time_piece(
                address_series,
                content_series,
                acceptance_gate,
                decay_vec,
                first_vec,
                retain_marker,
                article_labels,
                BLOCK,
            )

        def channel_local(values_in, gain_vec, bias_vec, factors):
            return channel_piece(values_in, gain_vec, bias_vec, factors, retain_marker)

        mixes, pull_first = jax.vjp(
            first_local,
            stream_f,
            gain_one.astype(jnp.float32),
            bias_one.astype(jnp.float32),
            tmix_w.astype(jnp.float32),
        )
        key_in = mixes[0].astype(jnp.bfloat16)
        value_in = mixes[1].astype(jnp.bfloat16)
        rec_in = mixes[2].astype(jnp.bfloat16)
        address_series = project(key_in, mix_part[0])
        content_series = project(value_in, mix_part[1])
        acceptance_gate = project(rec_in, mix_part[2])
        gated, pull_time = jax.vjp(
            time_local,
            address_series,
            content_series,
            acceptance_gate,
            decay_part.astype(jnp.float32),
            first_part.astype(jnp.float32),
        )
        gated_low = gated.astype(jnp.bfloat16)
        branch = project(gated_low, out_part)
        branch = lax.psum(branch, "mp")
        middle = stream_f + branch
        channel_ins, pull_channel = jax.vjp(
            channel_local,
            middle,
            gain_two.astype(jnp.float32),
            bias_two.astype(jnp.float32),
            cmix_w.astype(jnp.float32),
        )
        ckey_in = channel_ins[0].astype(jnp.bfloat16)
        crec_in = channel_ins[1].astype(jnp.bfloat16)
        hidden = project(ckey_in, key_w)
        active = jax.nn.relu(hidden)
        squared = (active * active).astype(jnp.bfloat16)
        carried = lax.psum(project(squared, value_w).astype(jnp.bfloat16), "mp").astype(jnp.float32)
        gate_sig = jax.nn.sigmoid(project(crec_in, mix_w[3]))
        outputs.append((middle + gate_sig * carried).astype(jnp.bfloat16))
        grad_carried = (grad_out * gate_sig).astype(jnp.bfloat16)
        grad_gate = (grad_out * carried * gate_sig * (1.0 - gate_sig)).astype(jnp.bfloat16)
        grad_value_w = weight_grad(squared, grad_carried)
        grad_hidden = (back_project(grad_carried, value_w) * 2.0 * active).astype(jnp.bfloat16)
        grad_key_w = weight_grad(ckey_in, grad_hidden)
        grad_crec_w = weight_grad(crec_in, grad_gate)
        grad_ckey = lax.psum(back_project(grad_hidden, key_w).astype(jnp.bfloat16), "mp").astype(
            jnp.float32
        )
        grad_crec = back_project(grad_gate, mix_w[3])
        grad_middle, grad_gain_two, grad_bias_two, grad_cmix = pull_channel((grad_ckey, grad_crec))
        grad_middle = grad_middle + grad_out
        grad_branch = grad_middle.astype(jnp.bfloat16)
        grad_out_w = weight_grad(gated_low, grad_branch)
        grad_gated = back_project(grad_branch, out_part)
        grad_keys, grad_values, grad_recept, grad_decay, grad_first = pull_time(grad_gated)
        grad_keys = grad_keys.astype(jnp.bfloat16)
        grad_values = grad_values.astype(jnp.bfloat16)
        grad_recept = grad_recept.astype(jnp.bfloat16)
        grad_mix_three = jnp.stack(
            [
                weight_grad(key_in, grad_keys),
                weight_grad(value_in, grad_values),
                weight_grad(rec_in, grad_recept),
            ]
        )
        grad_ins = (
            back_project(grad_keys, mix_part[0]),
            back_project(grad_values, mix_part[1]),
            back_project(grad_recept, mix_part[2]),
        )
        pulled = pull_first(grad_ins)
        pulled = (
            lax.psum(pulled[0].astype(jnp.bfloat16), "mp").astype(jnp.float32),
            lax.psum(pulled[1].astype(jnp.bfloat16), "mp").astype(jnp.float32),
            lax.psum(pulled[2].astype(jnp.bfloat16), "mp").astype(jnp.float32),
            lax.psum(pulled[3].astype(jnp.bfloat16), "mp").astype(jnp.float32),
        )
        grad_stream, grad_gain_one, grad_bias_one, grad_tmix = pulled
        input_grads.append(grad_stream + grad_middle)
        current = [
            grad_gain_one,
            grad_bias_one,
            grad_gain_two,
            grad_bias_two,
            grad_tmix,
            grad_cmix,
            grad_decay,
            grad_first,
            grad_mix_three,
            grad_crec_w,
            grad_out_w,
            grad_key_w,
            grad_value_w,
        ]
        totals = (
            current
            if totals is None
            else [earlier + latest for earlier, latest in zip(totals, current)]
        )

    def pick(gradient, axis_at):
        return take_share(gradient, axis_at, groups, shares, mp_place)

    split_grads = (
        lax.psum_scatter(pick(totals[0], 0), "dp", scatter_dimension=0, tiled=True),
        lax.psum_scatter(pick(totals[1], 0), "dp", scatter_dimension=0, tiled=True),
        lax.psum_scatter(pick(totals[2], 0), "dp", scatter_dimension=0, tiled=True),
        lax.psum_scatter(pick(totals[3], 0), "dp", scatter_dimension=0, tiled=True),
        lax.psum_scatter(pick(totals[4], 1), "dp", scatter_dimension=1, tiled=True),
        lax.psum_scatter(pick(totals[5], 1), "dp", scatter_dimension=1, tiled=True),
        lax.psum_scatter(totals[6], "dp", scatter_dimension=0, tiled=True),
        lax.psum_scatter(totals[7], "dp", scatter_dimension=0, tiled=True),
        lax.psum_scatter(totals[10], "dp", scatter_dimension=0, tiled=True),
    )
    feature_count = totals[9].shape[0]
    share_mask = jax.nn.one_hot(mp_place, shares, dtype=jnp.float32)
    three_full = (
        totals[8].reshape(3, feature_count, groups, 1, feature_count // (groups * shares))
        * share_mask[None, None, None, :, None]
    )
    three_full = three_full.reshape(3, feature_count, feature_count)
    crec_grad = totals[9] * (mp_place == 0).astype(jnp.float32)
    mix_grad = lax.psum_scatter(
        jnp.concatenate([three_full, crec_grad[None]], axis=0),
        ("dp", "mp"),
        scatter_dimension=1,
        tiled=True,
    )
    shared_grads = (
        split_grads[0],
        split_grads[1],
        split_grads[2],
        split_grads[3],
        split_grads[4],
        split_grads[5],
        split_grads[6],
        split_grads[7],
        mix_grad,
        split_grads[8],
    )
    channel_grads = (
        lax.psum_scatter(totals[11], "dp", scatter_dimension=0, tiled=True),
        lax.psum_scatter(totals[12], "dp", scatter_dimension=1, tiled=True),
    )
    output = jnp.concatenate(outputs, axis=0)
    input_grad = jnp.concatenate(input_grads, axis=0)
    return (
        output,
        input_grad,
        shared_grads[0],
        shared_grads[1],
        shared_grads[2],
        shared_grads[3],
        shared_grads[4],
        shared_grads[5],
        shared_grads[6],
        shared_grads[7],
        shared_grads[8],
        shared_grads[9],
        channel_grads[0],
        channel_grads[1],
    )


MESH = pl.DeviceIdType.MESH
MIB = 2**20

class Place:
    def __init__(self):
        self.dp = lax.axis_index("dp")
        self.mp = lax.axis_index("mp")
        self.core = self.dp % 2
        self.x = (self.dp // 2) % 2
        self.y = self.dp // 4
        self.sib = (self.dp + 1 - 2 * self.core, self.mp)
        self.xn = (self.dp + 2 - 4 * self.x, self.mp)
        self.yn = (self.dp + 4 - 8 * self.y, self.mp)
        self.up_z = (self.mp + 1) % 4
        self.down_z = (self.mp + 3) % 4
        self.far_z = (self.mp + 2) % 4
        self.up = (self.dp, self.up_z)
        self.down = (self.dp, self.down_z)
        self.pair = (self.dp, self.mp + 1 - 2 * (self.mp % 2))
        self.across = (self.dp + 6 - 4 * self.x - 8 * self.y, self.mp)


def greet(devices):
    barrier = pltpu.get_barrier_semaphore()
    for device in devices:
        pl.semaphore_signal(barrier, inc=1, device_id=device, device_id_type=MESH)
    pl.semaphore_wait(barrier, len(devices))


class Messages:
    def __init__(self, send_sem, recv_sems):
        self.send_sem, self.recv_sems, self.count, self.sent = send_sem, recv_sems, 0, []

    def send(self, source, target, arrival, device, when=None):
        index = self.count
        self.count += 1
        copy = pltpu.make_async_remote_copy(source, target, self.send_sem, self.recv_sems.at[index], device_id=device, device_id_type=MESH)
        only(when, copy.start)
        self.sent.append((when, copy))
        return pltpu.make_async_remote_copy(arrival, arrival, self.send_sem, self.recv_sems.at[index], device_id=device, device_id_type=MESH)

    def finish(self):
        for when, copy in self.sent:
            only(when, copy.wait_send)
        self.sent = []


def only(when, action):
    if when is None:
        action()
    else:
        pl.when(when)(action)


ALL = slice(None)


class Stream:
    def __init__(self, place, messages, order, piece, own, twin_sem):
        self.p, self.msg, self.order, self.piece, self.own, self.twin_sem = place, messages, order, piece, own, twin_sem
        p = place
        self.first = order.replace("z", "")[0]
        self.z_leads = order[0] == "z"
        self.a, self.b = (p.x, p.y) if self.first == "x" else (p.y, p.x)
        self.na, self.nb = (p.xn, p.yn) if self.first == "x" else (p.yn, p.xn)
        self.base = messages.count
        messages.count += 15

    def at(self, col, other, slab, core=None):
        a = self.a if col == 0 else 1 - self.a
        b = 1 - self.b if other else self.b
        y, x = (b, a) if self.first == "x" else (a, b)
        return self.piece(y, x, self.p.core if core is None else core, slab)

    def slab(self, j):
        m = self.p.mp
        if j == 0:
            return m
        flip = (m >= 2).astype(jnp.int32)
        near = m + flip * (3 - 2 * m)
        picked = j - (j <= near).astype(jnp.int32)
        return picked + flip * (3 - 2 * picked)

    def rank(self, m, slab):
        flip = (m >= 2).astype(jnp.int32)
        near = m + flip * (3 - 2 * m)
        picked = slab + flip * (3 - 2 * slab)
        return picked - (picked > near).astype(jnp.int32) + 1

    def index(self, kind, col, j):
        if self.z_leads:
            return self.base + {"z": j - 1, "a": 3 + j, "b": 7 + 4 * col + j}[kind]
        return self.base + {"z": 3 * col + j - 1, "a": 6, "b": 7 + 4 * col + j}[kind]

    def copy(self, piece, index, device, when=None, source=None):
        copy = pltpu.make_async_remote_copy(
            piece if source is None else source, piece, self.msg.send_sem, self.msg.recv_sems.at[index],
            device_id=device, device_id_type=MESH,
        )
        only(when, copy.start)
        self.msg.sent.append((when, copy))

    def twin(self, col, other, slab, source=None):
        piece = self.at(col, other, slab)
        sem = self.twin_sem(slab)
        copy = pltpu.make_async_remote_copy(
            piece if source is None else source, piece, self.msg.send_sem, sem,
            device_id=self.p.sib, device_id_type=MESH,
        )
        copy.start()
        self.msg.sent.append((None, copy))

    def send_z(self, col, j, source=None):
        m = self.p.mp
        slab = self.slab(j)
        piece = self.at(col, 0, slab)
        if j == 0:
            self.copy(piece, self.index("z", col, 1) + self.rank(m + 1, slab) - 1, self.p.up, m < 3, source)
            self.copy(piece, self.index("z", col, 1) + self.rank(m - 1, slab) - 1, self.p.down, m > 0, source)
            return
        target = m - 1 + 2 * (slab < m).astype(jnp.int32)
        safe = (target + 4) % 4
        self.copy(piece, self.index("z", col, 1) + self.rank(target, slab) - 1, (self.p.dp, safe), (target >= 0) & (target <= 3))

    def send_a(self, j, source=None):
        self.copy(self.at(0, 0, self.slab(j)), self.index("a", 0, j), self.na, source=source)

    def send_b(self, col, j, source=None):
        self.copy(self.at(col, 0, self.slab(j)), self.index("b", col, j), self.nb, source=source)

    def event(self, kind, col, j):
        if kind == "o":
            self.send_z(0, 0, self.own)
            self.send_a(0, self.own)
            self.send_b(0, 0, self.own)
            self.twin(0, 0, self.p.mp, self.own)
            return
        slab = self.slab(j)
        piece = self.at(1 if kind == "a" else col, kind == "b", slab)
        sem = self.msg.recv_sems.at[self.index(kind, col, j)]
        pltpu.make_async_remote_copy(piece, piece, self.msg.send_sem, sem, device_id=self.na, device_id_type=MESH).wait_recv()
        if kind == "z":
            self.send_z(col, j)
            if self.z_leads:
                self.send_a(j)
            self.send_b(col, j)
            self.twin(col, 0, slab)
        elif kind == "a":
            if not self.z_leads:
                self.send_z(1, 0)
            self.send_b(1, j)
            self.twin(1, 0, slab)
        else:
            self.twin(col, 1, slab)


PARTS = (
    ("t", 0, 48, "zxy"),
    ("t", 48, 32, "zyx"),
    ("t", 80, 48, "xzy"),
    ("k", 0, 96, "yzx"),
    ("v", 0, 96, "zxy"),
)
EVENTS = {
    "own": ("1o00", "0o00", "2o00", ),
    "relayA": ("1z01", "0z01", "0z02", "1z02", "0a00", "1z03", "1b01", "1a01", "0z03", "2b00", "0a01", "1b00", "1a00", "2a00", "3o00", "2z12", "0b02", "0a02", "0a03", "1b03", "1a03", "1b11", "1a02", "0b01", "1b10", "3z02", "4o00", "0b00", "1b02", "2z01", "2z11", "0b11", "1b13", "2b10", "3z01", "3a00", "1b12", "0b10", "2z02", "0b12", "0b03", "3b02", "0b13", "2z03", "4z01", ),
    "a0.0": ("2z13", ),
    "a0.1": ("3b00", "2b12", "3b01", "4a00", "4z02", ),
    "a0.2": (),
    "a1.0": (),
    "a1.1": ("4z03", "2b01", "3z11", ),
    "a1.2": (),
    "a2.0": (),
    "a2.1": (),
    "a2.2": (),
    "a3.0": ("3z12", "3b10", ),
    "a3.1": ("2b13", ),
    "a3.2": ("4a02", "2b02", "2b03", "2b11", "4b01", "3z13", ),
    "relayB": (),
    "b0.0": (),
    "b0.1": ("3z03", ),
    "b1.0": ("4a03", ),
    "b1.1": ("3b12", ),
    "b2.0": (),
    "b2.1": ("4b02", ),
    "b3.0": ("4b03", "4b12", "4b00", "4b10", ),
    "b3.1": (),
    "h0": ("3b13", "3b11", "4b13", "4a01", "3b03", ),
    "h1": (),
    "h2": (),
    "h3": ("4b11", ),
    "c0": (),
    "c1": (),
    "c2": (),
    "c3": (),
    "fin": (),
    "end": (),
}


def streams(place, messages, twin_sems, pk, kw, vt, tw, kg, vg):
    def piece_of(name, start, rows):
        if name == "t":
            return lambda y, x, c, m: tw.at[y, x, c, m, pl.ds(start, rows)]
        array = kg if name == "k" else vg
        return lambda y, x, c, m: array.at[m, y, x, c, pl.ds(start, rows)]

    made = []
    for name, start, rows, order in PARTS:
        own = {"t": pk, "k": kw, "v": vt}[name].at[pl.ds(start, rows)]
        if name == "t":
            twin = lambda slab, i=start // 80: twin_sems.at[i]
        else:
            twin = lambda slab, i=2 if name == "k" else 6: twin_sems.at[i + slab]
        made.append(Stream(place, messages, order, piece_of(name, start, rows), own, twin))
    return made


def play(made, marker):
    for event in EVENTS[marker]:
        made[int(event[0])].event(event[1], int(event[2]), int(event[3]))


def greet_all(p):
    barrier = pltpu.get_barrier_semaphore()
    for device in (p.sib, p.xn, p.yn):
        pl.semaphore_signal(barrier, inc=1, device_id=device, device_id_type=MESH)
    only(p.mp < 3, lambda: pl.semaphore_signal(barrier, inc=1, device_id=p.up, device_id_type=MESH))
    only(p.mp > 0, lambda: pl.semaphore_signal(barrier, inc=1, device_id=p.down, device_id_type=MESH))
    pl.semaphore_wait(barrier, 3 + (p.mp < 3).astype(jnp.int32) + (p.mp > 0).astype(jnp.int32))


TILE = 256
SPAN = 128
WIDE = 512


def dot(a, b):
    return jnp.dot(a, b, preferred_element_type=jnp.float32)


def dot_nt(a, b):
    return lax.dot_general(a, b, (((1,), (1,)), ((), ())), preferred_element_type=jnp.float32)


def dot_tn(a, b):
    return lax.dot_general(a, b, (((0,), (0,)), ((), ())), preferred_element_type=jnp.float32)


def low(values):
    return values.astype(jnp.bfloat16)


def wide(values):
    return values.astype(jnp.float32)


def row_sums(values):
    rows, width = values.shape
    return jnp.sum(values.reshape(rows // 8, 8, width), axis=0)


def standardise(values):
    centered = values - jnp.mean(values, axis=-1, keepdims=True)
    variance = jnp.mean(centered * centered, axis=-1, keepdims=True)
    scale = lax.rsqrt(variance + epsilon)
    return centered * scale, scale


def norm_back(grad, normal, scale):
    mean_grad = jnp.mean(grad, axis=-1, keepdims=True)
    mean_both = jnp.mean(grad * normal, axis=-1, keepdims=True)
    return scale * (grad - mean_grad - normal * mean_both)


def later(values, first_row):
    row = lax.broadcasted_iota(jnp.int32, values.shape, 0)
    return jnp.where(row == 0, first_row, pltpu.roll(values, 1, 0))


def sooner(values, last_row):
    rows = values.shape[0]
    row = lax.broadcasted_iota(jnp.int32, values.shape, 0)
    return jnp.where(row == rows - 1, last_row, pltpu.roll(values, rows - 1, 0))


def halves(target, values):
    for span in range(values.shape[0] // SPAN):
        part = values[span * SPAN : (span + 1) * SPAN]
        high = low(part)
        target[span, 0:SPAN, :] = high
        target[span, SPAN : 2 * SPAN, :] = low(part - wide(high))


GAIN1, BIAS1, GAIN2, BIAS2, MIX, DECAY, FIRST, BLEND = 0, 1, 2, 3, 4, 7, 8, 9


def vec(ref, index):
    return ref[index : index + 1, :]


def rows_at(start, count):
    return pl.ds(pl.multiple_of(start, 128), count)


def pack_block(p, proj, final, vectors, pk):
    spread = jnp.concatenate([wide(vectors[...]), jnp.zeros((16, 256), jnp.float32)], axis=1)
    spread = pltpu.roll(spread, 24 * ((4 * p.dp + p.mp) % 16), 1)
    spread = jnp.concatenate([spread[:8], spread[8:]], axis=1)
    rows = [wide(proj[0]), wide(proj[1]), wide(proj[2]), spread, wide(proj[3]), wide(final[...])]
    pk[...] = low(jnp.concatenate(rows, axis=0))


def row_of(docs, row):
    return wide(jnp.where(row == 0, docs[0:1, :], docs[1:2, :]))


def describe(docs, row, cols):
    own = row_of(docs, row)
    lane = lax.broadcasted_iota(jnp.int32, own.shape, 1)
    keep = jnp.where((lane > 0) & (own == pltpu.roll(own, 1, 1)), 1.0, 0.0)
    spans = own.shape[1] // SPAN
    none = jnp.zeros((1, SPAN), jnp.float32)
    for i in range(spans):
        part = own[:, i * SPAN : (i + 1) * SPAN]
        before = after = none
        if i > 0:
            before = jnp.where(part == own[:, i * SPAN - 1 : i * SPAN], 1.0, 0.0)
        if i < spans - 1:
            after = jnp.where(part == own[:, (i + 1) * SPAN : (i + 1) * SPAN + 1], 1.0, 0.0)
        rows = [part, keep[:, i * SPAN : (i + 1) * SPAN], before, after, jnp.zeros((SPAN - 4, SPAN), jnp.float32)]
        cols[i * SPAN : (i + 1) * SPAN, :] = jnp.concatenate(rows, axis=0).T


def forward_kernel(
    proj, final, vectors, kw, vt, docs, x_any, gy_any,
    kg, vg, acts, kvs, middle_o, sq_o, act_o, grads_o, out_o, wts_o, vecs_o, cols_o,
    w5, kv, sa, xb, st, f5, mid, sig, tables, vecs, prev, cols, split, pk, sems, twin_sems, send_sem, recv_sems,
):
    place_of = Place()
    p = place_of
    row = p.mp % 2
    load_x = pltpu.make_async_copy(x_any.at[row], xb, sems.at[0])
    load_x.start()
    pack_block(p, proj, final, vectors, pk)
    keep = [
        pltpu.make_async_copy(pk, sa.at[p.y, p.x, p.core, p.mp], sems.at[26]),
        pltpu.make_async_copy(kw, kg.at[p.mp, p.y, p.x, p.core], sems.at[27]),
        pltpu.make_async_copy(vt, vg.at[p.mp, p.y, p.x, p.core], sems.at[28]),
    ]
    for copy in keep:
        copy.start()
    greet_all(place_of)
    messages = Messages(send_sem, recv_sems)
    made = streams(place_of, messages, twin_sems, pk, kw, vt, sa, kg, vg)

    def twins(i, half):
        pltpu.make_async_copy(half, half, twin_sems.at[i]).wait()

    def time_twins(i):
        twins(i, sa.at[:, :, 1 - p.core, :, (pl.ds(0, 80), pl.ds(80, 48))[i]])

    prev[...] = jnp.zeros_like(prev)
    play(made, "own")
    describe(docs, row, cols)
    own_docs = row_of(docs, row)
    play(made, "relayA")
    for copy in keep:
        copy.wait()
    time_twins(0)

    def relay(half, first_row, count, slots):
        def body(i, total):
            core, m = i // 2, 2 * (i % 2)
            pair = 8 * half + i
            spot = half, i // 4, core % 2
            rows = pl.ds(first_row, count)
            one, two = wide(sa[spot + (m, rows)]), wide(sa[spot + (m + 1, rows)])
            for n, j in enumerate(slots):
                piece = jnp.concatenate([one[24 * n : 24 * n + 24], two[24 * n : 24 * n + 24]], axis=0)
                w5[j, pl.ds(pl.multiple_of(48 * pair, 16), 48), :] = low(piece)
            return total + one[count - 8 :] + two[count - 8 :]

        return lax.fori_loop(0, 8, body, jnp.zeros((8, 768), jnp.float32))

    left, right = relay(0, 0, 80, (0, 1, 2)), relay(1, 0, 80, (0, 1, 2))
    vecs[0:8, :] = jnp.concatenate([left[:, :384], right[:, :384]], axis=1)
    vecs[8:16, :] = jnp.concatenate([left[:, 384:], right[:, 384:]], axis=1)
    save_v = pltpu.make_async_copy(vecs, vecs_o, sems.at[11])
    save_v.start()

    rate = jnp.exp(vec(vecs, DECAY))
    fade = jnp.exp(-rate)
    place = wide(lax.broadcasted_iota(jnp.int32, (TILE, 1), 0) % SPAN)
    tables[0] = jnp.exp((place - 64.0) * rate)
    tables[1] = jnp.exp((65.0 - place) * rate)
    tables[2] = jnp.exp(-place * rate)
    load_x.wait()
    tiles = [(t, t * TILE, pl.ds(t * TILE, TILE)) for t in range(1024 // TILE)]
    for t, base, r in tiles:
        play(made, f"a{t}.0")

        def first(q, last):
            x = wide(xb[q, :])
            mean = jnp.mean(x, axis=-1, keepdims=True)
            centered = x - mean
            scale = lax.rsqrt(jnp.mean(centered * centered, axis=-1, keepdims=True) + epsilon)
            cols[q, 4:5] = mean
            cols[q, 5:6] = scale
            normed = centered * scale * vec(vecs, GAIN1) + vec(vecs, BIAS1)
            earlier = later(normed, last) * cols[q, 1:2]
            delta = normed - earlier
            for j in range(3):
                st[j, q, :] = low(earlier + delta * vec(vecs, MIX + j))
            st[6, q, :] = low(delta)
            return normed[TILE - 1 :]

        prev[0:1, :] = first(r, prev[0:1, :])
        for j in range(3):
            f5[j, r, :] = dot(st[j, r, :], w5[j])
        play(made, f"a{t}.1")

        key_exp = jnp.exp(f5[0, r, :])
        f5[2, r, :] = jax.nn.sigmoid(f5[2, r, :])
        grown = key_exp * tables[0]
        halves(split.at[0], grown * f5[1, r, :])
        halves(split.at[1], grown)
        time = lax.broadcasted_iota(jnp.int32, (SPAN, SPAN), 0)
        source = lax.broadcasted_iota(jnp.int32, (SPAN, SPAN), 1)
        for i in range(TILE // SPAN):
            block = t * (TILE // SPAN) + i
            same = cols[pl.ds(block * SPAN, SPAN), 0:1] == own_docs[:, block * SPAN : (block + 1) * SPAN]
            mask = jnp.where(same & (source < time), 1.0, 0.0).astype(jnp.bfloat16)
            mask = jnp.concatenate([mask, mask], axis=1)
            for k in range(2):
                f5[3 + k, pl.ds(block * SPAN, SPAN), :] = dot(mask, split[k, i])
        play(made, f"a{t}.2")
        for i in range(TILE // SPAN):
            begin = base + i * SPAN
            top_in, bottom_in = prev[2:3, :], prev[3:4, :]

            q = pl.ds(begin, SPAN)
            values = f5[1, q, :]
            link = cols[q, 2:3] * tables[2, 0:SPAN, :]
            top = f5[3, q, :] * tables[1, 0:SPAN, :] + link * top_in
            bottom = f5[4, q, :] * tables[1, 0:SPAN, :] + link * bottom_in
            f5[3, q, :] = top
            f5[4, q, :] = bottom
            bonus = jnp.exp(f5[0, q, :] + vec(vecs, FIRST))
            st[3, q, :] = low(f5[2, q, :] * ((top + bonus * values) / (bottom + bonus)))
            end = begin + SPAN - 1
            key_exp = jnp.exp(f5[0, end : end + 1, :])
            prev[2:3, :] = fade * f5[3, end : end + 1, :] + key_exp * f5[1, end : end + 1, :]
            prev[3:4, :] = fade * f5[4, end : end + 1, :] + key_exp
    saves = [pltpu.make_async_copy(f5, kvs, sems.at[16])]
    saves[0].start()
    play(made, "relayB")
    time_twins(1)
    relay(0, 80, 48, (3, 4))
    relay(1, 80, 48, (3, 4))
    save_w = pltpu.make_async_copy(w5, wts_o, sems.at[10])
    save_w.start()
    for t, base, r in tiles:
        play(made, f"b{t}.0")
        mid[r, :] = dot(st[3, r, :], w5[4])

        def fourth(q, last):
            middle = wide(xb[q, :]) + mid[q, :]
            mid[q, :] = middle
            mean = jnp.mean(middle, axis=-1, keepdims=True)
            centered = middle - mean
            scale = lax.rsqrt(jnp.mean(centered * centered, axis=-1, keepdims=True) + epsilon)
            cols[q, 6:7] = mean
            cols[q, 7:8] = scale
            normed = centered * scale * vec(vecs, GAIN2) + vec(vecs, BIAS2)
            earlier = later(normed, last) * cols[q, 1:2]
            delta = normed - earlier
            for j in range(2):
                st[4 + j, q, :] = low(earlier + delta * vec(vecs, BLEND + j))
            st[7, q, :] = low(delta)
            return normed[TILE - 1 :]

        prev[1:2, :] = fourth(r, prev[1:2, :])
        play(made, f"b{t}.1")
        sig[r, :] = dot(st[5, r, :], w5[3])
        saves += [
            pltpu.make_async_copy(st.at[:, r], acts.at[:, r], sems.at[12 + t]),
            pltpu.make_async_copy(mid.at[r], middle_o.at[r], sems.at[20 + t]),
        ]
        for copy in saves[-2:]:
            copy.start()
    saves.append(pltpu.make_async_copy(cols, cols_o, sems.at[36]))
    saves[-1].start()
    load_gy = pltpu.make_async_copy(gy_any.at[row], xb, sems.at[24])
    load_gy.start()
    messages.finish()

    def load_kv(m, which, array):
        target = kv.at[m]
        return pltpu.make_async_copy(array.at[m], target, sems.at[4 * which + 1 + m])

    pending = {}
    for m in range(4):
        play(made, f"h{m}")
        if m == 0:
            for slab in range(4):
                twins(2 + slab, kg.at[slab, :, :, 1 - p.core])
                load_kv(slab, 0, kg).start()
        load_kv(m, 0, kg).wait()
        if m == 0:
            for copy in saves:
                copy.wait()

        def hidden(t, carry):
            r = rows_at(t * WIDE, WIDE)
            active = jnp.maximum(dot(st[4, r, :], kv[m].reshape(768, 768)), 0.0)
            squared = low(active * active)
            spot = m // 2, m % 2, t
            sa[spot] = squared.reshape(4, 128, 768)
            st[m, r, :] = low(active)
            return carry

        lax.fori_loop(0, 1024 // WIDE, hidden, 0)
        pending[m] = pltpu.make_async_copy(st.at[m], act_o.at[m], sems.at[29 + m])
        pending[m].start()
    save_sq = pltpu.make_async_copy(sa, sq_o, sems.at[33])
    save_sq.start()
    pair = p.mp // 2
    for turn in range(2):
        play(made, f"c{2 * turn}")
        at = pair if turn == 0 else 1 - pair
        loads = []
        for i in range(2):
            slab = 2 * at + i
            twins(6 + slab, vg.at[slab, :, :, 1 - p.core])
            loads.append(pltpu.make_async_copy(vg.at[slab], kv.at[2 * turn + i], sems.at[5 + 2 * turn + i]))
            loads[-1].start()
        for i in range(2):
            loads[i].wait()
            if i == 1:
                play(made, f"c{2 * turn + 1}")

            def content(t, carry):
                r = rows_at(t * WIDE, WIDE)
                squared = sa[at, i, t].reshape(WIDE, 768)
                part = dot_nt(squared, kv[2 * turn + i].reshape(768, 768))
                f5[turn, r, :] = part if i == 0 else f5[turn, r, :] + part
                return carry

            lax.fori_loop(0, 1024 // WIDE, content, 0)

    play(made, "fin")
    play(made, "end")
    load_gy.wait()

    last = []
    for t, _, q in tiles:
        gate = jax.nn.sigmoid(sig[q, :])
        carried = f5[0, q, :] + f5[1, q, :]
        st[5, q, :] = low(mid[q, :] + gate * carried)
        passed = wide(xb[q, :]) * gate
        st[6, q, :] = low(passed)
        st[7, q, :] = low(passed * carried * (1.0 - gate))
        last += [
            pltpu.make_async_copy(st.at[5, q], out_o.at[q], sems.at[37 + t]),
            pltpu.make_async_copy(st.at[pl.ds(6, 2), q], grads_o.at[:, q], sems.at[41 + t]),
        ]
        for copy in last[-2:]:
            copy.start()
    save_w.wait()
    save_v.wait()
    save_sq.wait()
    for m in range(4):
        pending.pop(m).wait()
    messages.finish()
    for copy in last:
        copy.wait()


ANY = pl.BlockSpec(memory_space=pl.ANY)
ON_CORE = pl.BlockSpec(memory_space=pltpu.VMEM)
LIMIT = 63 * MIB


def forward(proj, final, vectors, kw, vt, docs, x, gy):
    bf, f32 = jnp.bfloat16, jnp.float32
    shape = jax.ShapeDtypeStruct
    return pl.pallas_call(
        forward_kernel,
        out_shape=(
            shape((4, 2, 2, 2, 96, 768), bf), shape((4, 2, 2, 2, 96, 768), bf),
            shape((8, 1024, 768), bf), shape((5, 1024, 768), f32), shape((1024, 768), f32),
            shape((2, 2, 2, 4, 128, 768), bf), shape((4, 1024, 768), bf), shape((2, 1024, 768), bf),
            shape((1024, 768), bf), shape((5, 768, 768), bf), shape((16, 768), f32), shape((1024, 128), f32),
        ),
        in_specs=[ON_CORE] * 6 + [ANY] * 2,
        out_specs=[ANY] * 12,
        scratch_shapes=[
            pltpu.VMEM((5, 768, 768), bf), pltpu.VMEM((4, 2, 2, 2, 96, 768), bf), pltpu.VMEM((2, 2, 2, 4, 128, 768), bf),
            pltpu.VMEM((1024, 768), bf), pltpu.VMEM((8, 1024, 768), bf), pltpu.VMEM((5, 1024, 768), f32),
            pltpu.VMEM((1024, 768), f32), pltpu.VMEM((1024, 768), f32),
            pltpu.VMEM((3, TILE, 768), f32), pltpu.VMEM((16, 768), f32), pltpu.VMEM((8, 768), f32),
            pltpu.VMEM((1024, 128), f32), pltpu.VMEM((2, 2, 2 * SPAN, 768), bf), pltpu.VMEM((128, 768), bf),
            pltpu.SemaphoreType.DMA((45,)), pltpu.SemaphoreType.DMA((10,)), pltpu.SemaphoreType.DMA,
            pltpu.SemaphoreType.DMA((15 * len(PARTS),)),
        ],
        compiler_params=pltpu.CompilerParams(vmem_limit_bytes=LIMIT, collective_id=0, has_side_effects=True),
        name="forward",
    )(proj, final, vectors, kw, vt, docs, x, gy)


class Scatter:
    def __init__(self, place, messages, source, received, kept, steps, final, orders):
        self.p, self.msg = place, messages
        self.source, self.received, self.kept, self.steps, self.final = source, received, kept, steps, final
        self.orders = orders
        self.parts = len(orders)
        self.core_waits, self.waits = {}, []

    def cols(self, part):
        width = self.kept.shape[-1] // self.parts
        return pl.ds(part * width, width)

    def start(self, j):
        p = self.p
        target = self.received.at[:, j]
        self.core_waits[j] = self.msg.send(self.source.at[:, j, :, :, 1 - p.core], target, target, p.sib)

    def core(self, j):
        p = self.p
        self.core_waits[j].wait_recv()
        for i in range(self.kept.shape[0]):
            for y in range(2):
                for x in range(2):
                    self.kept[i, j, y, x] = self.source[i, j, y, x, p.core] + self.received[i, j, y, x]
        self.send(0, j)

    def index(self, order, step, flip):
        p = self.p
        mine = {"x": p.x, "y": p.y, "j": p.mp % 2}
        picked = {}
        for at, axis in enumerate(order):
            if at < step:
                picked[axis] = mine[axis]
            elif at == step:
                picked[axis] = 1 - mine[axis] if flip else mine[axis]
            else:
                picked[axis] = None
        return picked

    def send(self, step, j=None):
        p = self.p
        device = {"x": p.xn, "y": p.yn, "j": p.pair}
        if step > 0:
            self.waits = []
        for part in range(self.parts):
            order = self.orders[part]
            picked = self.index(order, step, True)
            target = self.steps[step].at[part]
            if j is not None:
                picked["j"] = j
                target = self.steps[step].at[part, :, j]
            select = tuple(ALL if picked[a] is None else picked[a] for a in "jyx")
            piece = self.kept.at[(ALL,) + select + (ALL, self.cols(part))]
            self.waits.append(self.msg.send(piece, target, target, device[order[step]]))

    def add(self, step, last=False):
        for wait in self.waits:
            wait.wait_recv()
        for part in range(self.parts):
            picked = self.index(self.orders[part], step, False)
            free = [a for a in "jyx" if picked[a] is None]
            for i in range(self.kept.shape[0]):
                for number in range(2 ** len(free)):
                    bits = {a: (number >> (len(free) - 1 - k)) & 1 for k, a in enumerate(free)}
                    select = tuple(bits[a] if picked[a] is None else picked[a] for a in "jyx")
                    spot = (i,) + select + (ALL, self.cols(part))
                    arrived = self.steps[step][(part, i) + tuple(bits[a] for a in free)]
                    if step == 2:
                        self.final[i, :, self.cols(part)] = wide(self.kept[spot]) + wide(arrived)
                    else:
                        self.kept[spot] = self.kept[spot] + arrived
        if step < 2 and not last:
            self.send(step + 1)


class Plane:
    def __init__(self, place, messages, source, received, kept, arrived, last, final):
        self.p, self.msg = place, messages
        self.source, self.received, self.kept, self.arrived, self.last, self.final = source, received, kept, arrived, last, final

    def start(self):
        p = self.p
        self.wait = self.msg.send(self.source.at[:, :, :, 1 - p.core], self.received, self.received, p.sib)

    def core(self):
        p, kept = self.p, self.kept
        self.wait.wait_recv()
        for j in range(2):
            for y in range(2):
                for x in range(2):
                    kept[j, y, x] = self.source[j, y, x, p.core] + self.received[j, y, x]
        pieces = (
            (kept.at[:, 1 - p.y, 1 - p.x], p.across), (kept.at[:, p.y, 1 - p.x], p.xn), (kept.at[:, 1 - p.y, p.x], p.yn),
        )
        self.waits = [
            self.msg.send(piece, self.arrived.at[n], self.arrived.at[n], device) for n, (piece, device) in enumerate(pieces)
        ]

    def plane(self):
        p, kept = self.p, self.kept
        for wait in self.waits:
            wait.wait_recv()
        for j in range(2):
            total = wide(kept[j, p.y, p.x])
            for n in range(3):
                total += wide(self.arrived[n, j])
            kept[j, p.y, p.x] = total.astype(kept.dtype)
        self.wait = self.msg.send(kept.at[1 - p.mp % 2, p.y, p.x], self.last, self.last, p.pair)

    def z(self):
        p = self.p
        self.wait.wait_recv()
        self.final[...] = wide(self.kept[p.mp % 2, p.y, p.x]) + wide(self.last[...])


def plane_scratch(rows, cols, dtype):
    return [
        pltpu.VMEM((2, 2, 2, rows, cols), dtype), pltpu.VMEM((2, 2, 2, rows, cols), dtype),
        pltpu.VMEM((3, 2, rows, cols), dtype), pltpu.VMEM((rows, cols), dtype),
    ]


def channel_back_kernel(
    kg, vg, wts, acts, sq, act, grads, middle, gy_any, out_row, cols, vecs,
    gm_o, kept_o, out_o, sums_o,
    kv, sqs, acs, gcg, cc, dh, acc, wg, mid, gy, gm, delta, stage, gate_w, sums, nxt, result, received, kept, first_step, sems, send_sem, recv_sems,
):
    place = Place()
    mp = place.mp
    row, pair = mp % 2, mp // 2
    load_row = pltpu.make_async_copy(out_row, result, sems.at[22])
    load_row.start()
    greet([place.sib, place.xn, place.yn, place.pair])
    messages = Messages(send_sem, recv_sems)
    arrival = messages.send(out_row, out_o.at[row], out_o.at[1 - row], place.pair)
    load_row.wait()
    channel = Scatter(place, messages, stage, received, kept, [first_step], None, ("xyj", "yxj"))
    keep_row = pltpu.make_async_copy(result, out_o.at[row], sems.at[21])
    keep_row.start()
    order = [2 * pair, 2 * pair + 1, 2 - 2 * pair, 3 - 2 * pair]

    def loads(j):
        m, slot = order[j], j % 2
        copies = [
            pltpu.make_async_copy(kg.at[m], kv.at[0, slot], sems.at[3 * j]),
            pltpu.make_async_copy(vg.at[m], kv.at[1, slot], sems.at[3 * j + 1]),
            pltpu.make_async_copy(act.at[m], acs.at[slot], sems.at[3 * j + 2]),
        ]
        return copies

    load_g = pltpu.make_async_copy(grads, gcg, sems.at[12])
    load_g.start()
    others = [
        pltpu.make_async_copy(sq.at[pl.ds(2 * pair, 2)], sqs, sems.at[13]),
        pltpu.make_async_copy(acts.at[pl.ds(4, 2)], cc, sems.at[14]),
        pltpu.make_async_copy(wts.at[3], wg, sems.at[15]),
        pltpu.make_async_copy(middle, mid, sems.at[16]),
        pltpu.make_async_copy(acts.at[7], delta, sems.at[19]),
        pltpu.make_async_copy(gy_any.at[row], gy, sems.at[17]),
    ]
    for copy in [others[1]] + loads(0) + [others[0]] + loads(1) + others[2:]:
        copy.start()
    load_g.wait()
    others[1].wait()

    def gate_weights(t, carry):
        c = pl.ds(pl.multiple_of(t * 384, 128), 384)
        gate_w[c, :] = dot_tn(cc[1, :, c], gcg[1])
        return carry

    lax.fori_loop(0, 2, gate_weights, 0)

    def gate_pack(dp, carry):
        for j in range(2):
            start = pl.multiple_of(96 * dp + 48 * pair + 24 * j, 8)
            piece = jnp.concatenate([gate_w[pl.ds(start, 24), :], jnp.zeros((8, 768), jnp.float32)], axis=0)
            stage[0, j, dp // 4, (dp // 2) % 2, dp % 2, 192:224, :] = low(piece)
        return carry

    lax.fori_loop(0, 8, gate_pack, 0)
    for j in range(4):
        slot = j % 2
        for copy in loads(j):
            copy.wait()

        def hidden_back(t, carry):
            r = rows_at(t * WIDE, WIDE)
            active = wide(acs[slot, r, :])
            grad = low(dot(gcg[0, r, :], kv[1, slot]) * (2.0 * active))
            if j < 2:
                dh[j, r, :] = grad
            part = dot_nt(grad, kv[0, slot])
            acc[j // 2, r, :] = part if j % 2 == 0 else acc[j // 2, r, :] + part
            return carry

        lax.fori_loop(0, 1024 // WIDE, hidden_back, 0)
        if j < 2:
            for copy in loads(j + 2):
                copy.start()
            if j == 0:
                others[0].wait()
            else:
                channel.core(0)

            def weights(t, carry):
                c = pl.ds(pl.multiple_of(t * 384, 128), 384)
                key = low(dot_tn(cc[0, :, c], dh[j]))
                stage[0, j, t, :, :, 0:96, :] = key.reshape(2, 2, 96, 768)
                value = low(dot_tn(gcg[0, :, c], sqs[j].reshape(1024, 768)))
                stage[0, j, t, :, :, 96:192, :] = value.reshape(2, 2, 96, 768)
                return carry

            lax.fori_loop(0, 2, weights, 0)
            channel.start(j)
        elif j == 2:
            channel.core(1)
            for copy in others[2:]:
                copy.wait()

    sums[...] = jnp.zeros_like(sums)
    nxt[...] = jnp.zeros_like(nxt)

    def gate_back(t, carry):
        r = rows_at(t * WIDE, WIDE)
        gm[r, :] = dot_nt(gcg[1, r, :], wg[...])
        return carry

    lax.fori_loop(0, 1024 // WIDE, gate_back, 0)
    gain = vec(vecs, GAIN2)
    key_mix, rec_mix = vec(vecs, BLEND), vec(vecs, BLEND + 1)

    def tokens(n, state):
        q = rows_at((1024 // TILE - 1 - n) * TILE, TILE)
        grad_key, grad_rec = acc[0, q, :] + acc[1, q, :], gm[q, :]
        step = wide(delta[q, :])
        sums[2] += row_sums(grad_key * step)
        sums[3] += row_sums(grad_rec * step)
        grad = grad_key * key_mix + grad_rec * rec_mix
        back = (grad_key + grad_rec - grad) * cols[q, 1:2]
        grad = grad + sooner(back, state)
        scale = cols[q, 7:8]
        normal = (mid[q, :] - cols[q, 6:7]) * scale
        sums[0] += row_sums(grad * normal)
        sums[1] += row_sums(grad)
        gm[q, :] = wide(gy[q, :]) + norm_back(grad * gain, normal, scale)
        return back[0:1]

    lax.fori_loop(0, 1024 // TILE, tokens, jnp.zeros((1, 768), jnp.float32))
    store_gm = pltpu.make_async_copy(gm, gm_o, sems.at[20])
    store_gm.start()
    for i in range(4):
        sums_o[i : i + 1, :] = jnp.sum(sums[i], axis=0, keepdims=True)
    sums_o[4:8, :] = jnp.zeros((4, 768), jnp.float32)
    channel.add(0, last=True)
    store = pltpu.make_async_copy(kept, kept_o, sems.at[18])
    store.start()
    store.wait()
    store_gm.wait()
    keep_row.wait()
    arrival.wait_recv()
    messages.finish()


def channel_back(kg, vg, wts, acts, sq, act, grads, middle, gy, out_row, cols, vecs):
    bf, f32 = jnp.bfloat16, jnp.float32
    shape = jax.ShapeDtypeStruct
    return pl.pallas_call(
        channel_back_kernel,
        out_shape=(
            shape((1024, 768), f32), shape((1, 2, 2, 2, 224, 768), bf),
            shape((2, 1024, 768), bf), shape((8, 768), f32),
        ),
        in_specs=[ANY] * 10 + [ON_CORE] * 2,
        out_specs=[ANY] * 3 + [ON_CORE],
        scratch_shapes=[
            pltpu.VMEM((2, 2, 768, 768), bf), pltpu.VMEM((2, 8, 128, 768), bf), pltpu.VMEM((2, 1024, 768), bf),
            pltpu.VMEM((2, 1024, 768), bf), pltpu.VMEM((2, 1024, 768), bf), pltpu.VMEM((2, 1024, 768), bf),
            pltpu.VMEM((2, 1024, 768), f32), pltpu.VMEM((768, 768), bf), pltpu.VMEM((1024, 768), f32),
            pltpu.VMEM((1024, 768), bf), pltpu.VMEM((1024, 768), f32), pltpu.VMEM((1024, 768), bf), pltpu.VMEM((1, 2, 2, 2, 2, 224, 768), bf),
            pltpu.VMEM((768, 768), f32), pltpu.VMEM((4, 8, 768), f32), pltpu.VMEM((8, 768), f32),
            pltpu.VMEM((1024, 768), bf), pltpu.VMEM((1, 2, 2, 2, 224, 768), bf), pltpu.VMEM((1, 2, 2, 2, 224, 768), bf),
            pltpu.VMEM((2, 1, 2, 2, 224, 384), bf),
            pltpu.SemaphoreType.DMA((23,)), pltpu.SemaphoreType.DMA, pltpu.SemaphoreType.DMA((7,)),
        ],
        compiler_params=pltpu.CompilerParams(vmem_limit_bytes=LIMIT, collective_id=1, has_side_effects=True),
        name="channel_back",
    )(kg, vg, wts, acts, sq, act, grads, middle, gy, out_row, cols, vecs)


def time_back_kernel(
    wts, acts, kvs, gm_any, x_any, kept_any, cols, docs, vecs, sums_c,
    ig_o, gkv_o, gt_o, small_o,
    w4, ins, f5, gm, xb, gb, gkvr, delta, grads, split, pack, tables, sums, nxt, small_cut, *scratch,
):
    kept, second_step, third_step = scratch[:3]
    s_scratch = scratch[3:7]
    t_scratch = [scratch[7 + 4 * i : 11 + 4 * i] for i in range(4)]
    sems, send_sem, recv_sems = scratch[23:]
    place_of = Place()
    mp = place_of.mp
    row, pair = mp % 2, mp // 2
    load_kept = pltpu.make_async_copy(kept_any, kept, sems.at[8])
    load_w = [
        pltpu.make_async_copy(wts.at[4], w4.at[3], sems.at[1]),
        pltpu.make_async_copy(wts.at[pl.ds(0, 3)], w4.at[pl.ds(0, 3)], sems.at[2]),
    ]
    tile_loads = {}
    for t in reversed(range(1024 // TILE)):
        r = pl.ds(t * TILE, TILE)
        tile_loads[t] = [
            pltpu.make_async_copy(gm_any.at[r], gm.at[r], sems.at[18 + 4 * t]),
            pltpu.make_async_copy(kvs.at[:, r], f5.at[:, r], sems.at[19 + 4 * t]),
            pltpu.make_async_copy(x_any.at[row, r], xb.at[r], sems.at[20 + 4 * t]),
            pltpu.make_async_copy(acts.at[6, r], delta.at[r], sems.at[21 + 4 * t]),
        ]
    load_ins = [pltpu.make_async_copy(acts.at[i], ins.at[i % 2], sems.at[4 + i]) for i in range(4)]
    for copy in load_w[:1] + tile_loads[3] + load_w[1:] + [load_kept] + tile_loads[2] + tile_loads[1] + tile_loads[0] + load_ins[:2]:
        copy.start()
    greet([place_of.sib, place_of.xn, place_of.yn, place_of.across, place_of.pair])
    messages = Messages(send_sem, recv_sems)
    channel = Scatter(place_of, messages, None, None, kept, [None, second_step, third_step], gkv_o, ("xyj", "yxj"))
    vectors = Plane(place_of, messages, small_cut.at[0], *s_scratch, small_o.at[0])
    mixing = [Plane(place_of, messages, pack.at[i], *t_scratch[i], gt_o.at[i]) for i in range(4)]
    rate = jnp.exp(vec(vecs, DECAY))
    fade = jnp.exp(-rate)
    place = wide(lax.broadcasted_iota(jnp.int32, (TILE, 1), 0) % SPAN)
    tables[0] = jnp.exp((64.0 - place) * rate)
    tables[1] = jnp.exp((place - 63.0) * rate)
    tables[2] = jnp.exp((place - 127.0) * rate)
    sums[...] = jnp.zeros_like(sums)
    nxt[...] = jnp.zeros_like(nxt)
    gain = vec(vecs, GAIN1)
    own_docs = row_of(docs, row)

    def tile(t):
        base = t * TILE
        r = pl.ds(base, TILE)
        for copy in tile_loads[t]:
            copy.wait()
        gb[r, :] = low(gm[r, :])
        if t == 3:
            load_w[0].wait()
        grads[0] = dot_nt(gb[r, :], w4[3])

        values, gate = f5[1, r, :], f5[2, r, :]
        bonus = jnp.exp(f5[0, r, :] + vec(vecs, FIRST))
        inverse = 1.0 / (f5[4, r, :] + bonus)
        mixed = (f5[3, r, :] + bonus * values) * inverse
        grad_mixed = grads[0] * gate
        gkvr[2, r, :] = low(grad_mixed * mixed * (1.0 - gate))
        grad_top = grad_mixed * inverse
        shrunk = grad_top * tables[0]
        halves(split.at[0], shrunk)
        halves(split.at[1], -shrunk * mixed)
        direct = bonus * grad_top
        own = direct * (values - mixed)
        grads[0] = direct
        grads[1] = own
        sums[0] += row_sums(own)
        grads[3] = grad_top
        edges = [grads[3, i * SPAN : i * SPAN + 1, :] for i in range(TILE // SPAN)]
        time = lax.broadcasted_iota(jnp.int32, (SPAN, SPAN), 0)
        source = lax.broadcasted_iota(jnp.int32, (SPAN, SPAN), 1)
        for i in reversed(range(TILE // SPAN)):
            block = t * (TILE // SPAN) + i
            same = cols[pl.ds(block * SPAN, SPAN), 0:1] == own_docs[:, block * SPAN : (block + 1) * SPAN]
            mask = jnp.where(same & (source > time), 1.0, 0.0).astype(jnp.bfloat16)
            mask = jnp.concatenate([mask, mask], axis=1)
            for k in range(2):
                grads[2 + k, pl.ds(i * SPAN, SPAN), :] = dot(mask, split[k, i])
        for i in reversed(range(TILE // SPAN)):
            begin = base + i * SPAN
            top_in, bottom_in = nxt[1:2, :], nxt[2:3, :]

            q, here = pl.ds(begin, SPAN), pl.ds(i * SPAN, SPAN)
            link = cols[q, 3:4] * tables[2, 0:SPAN, :]
            state_top = grads[2, here, :] * tables[1, 0:SPAN, :] + link * top_in
            state_bottom = grads[3, here, :] * tables[1, 0:SPAN, :] + link * bottom_in
            key_exp = jnp.exp(f5[0, q, :])
            gkvr[0, q, :] = low(grads[1, here, :] + key_exp * (state_top * f5[1, q, :] + state_bottom))
            gkvr[1, q, :] = low(grads[0, here, :] + key_exp * state_top)
            sums[1] += row_sums(state_top * f5[3, q, :] + state_bottom * f5[4, q, :])
            row_top, row_bottom = state_top[0:1], state_bottom[0:1]
            bonus = jnp.exp(f5[0, begin : begin + 1, :] + vec(vecs, FIRST))
            bottom = f5[4, begin : begin + 1, :] + bonus
            mixed = (f5[3, begin : begin + 1, :] + bonus * f5[1, begin : begin + 1, :]) / bottom
            nxt[1:2, :] = fade * row_top + edges[i]
            nxt[2:3, :] = fade * row_bottom - edges[i] * mixed
        if t == 3:
            load_w[1].wait()
        for j in range(3):
            grads[j] = dot_nt(gkvr[j, r, :], w4[j])

        def third(q, state):
            step = wide(delta[q, :])
            grad, whole = 0.0, 0.0
            for j in range(3):
                into = grads[j]
                sums[4 + j] += row_sums(into * step)
                grad += into * vec(vecs, MIX + j)
                whole += into
            back = (whole - grad) * cols[q, 1:2]
            grad = grad + sooner(back, state)
            scale = cols[q, 5:6]
            normal = (wide(xb[q, :]) - cols[q, 4:5]) * scale
            sums[2] += row_sums(grad * normal)
            sums[3] += row_sums(grad)
            xb[q, :] = low(gm[q, :] + norm_back(grad * gain, normal, scale))
            return back[0:1]

        nxt[0:1, :] = third(r, nxt[0:1, :])

    arrivals = []
    keeps = []
    for t in reversed(range(1024 // TILE)):
        tile(t)
        r = pl.ds(t * TILE, TILE)
        done = xb.at[r]
        arrivals.append(messages.send(done, ig_o.at[row, r], ig_o.at[1 - row, r], place_of.pair))
        keeps.append(pltpu.make_async_copy(done, ig_o.at[row, r], sems.at[14 + t]))
        keeps[-1].start()
        if t == 3:
            load_kept.wait()
            channel.send(1)
        elif t == 1:
            channel.add(1)

    def product(slot, right):
        load_ins[slot].wait()
        left = ins.at[slot % 2]
        def body(t, carry):
            c = pl.ds(pl.multiple_of(t * 384, 128), 384)
            f5[0, c, :] = dot_tn(left[:, c], right[...])
            return carry

        lax.fori_loop(0, 2, body, 0)

        def packed(dp, carry):
            for j in range(2):
                start = pl.multiple_of(96 * dp + 48 * pair + 24 * j, 8)
                piece = jnp.concatenate([f5[0, pl.ds(start, 24), :], jnp.zeros((8, 768), jnp.float32)], axis=0)
                pack[slot, j, dp // 4, (dp // 2) % 2, dp % 2] = low(piece)
            return carry

        lax.fori_loop(0, 8, packed, 0)
        if slot < 2:
            load_ins[slot + 2].start()
        mixing[slot].start()

    totals = [jnp.sum(sums[i], axis=0, keepdims=True) for i in range(7)]
    totals[1] = totals[1] * (-rate * fade)
    small = jnp.concatenate([sums_c[0:4, :]] + totals + [jnp.zeros((5, 768), jnp.float32)], axis=0)
    turned = pltpu.roll(small, (768 - 48 * pair) % 768, 1)
    for dp in range(8):
        for j in range(2):
            start = 96 * dp + 24 * j
            piece = turned if start == 0 else pltpu.roll(turned, 768 - start, 1)
            small_cut[0, j, dp // 4, (dp // 2) % 2, dp % 2] = piece[:, :128]
    vectors.start()
    product(0, gkvr.at[0])
    vectors.core()
    product(1, gkvr.at[1])
    mixing[0].core()
    product(2, gkvr.at[2])
    mixing[1].core()
    mixing[0].plane()
    vectors.plane()
    product(3, gb)
    mixing[2].core()
    mixing[1].plane()
    mixing[3].core()
    mixing[2].plane()
    channel.add(2)
    vectors.z()
    mixing[0].z()
    mixing[1].z()
    mixing[3].plane()
    mixing[2].z()
    mixing[3].z()
    for copy in keeps:
        copy.wait()
    for wait in arrivals:
        wait.wait_recv()
    messages.finish()


def time_back(wts, acts, kvs, gm, x, kept, cols, docs, vecs, sums_c):
    bf, f32 = jnp.bfloat16, jnp.float32
    shape = jax.ShapeDtypeStruct
    return pl.pallas_call(
        time_back_kernel,
        out_shape=(
            shape((2, 1024, 768), bf), shape((1, 224, 768), f32), shape((4, 32, 768), f32), shape((1, 16, 128), f32),
        ),
        in_specs=[ANY] * 6 + [ON_CORE] * 4,
        out_specs=[ANY] + [ON_CORE] * 3,
        scratch_shapes=[
            pltpu.VMEM((4, 768, 768), bf), pltpu.VMEM((2, 1024, 768), bf), pltpu.VMEM((5, 1024, 768), f32),
            pltpu.VMEM((1024, 768), f32), pltpu.VMEM((1024, 768), bf), pltpu.VMEM((1024, 768), bf),
            pltpu.VMEM((3, 1024, 768), bf), pltpu.VMEM((1024, 768), bf), pltpu.VMEM((4, TILE, 768), f32),
            pltpu.VMEM((2, 2, 2 * SPAN, 768), bf),
            pltpu.VMEM((4, 2, 2, 2, 2, 32, 768), bf), pltpu.VMEM((3, TILE, 768), f32), pltpu.VMEM((7, 8, 768), f32),
            pltpu.VMEM((8, 768), f32), pltpu.VMEM((1, 2, 2, 2, 2, 16, 128), f32),
        ]
        + [pltpu.VMEM((1, 2, 2, 2, 224, 768), bf), pltpu.VMEM((2, 1, 2, 224, 384), bf), pltpu.VMEM((2, 1, 224, 384), bf)]
        + plane_scratch(16, 128, f32)
        + plane_scratch(32, 768, bf) * 4
        + [pltpu.SemaphoreType.DMA((34,)), pltpu.SemaphoreType.DMA, pltpu.SemaphoreType.DMA((36,))],
        compiler_params=pltpu.CompilerParams(vmem_limit_bytes=LIMIT, collective_id=2, has_side_effects=True),
        name="time_back",
    )(wts, acts, kvs, gm, x, kept, cols, docs, vecs, sums_c)


def results_kernel(
    out_any, ig_any, gkv_any, gt_any, small,
    out_o, ig_o, gain1, bias1, gain2, bias2, mix, blend_o, decay, first, grad_mix, grad_out, grad_key, grad_value,
    rows, halves_in, halves_out, gkv, gt, sems,
):
    cut = 256
    parts = [(i, pl.ds(j * cut, cut)) for i in range(2) for j in range(1024 // cut)]
    loads = [pltpu.make_async_copy(ig_any.at[i, r], halves_in.at[i, r], sems.at[n]) for n, (i, r) in enumerate(parts)]
    load_out = [pltpu.make_async_copy(out_any.at[i], rows.at[i], sems.at[16 + i]) for i in range(2)]
    load_w = [pltpu.make_async_copy(gkv_any, gkv, sems.at[18]), pltpu.make_async_copy(gt_any, gt, sems.at[19])]
    for copy in loads[:4] + load_w + loads[4:] + load_out:
        copy.start()
    for ref, slot in ((gain2, 0), (bias2, 1), (first, 4), (decay, 5), (gain1, 6), (bias1, 7)):
        ref[...] = small[0, slot, 0:24]
    blend_o[...] = small[0, 2:4, 0:24]
    mix[...] = small[0, 8:11, 0:24]
    stores = []

    def store(source, target):
        copy = pltpu.make_async_copy(source, target, sems.at[20 + len(stores)])
        copy.start()
        stores.append(copy)

    for n, (i, r) in enumerate(parts):
        loads[n].wait()
        halves_out[i, r, :] = wide(halves_in[i, r, :])
        store(halves_out.at[i, r], ig_o.at[i, r])
        if n == 3:
            for copy in load_w:
                copy.wait()
            store(gt.at[pl.ds(0, 3), pl.ds(0, 24)], grad_mix.at[pl.ds(0, 3)])
            store(gkv.at[0, pl.ds(192, 24)], grad_mix.at[3])
            store(gt.at[3, pl.ds(0, 24)], grad_out)
            store(gkv.at[0, pl.ds(0, 96)], grad_key)
            store(gkv.at[0, pl.ds(96, 96)], grad_value)
    for i in range(2):
        load_out[i].wait()
        store(rows.at[i], out_o.at[i])
    for copy in stores:
        copy.wait()


def results(out, ig, gkv, gt, small):
    bf, f32 = jnp.bfloat16, jnp.float32
    shape = jax.ShapeDtypeStruct
    vector = shape((24,), f32)
    return pl.pallas_call(
        results_kernel,
        out_shape=(
            shape((2, 1024, 768), bf), shape((2, 1024, 768), f32), vector, vector, vector, vector,
            shape((3, 24), f32), shape((2, 24), f32), vector, vector,
            shape((4, 24, 768), f32), shape((24, 768), f32), shape((96, 768), f32), shape((96, 768), f32),
        ),
        in_specs=[ANY] * 4 + [ON_CORE],
        out_specs=[ANY] * 2 + [ON_CORE] * 8 + [ANY] * 4,
        scratch_shapes=[
            pltpu.VMEM((2, 1024, 768), bf), pltpu.VMEM((2, 1024, 768), bf), pltpu.VMEM((2, 1024, 768), f32),
            pltpu.VMEM((1, 224, 768), f32), pltpu.VMEM((4, 32, 768), f32), pltpu.SemaphoreType.DMA((40,)),
        ],
        compiler_params=pltpu.CompilerParams(vmem_limit_bytes=LIMIT),
        name="results",
    )(out, ig, gkv, gt, small)


def on_device(
    residual_input, article_numbers, upstream_gradient,
    prenorm_scaling, prenorm_offset, postnorm_scaling, postnorm_offset,
    attention_blend, feedforward_blend, forgetting_logrates, present_reward,
    projection_matrices, final_matrix, address_matrix, content_matrix,
):
    pieces = (
        prenorm_scaling[None], prenorm_offset[None], postnorm_scaling[None], postnorm_offset[None],
        attention_blend, forgetting_logrates[None], present_reward[None], feedforward_blend,
    )
    vectors, first_row = 0.0, 0
    for piece in pieces:
        count, lanes = piece.shape
        vectors = vectors + jnp.pad(piece, ((first_row, 16 - first_row - count), (0, 128 - lanes)))
        first_row += count
    vectors = vectors.astype(jnp.bfloat16)
    kg, vg, acts, kvs, middle, sq, act, grads, out_row, wts, vecs, cols = forward(
        projection_matrices, final_matrix, vectors, address_matrix, content_matrix.T, article_numbers,
        residual_input, upstream_gradient,
    )
    kg, vg, sq = kg.reshape(4, 768, 768), vg.reshape(4, 768, 768), sq.reshape(4, 8, 128, 768)
    gm, kept, output, sums_c = channel_back(
        kg, vg, wts, acts, sq, act, grads, middle, upstream_gradient, out_row, cols, vecs
    )
    input_grad, gkv, gt, small = time_back(
        wts, acts, kvs, gm, residual_input, kept, cols, article_numbers, vecs, sums_c
    )
    *others, grad_value = results(output, input_grad, gkv, gt, small)
    return (*others, grad_value.T)


def fits(mesh):
    return dict(mesh.shape) == {"dp": 8, "mp": 4}


def solution(mesh):
    return jax.shard_map(
        on_device if fits(mesh) else general_device,
        mesh=mesh,
        in_specs=(
            P("dp", None, None),
            P("dp", None),
            P("dp", None, None),
            P(("dp", "mp")),
            P(("dp", "mp")),
            P(("dp", "mp")),
            P(("dp", "mp")),
            P(None, ("dp", "mp")),
            P(None, ("dp", "mp")),
            P(("dp", "mp")),
            P(("dp", "mp")),
            P(None, ("dp", "mp"), None),
            P(("dp", "mp"), None),
            P("dp", "mp"),
            P("mp", "dp"),
        ),
        out_specs=(
            P("dp", None, None),
            P("dp", None, None),
            P(("dp", "mp")),
            P(("dp", "mp")),
            P(("dp", "mp")),
            P(("dp", "mp")),
            P(None, ("dp", "mp")),
            P(None, ("dp", "mp")),
            P(("dp", "mp")),
            P(("dp", "mp")),
            P(None, ("dp", "mp"), None),
            P(("dp", "mp"), None),
            P("dp", "mp"),
            P("mp", "dp"),
        ),
        check_vma=False,
    )
```
